256 devices in a mesh: trainer: 32 (over z, y), vocab: 8 (over x, core).
Axes of the slice: x: 4, y: 4, z: 8, core: 2. Of those that a mesh axis runs over, the one named last changes fastest.
Arguments:
- hidden_table: bfloat16 [1024, 3072], P('trainer')
- head_weight: bfloat16 [3072, 8, 12288], P(None, 'vocab', 'trainer'), may hold values from -0.109375 to 0.109375
- targets: bfloat16 [1024, 8, 12288], P('trainer', 'vocab')
- counts: int32 [32], replicated, may hold values from 8 to 32, as said below
- dest: int32 [1024], replicated, may hold values from 0 to 31
- token: int32 [1024], replicated, may hold values from 0 to 31
Outputs:
- head_grad: float32 [3072, 8, 12288], P(None, 'vocab', 'trainer')
- table_grad: float32 [1024, 3072], P('trainer', 'vocab')
- mean_loss: float32 [], replicated
The draws below stay inside these ranges and needn't reach their ends.
Inputs may be any that keep to these rules, and one draw needn't show every extreme that they name: `counts`: some replica has all 32 rows live and some has 8.
All inputs are finite; a program needn't handle non-finite values.
Results may differ from the reference program's by a relative error of at most 0.00095.
The reference program's roundings to bfloat16 on the way (of `drafts`, `grad_logits` and `gsum`) count: a program that leaves them out, or rounds other values in their place, can miss the bound.
Values may be sent and summed in bfloat16 or wider, within the bound.
No kernel may reach another device: no remote copies, remote signals or barrier semaphores. Data moves between devices by JAX's collectives and lax.ppermute only.
A program may use at most 128 MiB of HBM per device.

```python
import jax
import jax.numpy as jnp
from jax import lax

D = 3072
VOCAB = 98304
SLOTS = 32
TRAINERS = 32
ROWS_ALL = 1024
SHARDS = 8
SHARD_VOCAB = 12288


def draw_counts(key, part):
    key = jax.random.fold_in(key, 1)
    low = SLOTS // 4
    first, second = jax.random.split(key)
    values = jax.random.randint(first, (TRAINERS,), low, SLOTS + 1)
    where = jax.random.randint(second, (), 0, TRAINERS)
    values = values.at[where].set(SLOTS)
    values = values.at[(where + 1) % TRAINERS].set(low)
    return values.astype(jnp.int32)


def draw_hidden_table(key, part):
    key = jax.random.fold_in(key, 2)
    first, second = jax.random.split(key)
    values = jax.random.normal(first, (ROWS_ALL, D), jnp.float32)
    scales = jnp.exp(jax.random.uniform(second, (ROWS_ALL, 1), jnp.float32, -0.7, 0.7))
    return jnp.clip(values * scales, -500.0, 500.0).astype(jnp.bfloat16)


def draw_targets(key, part):
    key = jax.random.fold_in(key, 3)
    logits = 2.0 * jax.random.normal(key, (ROWS_ALL, VOCAB), jnp.float32)
    probs = jax.nn.softmax(logits, axis=1)
    return probs.reshape(ROWS_ALL, SHARDS, SHARD_VOCAB).astype(jnp.bfloat16)


def place_ends(result, key, least, high):
    longest = result.shape.index(max(result.shape))
    spots = []
    for shift in (0, 1):
        where = [jax.random.randint(jax.random.fold_in(key, axis), (), 0, length) for axis, length in enumerate(result.shape)]
        where[longest] = (where[longest] + shift) % result.shape[longest]
        spots.append(tuple(where))
    return result.at[spots[0]].set(least).at[spots[1]].set(high)


def block_scale(stream_key, shape, cuts, low, largest):
    loudness = 1.0
    for position, parts in cuts:
        steps = jax.random.uniform(jax.random.fold_in(jax.random.fold_in(stream_key, 6), position), (parts,), jnp.float32, low / len(cuts), largest / len(cuts))
        loudness = loudness * jnp.repeat(jnp.exp(steps), shape[position] // parts).reshape((-1,) + (1,) * (len(shape) - 1 - position))
    return loudness


def normal_values(own_key, shape, scale, limit, pieces=(), kind=jnp.bfloat16):
    factor_of = block_scale(own_key, shape, pieces, -0.22, 0.18) if pieces else 1.0
    drawn = jax.random.normal(own_key, shape, jnp.float32) * scale * factor_of
    return jnp.minimum(jnp.maximum(drawn, -limit), limit).astype(kind)


def setup_inputs(seed: int = 0) -> dict:
    arg_keys = jax.random.split(jax.random.key(seed), 7)
    hidden_table = draw_hidden_table(jax.random.fold_in(arg_keys[6], 71), 0)
    head_weight = normal_values(arg_keys[1], (D, SHARDS, SHARD_VOCAB), D ** -0.5, 0.109375, ((1, 8), (2, 32)))
    targets = draw_targets(jax.random.fold_in(arg_keys[6], 71), 0)
    counts = draw_counts(jax.random.fold_in(arg_keys[6], 71), 0)
    dest = place_ends(jax.random.randint(arg_keys[4], (ROWS_ALL,), 0, TRAINERS), jax.random.fold_in(arg_keys[4], 1), 0, TRAINERS - 1).astype(jnp.int32)
    token = place_ends(jax.random.randint(arg_keys[5], (ROWS_ALL,), 0, SLOTS), jax.random.fold_in(arg_keys[5], 1), 0, SLOTS - 1).astype(jnp.int32)
    return {"hidden_table": hidden_table, "head_weight": head_weight, "targets": targets, "counts": counts, "dest": dest, "token": token}


def reference(hidden_table, head_weight, targets, counts, dest, token):
    weight = head_weight.reshape(D, VOCAB)
    probs = targets.reshape(ROWS_ALL, VOCAB)
    gid = (dest * SLOTS + token).astype(jnp.int32)
    index = jnp.arange(ROWS_ALL, dtype=jnp.int32)
    live = (index % SLOTS < jnp.repeat(counts, SLOTS)).astype(jnp.float32)
    drafts = hidden_table[gid]
    logits = jnp.dot(drafts, weight, preferred_element_type=jnp.float32)
    top = jnp.max(logits, axis=1)
    total = jnp.sum(jnp.exp(logits - top[:, None]), axis=1)
    lse = top + jnp.log(total)
    scale = VOCAB / (ROWS_ALL ** 0.5)
    probs_f = probs.astype(jnp.float32)
    grad_logits = (live[:, None] * scale * (jnp.exp(logits - lse[:, None]) - probs_f)).astype(jnp.bfloat16)
    head_grad = lax.dot_general(drafts, grad_logits, (((0,), (0,)), ((), ())), preferred_element_type=jnp.float32)
    head_grad = head_grad.reshape(D, SHARDS, SHARD_VOCAB)
    gsum = jax.ops.segment_sum(grad_logits.astype(jnp.float32), gid, num_segments=ROWS_ALL).astype(jnp.bfloat16)
    table_grad = lax.dot_general(gsum, weight, (((1,), (1,)), ((), ())), preferred_element_type=jnp.float32)
    psum_rows = jnp.sum(probs_f, axis=1)
    pz = jnp.sum(probs_f * logits, axis=1)
    mean_loss = jnp.sum(live * (lse * psum_rows - pz)) / jnp.sum(counts).astype(jnp.float32)
    return head_grad, table_grad, mean_loss
```

```python
import functools
import math

import jax
import jax.numpy as jnp
from jax import lax
from jax.experimental import pallas as pl
from jax.experimental.pallas import tpu as pltpu
from jax.sharding import PartitionSpec as P

D = 3072
VOCAB = 98304
ROWS = 1024
TRAINERS = 32
SLOTS = 32
SHARDS = 8
LOCAL = VOCAB // (TRAINERS * SHARDS)
HALF = D // 2
BLOCK = 256
BF16 = jnp.bfloat16
F32 = jnp.float32
VMEM_LIMIT = 48 * 1024 * 1024
PARAMS = pltpu.CompilerParams(vmem_limit_bytes=VMEM_LIMIT)
VMEM = pl.BlockSpec(memory_space=pltpu.VMEM)
SMEM = pl.BlockSpec(memory_space=pltpu.SMEM)


def dot(a, b, dims=((1,), (0,))):
    return lax.dot_general(a, b, (dims, ((), ())), preferred_element_type=F32)


def split_kernel(x_ref, o_ref):
    for j in range(TRAINERS):
        o_ref[j] = x_ref[:, j * LOCAL : (j + 1) * LOCAL]


def split_targets(x):
    return pl.pallas_call(
        split_kernel,
        out_shape=jax.ShapeDtypeStruct((TRAINERS, SLOTS, LOCAL), BF16),
        in_specs=[VMEM],
        out_specs=VMEM,
        compiler_params=PARAMS,
    )(x)


def target_kernel(gid_ref, live_ref, p_ref, psum_ref, stat_ref):
    base = pl.program_id(0) * BLOCK
    rows = lax.broadcasted_iota(jnp.int32, (BLOCK, ROWS), 0) + base
    hot = jnp.where(gid_ref[...] == rows, live_ref[...], 0.0).astype(BF16)
    psum = dot(hot, p_ref[...])
    psum_ref[...] = psum
    lane = lax.broadcasted_iota(jnp.int32, (BLOCK, 128), 1)
    mass = jnp.sum(psum, axis=1, keepdims=True)
    stat_ref[...] = jnp.where(lane == 1, mass, 0.0)


def target_sums(gid, live, probs):
    return pl.pallas_call(
        target_kernel,
        grid=(ROWS // BLOCK,),
        out_shape=(
            jax.ShapeDtypeStruct((ROWS, LOCAL), F32),
            jax.ShapeDtypeStruct((ROWS, 128), F32),
        ),
        in_specs=[
            pl.BlockSpec((1, ROWS), lambda i: (0, 0)),
            pl.BlockSpec((1, ROWS), lambda i: (0, 0)),
            pl.BlockSpec((ROWS, LOCAL), lambda i: (0, 0)),
        ],
        out_specs=(
            pl.BlockSpec((BLOCK, LOCAL), lambda i: (i, 0)),
            pl.BlockSpec((BLOCK, 128), lambda i: (i, 0)),
        ),
        compiler_params=PARAMS,
    )(gid, live, probs)


def logit_kernel(c_ref, own_ref, other_ref, w_ref, psum_ref, stat_ref, logits_ref, o_ref):
    c = c_ref[0]
    near = pl.multiple_of(c * HALF, HALF)
    far = pl.multiple_of((1 - c) * HALF, HALF)
    logits = dot(own_ref[...], w_ref[pl.ds(near, HALF), :])
    logits += dot(other_ref[...], w_ref[pl.ds(far, HALF), :])
    logits_ref[...] = logits
    top = jnp.max(logits, axis=1, keepdims=True)
    lse = top + jnp.log(jnp.sum(jnp.exp(logits - top), axis=1, keepdims=True))
    cross = jnp.sum(psum_ref[...] * logits, axis=1, keepdims=True)
    lane = lax.broadcasted_iota(jnp.int32, (BLOCK, 128), 1)
    stat = jnp.where(lane == 0, lse, jnp.where(lane == 2, cross, stat_ref[...]))
    flat = stat.T[0:4]
    for k in range(SHARDS):
        o_ref[k] = flat


def logits_and_stats(c, own, other, weight, psum, stat):
    return pl.pallas_call(
        logit_kernel,
        grid_spec=pltpu.PrefetchScalarGridSpec(
            num_scalar_prefetch=1,
            grid=(ROWS // BLOCK,),
            in_specs=[
                pl.BlockSpec((BLOCK, HALF), lambda i, c: (i, 0)),
                pl.BlockSpec((BLOCK, HALF), lambda i, c: (i, 0)),
                pl.BlockSpec((D, LOCAL), lambda i, c: (0, 0)),
                pl.BlockSpec((BLOCK, LOCAL), lambda i, c: (i, 0)),
                pl.BlockSpec((BLOCK, 128), lambda i, c: (i, 0)),
            ],
            out_specs=(
                pl.BlockSpec((BLOCK, LOCAL), lambda i, c: (i, 0)),
                pl.BlockSpec((SHARDS, 4, BLOCK), lambda i, c: (0, 0, i)),
            ),
        ),
        out_shape=(
            jax.ShapeDtypeStruct((ROWS, LOCAL), F32),
            jax.ShapeDtypeStruct((SHARDS, 4, ROWS), F32),
        ),
        compiler_params=PARAMS,
    )(c, own, other, weight, psum, stat)


def merge(x):
    lse = x[:, 0, :]
    top = jnp.max(lse, axis=0, keepdims=True)
    lse = top + jnp.log(jnp.sum(jnp.exp(lse - top), axis=0, keepdims=True))
    rest = jnp.sum(x[:, 1:3, :], axis=0)
    return lse, rest[0:1], rest[1:2]


def merge_kernel(x_ref, o_ref):
    lse, mass, cross = merge(x_ref[...])
    flat = jnp.concatenate([lse, mass, cross, jnp.zeros_like(lse)], axis=0)
    for k in range(TRAINERS):
        o_ref[k] = flat


def merge_stats(x):
    return pl.pallas_call(
        merge_kernel,
        out_shape=jax.ShapeDtypeStruct((TRAINERS, 4, ROWS), F32),
        in_specs=[VMEM],
        out_specs=VMEM,
        compiler_params=PARAMS,
    )(x)


def column(row):
    return jnp.broadcast_to(row, (128, row.shape[1])).T


def grad_kernel(
    x_ref, logits_ref, p_ref, gid_ref, live_ref, sum_ref, loss_ref, parts_ref, g_ref
):
    lse, mass, cross = merge(x_ref[...])
    loss_ref[0, 0] = jnp.sum(lse * mass - cross)
    lse_col = column(lse)
    for j in range(LOCAL // 128):
        cols = pl.ds(j * 128, 128)
        p = jnp.exp(logits_ref[:, cols] - lse_col)
        first = p.astype(BF16)
        p = p - first.astype(F32)
        second = p.astype(BF16)
        third = (p - second.astype(F32)).astype(BF16)
        parts_ref[:, pl.ds(j * 128, 128)] = first
        parts_ref[:, pl.ds(LOCAL + j * 128, 128)] = second
        parts_ref[:, pl.ds(2 * LOCAL + j * 128, 128)] = third
    scale = VOCAB / math.sqrt(ROWS)

    @pl.loop(0, ROWS // BLOCK)
    def _(i):
        rows = pl.ds(pl.multiple_of(i * BLOCK, BLOCK), BLOCK)
        gid = column(gid_ref[:, rows])
        live = column(live_ref[:, rows])
        lane = lax.broadcasted_iota(jnp.int32, (BLOCK, 128), 1).astype(F32)
        hot = jnp.concatenate(
            [
                jnp.where(gid == lane + float(128 * k), 1.0, 0.0).astype(BF16)
                for k in range(ROWS // 128)
            ],
            axis=1,
        )
        sel = dot(hot, parts_ref[...])
        p = sel[:, 0:LOCAL] + sel[:, LOCAL : 2 * LOCAL] + sel[:, 2 * LOCAL :]
        diff = p - p_ref[rows, :].astype(F32)
        factor = live * scale
        g = jnp.concatenate(
            [factor * diff[:, j * 128 : (j + 1) * 128] for j in range(LOCAL // 128)],
            axis=1,
        )
        g_ref[rows, :] = g.astype(BF16)

    @pl.loop(0, ROWS // BLOCK)
    def _(i):
        rows = pl.ds(pl.multiple_of(i * BLOCK, BLOCK), BLOCK)
        row = lax.broadcasted_iota(jnp.int32, (BLOCK, ROWS), 0) + i * BLOCK
        hot = jnp.where(gid_ref[...] == row.astype(F32), 1.0, 0.0).astype(BF16)
        total = dot(hot, g_ref[...])
        high = total.astype(BF16)
        low = (total - high.astype(F32)).astype(BF16)
        sum_ref[0, rows, :] = high
        sum_ref[1, rows, :] = low


def gradients(x, logits, probs, gid, live):
    return pl.pallas_call(
        grad_kernel,
        out_shape=(
            jax.ShapeDtypeStruct((2, ROWS, LOCAL), BF16),
            jax.ShapeDtypeStruct((1, 1), F32),
        ),
        in_specs=[VMEM] * 5,
        out_specs=(VMEM, SMEM),
        scratch_shapes=[
            pltpu.VMEM((ROWS, 3 * LOCAL), BF16),
            pltpu.VMEM((ROWS, LOCAL), BF16),
        ],
        compiler_params=PARAMS,
    )(x, logits, probs, gid, live)


def term_kernel(x_ref, own_ref, other_ref, w_own_ref, w_other_ref, c0, c1, c2, c3):
    for k, out in enumerate((c0, c1, c2, c3)):
        at = lax.rem(x_ref[0] + k, 4)
        w_own = w_own_ref[at]
        w_other = w_other_ref[at]

        @pl.loop(0, ROWS // BLOCK)
        def _(i):
            rows = pl.ds(pl.multiple_of(i * BLOCK, BLOCK), BLOCK)
            nt = ((1,), (1,))
            val = dot(own_ref[0, rows, :], w_own, nt) + dot(other_ref[rows, :], w_other, nt)
            if k == 0:
                out[rows, :] = val
            else:
                half = ROWS // 2 // BLOCK
                at = pl.ds(pl.multiple_of(lax.rem(i, half) * BLOCK, BLOCK), BLOCK)
                out[i // half, at, :] = val


def terms(x, own, other, w_own, w_other):
    split = jax.ShapeDtypeStruct((2, ROWS // 2, LOCAL), F32)
    return pl.pallas_call(
        term_kernel,
        out_shape=(jax.ShapeDtypeStruct((ROWS, LOCAL), F32), split, split, split),
        in_specs=[SMEM] + [VMEM] * 4,
        out_specs=(VMEM,) * 4,
        compiler_params=PARAMS,
    )(x, own, other, w_own, w_other)


HEAD_BLOCK = 256
HEAD_STEPS = HALF // HEAD_BLOCK


def head_kernel(c_ref, own_ref, other_ref, sum_ref, o_ref):
    i = pl.program_id(0)

    def work(t_ref):
        both = dot(t_ref[...], sum_ref[0], ((0,), (0,)))
        both += dot(t_ref[...], sum_ref[1], ((0,), (0,)))
        for j in range(LOCAL // 128):
            o_ref[pl.ds(j, HEAD_BLOCK, stride=LOCAL // 128), :] = both[:, j * 128 : (j + 1) * 128]

    @pl.when(i < HEAD_STEPS)
    def _():
        work(own_ref)

    @pl.when(i >= HEAD_STEPS)
    def _():
        work(other_ref)


def head_gradient(c, own, other, sums):
    def place(i, c):
        mine = i < HEAD_STEPS
        side = jnp.where(mine, c[0], 1 - c[0])
        return (side * HEAD_STEPS + jnp.where(mine, i, i - HEAD_STEPS), 0)

    return pl.pallas_call(
        head_kernel,
        grid_spec=pltpu.PrefetchScalarGridSpec(
            num_scalar_prefetch=1,
            grid=(2 * HEAD_STEPS,),
            in_specs=[
                pl.BlockSpec((ROWS, HEAD_BLOCK), lambda i, c: (0, jnp.minimum(i, HEAD_STEPS - 1))),
                pl.BlockSpec((ROWS, HEAD_BLOCK), lambda i, c: (0, jnp.maximum(i - HEAD_STEPS, 0))),
                pl.BlockSpec((2, ROWS, LOCAL), lambda i, c: (0, 0, 0)),
            ],
            out_specs=pl.BlockSpec((HEAD_BLOCK * LOCAL // 128, 128), place),
        ),
        out_shape=jax.ShapeDtypeStruct((D * LOCAL // 128, 128), F32),
        compiler_params=PARAMS,
        cost_estimate=pl.CostEstimate(
            flops=4 * ROWS * D * LOCAL, bytes_accessed=12 * 1024 * 1024, transcendentals=0
        ),
    )(c, own, other, sums)


PAIR = [(i, i ^ 1) for i in range(SHARDS)]
RIGHT = [(i, (i + 2) % SHARDS) for i in range(SHARDS)]
LEFT = [(i, (i - 2) % SHARDS) for i in range(SHARDS)]


def on_device(hidden_table, head_weight, targets, counts, dest, token):
    me = lax.axis_index("vocab")
    c = lax.rem(me, 2)
    x = me // 2
    c1 = c.reshape(1).astype(jnp.int32)
    x1 = x.reshape(1).astype(jnp.int32)
    weight = head_weight[:, 0, :]

    half = lax.dynamic_slice(hidden_table, (0, c * HALF), (SLOTS, HALF))
    own = lax.all_gather(half, "trainer", axis=0, tiled=True)

    moved = lax.all_to_all(
        split_targets(targets[:, 0, :]), "trainer", split_axis=0, concat_axis=0, tiled=True
    )
    probs = moved.reshape(ROWS, LOCAL)

    blocks = weight.reshape(4, 2, LOCAL, LOCAL)
    w_own = lax.dynamic_index_in_dim(blocks, c, axis=1, keepdims=False)
    w_give = lax.dynamic_index_in_dim(blocks, 1 - c, axis=1, keepdims=False)
    w_other = lax.ppermute(w_give, "vocab", PAIR)

    gid = dest * SLOTS + token
    index = jnp.arange(ROWS, dtype=jnp.int32)
    live = (index % SLOTS < jnp.repeat(counts, SLOTS)).astype(F32).reshape(1, ROWS)
    psum, mass = target_sums(gid.reshape(1, ROWS), live, probs)

    other = lax.ppermute(own, "vocab", PAIR)
    logits, stats = logits_and_stats(c1, own, other, weight, psum, mass)
    stats = lax.all_to_all(stats, "vocab", split_axis=0, concat_axis=0, tiled=True)
    stats = lax.all_to_all(merge_stats(stats), "trainer", split_axis=0, concat_axis=0, tiled=True)

    sums, loss = gradients(stats, logits, probs, gid.astype(F32).reshape(1, ROWS), live)
    mean_loss = loss[0, 0] / jnp.sum(counts).astype(F32)

    sum_other = lax.ppermute(sums[0], "vocab", PAIR)
    t0, t1, t2, t3 = terms(x1, sums, sum_other, w_own, w_other)
    low_r = lax.ppermute(t2[0], "vocab", RIGHT)
    high_l = lax.ppermute(t2[1], "vocab", LEFT)
    high_r = lax.ppermute(t1[1], "vocab", RIGHT)
    low_l = lax.ppermute(t3[0], "vocab", LEFT)
    low_r = lax.ppermute(t1[0] + low_r, "vocab", RIGHT)
    high_l = lax.ppermute(t3[1] + high_l, "vocab", LEFT)
    head = head_gradient(c1, own, other, sums)
    total = t0 + jnp.concatenate([low_r + low_l, high_r + high_l], axis=0)
    got = lax.all_to_all(
        total.reshape(TRAINERS, SLOTS, LOCAL), "trainer", split_axis=0, concat_axis=0, tiled=True
    )
    table_grad = jnp.sum(got, axis=0)
    return head.reshape(D, 1, LOCAL), table_grad, mean_loss


def solution(mesh):
    return jax.shard_map(
        on_device,
        mesh=mesh,
        in_specs=(
            P("trainer", None),
            P(None, "vocab", "trainer"),
            P("trainer", "vocab", None),
            P(),
            P(),
            P(),
        ),
        out_specs=(P(None, "vocab", "trainer"), P("trainer", "vocab"), P()),
        check_vma=False,
    )
```

```python
import functools
import math

import jax
import jax.numpy as jnp
from jax import lax
from jax.experimental import pallas as pl
from jax.experimental.pallas import tpu as pltpu
from jax.sharding import PartitionSpec as P

D = 3072
VOCAB = 98304
ROWS = 1024
TRAINERS = 32
SLOTS = 32
SHARDS = 8
LOCAL = VOCAB // (TRAINERS * SHARDS)
HALF = D // 2
BLOCK = 256
BF16 = jnp.bfloat16
F32 = jnp.float32
VMEM_LIMIT = 48 * 1024 * 1024
PARAMS = pltpu.CompilerParams(vmem_limit_bytes=VMEM_LIMIT)
VMEM = pl.BlockSpec(memory_space=pltpu.VMEM)
SMEM = pl.BlockSpec(memory_space=pltpu.SMEM)


def dot(a, b, dims=((1,), (0,))):
    return lax.dot_general(a, b, (dims, ((), ())), preferred_element_type=F32)


def split_kernel(x_ref, o_ref):
    for j in range(TRAINERS):
        o_ref[j] = x_ref[:, j * LOCAL : (j + 1) * LOCAL]


def split_targets(x):
    return pl.pallas_call(
        split_kernel,
        out_shape=jax.ShapeDtypeStruct((TRAINERS, SLOTS, LOCAL), BF16),
        in_specs=[VMEM],
        out_specs=VMEM,
        compiler_params=PARAMS,
    )(x)


def target_kernel(gid_ref, live_ref, p_ref, psum_ref, stat_ref):
    base = pl.program_id(0) * BLOCK
    rows = lax.broadcasted_iota(jnp.int32, (BLOCK, ROWS), 0) + base
    hot = jnp.where(gid_ref[...] == rows, live_ref[...], 0.0).astype(BF16)
    psum = dot(hot, p_ref[...])
    psum_ref[...] = psum
    lane = lax.broadcasted_iota(jnp.int32, (BLOCK, 128), 1)
    mass = jnp.sum(psum, axis=1, keepdims=True)
    stat_ref[...] = jnp.where(lane == 1, mass, 0.0)


def target_sums(gid, live, probs):
    return pl.pallas_call(
        target_kernel,
        grid=(ROWS // BLOCK,),
        out_shape=(
            jax.ShapeDtypeStruct((ROWS, LOCAL), F32),
            jax.ShapeDtypeStruct((ROWS, 128), F32),
        ),
        in_specs=[
            pl.BlockSpec((1, ROWS), lambda i: (0, 0)),
            pl.BlockSpec((1, ROWS), lambda i: (0, 0)),
            pl.BlockSpec((ROWS, LOCAL), lambda i: (0, 0)),
        ],
        out_specs=(
            pl.BlockSpec((BLOCK, LOCAL), lambda i: (i, 0)),
            pl.BlockSpec((BLOCK, 128), lambda i: (i, 0)),
        ),
        compiler_params=PARAMS,
    )(gid, live, probs)


Z = 8
Y = 4
PIECE = (Z // 2, SLOTS, HALF)


def logit_kernel(at_ref, *refs):
    pieces, refs = refs[:16], refs[16:]
    w_ref, psum_ref, stat_ref, own_ref, other_ref, logits_ref, o_ref = refs
    c, y, z = at_ref[0], at_ref[1], at_ref[2]
    for side, tab_ref in enumerate((own_ref, other_ref)):
        for dy in range(Y):
            for dz in range(Z):
                z_at = lax.rem(z + Z - dz, Z)
                y_at = lax.rem(y + Y - dy, Y)
                piece = pieces[side * 8 + dy * 2 + dz // 4]
                rows = pl.ds(pl.multiple_of((z_at * Y + y_at) * SLOTS, SLOTS), SLOTS)
                tab_ref[rows, :] = piece[dz % 4]
    near = pl.ds(pl.multiple_of(c * HALF, HALF), HALF)
    far = pl.ds(pl.multiple_of((1 - c) * HALF, HALF), HALF)
    block = 2 * BLOCK

    @pl.loop(0, ROWS // block)
    def _(i):
        rows = pl.ds(pl.multiple_of(i * block, block), block)
        logits = dot(own_ref[rows, :], w_ref[near, :])
        logits += dot(other_ref[rows, :], w_ref[far, :])
        logits_ref[rows, :] = logits
        top = jnp.max(logits, axis=1, keepdims=True)
        lse = top + jnp.log(jnp.sum(jnp.exp(logits - top), axis=1, keepdims=True))
        cross = jnp.sum(psum_ref[rows, :] * logits, axis=1, keepdims=True)
        lane = lax.broadcasted_iota(jnp.int32, (block, 128), 1)
        stat = jnp.where(lane == 0, lse, jnp.where(lane == 2, cross, stat_ref[rows, :]))
        flat = stat.T[0:4]
        for k in range(SHARDS):
            o_ref[k, :, rows] = flat


def logits_and_stats(at, pieces, weight, psum, stat):
    table = jax.ShapeDtypeStruct((ROWS, HALF), BF16)
    return pl.pallas_call(
        logit_kernel,
        out_shape=(
            table,
            table,
            jax.ShapeDtypeStruct((ROWS, LOCAL), F32),
            jax.ShapeDtypeStruct((SHARDS, 4, ROWS), F32),
        ),
        in_specs=[SMEM] + [VMEM] * 19,
        out_specs=(VMEM,) * 4,
        compiler_params=PARAMS,
    )(at, *pieces, weight, psum, stat)


def merge(x):
    lse = x[:, 0, :]
    top = jnp.max(lse, axis=0, keepdims=True)
    lse = top + jnp.log(jnp.sum(jnp.exp(lse - top), axis=0, keepdims=True))
    rest = jnp.sum(x[:, 1:3, :], axis=0)
    return lse, rest[0:1], rest[1:2]


def merge_kernel(x_ref, o_ref):
    lse, mass, cross = merge(x_ref[...])
    flat = jnp.concatenate([lse, mass, cross, jnp.zeros_like(lse)], axis=0)
    for k in range(TRAINERS):
        o_ref[k] = flat


def merge_stats(x):
    return pl.pallas_call(
        merge_kernel,
        out_shape=jax.ShapeDtypeStruct((TRAINERS, 4, ROWS), F32),
        in_specs=[VMEM],
        out_specs=VMEM,
        compiler_params=PARAMS,
    )(x)


def column(row):
    return jnp.broadcast_to(row, (128, row.shape[1])).T


def grad_kernel(
    x_ref, logits_ref, p_ref, gid_ref, live_ref, high_ref, low_ref, loss_ref, parts_ref, g_ref
):
    lse, mass, cross = merge(x_ref[...])
    loss_ref[0, 0] = jnp.sum(lse * mass - cross)
    lse_col = column(lse)
    for j in range(LOCAL // 128):
        cols = pl.ds(j * 128, 128)
        p = jnp.exp(logits_ref[:, cols] - lse_col)
        first = p.astype(BF16)
        p = p - first.astype(F32)
        second = p.astype(BF16)
        third = (p - second.astype(F32)).astype(BF16)
        parts_ref[:, pl.ds(j * 128, 128)] = first
        parts_ref[:, pl.ds(LOCAL + j * 128, 128)] = second
        parts_ref[:, pl.ds(2 * LOCAL + j * 128, 128)] = third
    scale = VOCAB / math.sqrt(ROWS)

    @pl.loop(0, ROWS // BLOCK)
    def _(i):
        rows = pl.ds(pl.multiple_of(i * BLOCK, BLOCK), BLOCK)
        gid = column(gid_ref[:, rows])
        live = column(live_ref[:, rows])
        lane = lax.broadcasted_iota(jnp.int32, (BLOCK, 128), 1).astype(F32)
        hot = jnp.concatenate(
            [
                jnp.where(gid == lane + float(128 * k), 1.0, 0.0).astype(BF16)
                for k in range(ROWS // 128)
            ],
            axis=1,
        )
        sel = dot(hot, parts_ref[...])
        p = sel[:, 0:LOCAL] + sel[:, LOCAL : 2 * LOCAL] + sel[:, 2 * LOCAL :]
        diff = p - p_ref[rows, :].astype(F32)
        factor = live * scale
        g = jnp.concatenate(
            [factor * diff[:, j * 128 : (j + 1) * 128] for j in range(LOCAL // 128)],
            axis=1,
        )
        g_ref[rows, :] = g.astype(BF16)

    @pl.loop(0, ROWS // BLOCK)
    def _(i):
        rows = pl.ds(pl.multiple_of(i * BLOCK, BLOCK), BLOCK)
        row = lax.broadcasted_iota(jnp.int32, (BLOCK, ROWS), 0) + i * BLOCK
        hot = jnp.where(gid_ref[...] == row.astype(F32), 1.0, 0.0).astype(BF16)
        total = dot(hot, g_ref[...])
        high = total.astype(BF16)
        low = (total - high.astype(F32)).astype(BF16)
        high_ref[rows, :] = high
        low_ref[rows, :] = low


def gradients(x, logits, probs, gid, live):
    return pl.pallas_call(
        grad_kernel,
        out_shape=(
            jax.ShapeDtypeStruct((ROWS, LOCAL), BF16),
            jax.ShapeDtypeStruct((ROWS, LOCAL), BF16),
            jax.ShapeDtypeStruct((1, 1), F32),
        ),
        in_specs=[VMEM] * 5,
        out_specs=(VMEM, VMEM, SMEM),
        scratch_shapes=[
            pltpu.VMEM((ROWS, 3 * LOCAL), BF16),
            pltpu.VMEM((ROWS, LOCAL), BF16),
        ],
        compiler_params=PARAMS,
    )(x, logits, probs, gid, live)


def weight_kernel(x_ref, own_ref, other_ref, o_ref):
    for k in range(4):
        at = lax.rem(x_ref[0] + k, 4)
        cols = pl.ds(k * LOCAL, LOCAL)
        o_ref[0:LOCAL, cols] = own_ref[at].T
        o_ref[LOCAL : 2 * LOCAL, cols] = other_ref[at].T


def pair_weights(x, own, other):
    return pl.pallas_call(
        weight_kernel,
        out_shape=jax.ShapeDtypeStruct((2 * LOCAL, 4 * LOCAL), BF16),
        in_specs=[SMEM, VMEM, VMEM],
        out_specs=VMEM,
        compiler_params=PARAMS,
    )(x, own, other)


ROWS2 = ROWS // 2


def term_kernel(own_ref, other_ref, w_ref, c0, l1, h1, l2, h2, l3, h3, g_ref):
    g_ref[:, 0:LOCAL] = own_ref[...]
    g_ref[:, LOCAL:] = other_ref[...]
    outs = {1: (l1, h1), 2: (l2, h2), 3: (l3, h3)}

    for i in range(2):
        rows = pl.ds(i * ROWS2, ROWS2)
        val = dot(g_ref[rows, :], w_ref[...])
        c0[rows, :] = val[:, 0:LOCAL]
        for k in range(1, 4):
            outs[k][i][...] = val[:, k * LOCAL : (k + 1) * LOCAL]


def terms(own, other, weights):
    part = jax.ShapeDtypeStruct((ROWS2, LOCAL), F32)
    return pl.pallas_call(
        term_kernel,
        out_shape=(jax.ShapeDtypeStruct((ROWS, LOCAL), F32),) + (part,) * 6,
        in_specs=[VMEM] * 3,
        out_specs=(VMEM,) * 7,
        scratch_shapes=[pltpu.VMEM((ROWS, 2 * LOCAL), BF16)],
        compiler_params=PARAMS,
    )(own, other, weights)


HEAD_BLOCK = 256
HEAD_STEPS = HALF // HEAD_BLOCK


def head_kernel(c_ref, own_ref, other_ref, high_ref, low_ref, o_ref):
    i = pl.program_id(0)

    def work(t_ref):
        both = dot(t_ref[...], high_ref[...], ((0,), (0,)))
        both += dot(t_ref[...], low_ref[...], ((0,), (0,)))
        for j in range(LOCAL // 128):
            o_ref[pl.ds(j, HEAD_BLOCK, stride=LOCAL // 128), :] = both[:, j * 128 : (j + 1) * 128]

    @pl.when(i < HEAD_STEPS)
    def _():
        work(own_ref)

    @pl.when(i >= HEAD_STEPS)
    def _():
        work(other_ref)


def head_gradient(c, own, other, high, low):
    def place(i, c):
        mine = i < HEAD_STEPS
        side = jnp.where(mine, c[0], 1 - c[0])
        return (side * HEAD_STEPS + jnp.where(mine, i, i - HEAD_STEPS), 0)

    return pl.pallas_call(
        head_kernel,
        grid_spec=pltpu.PrefetchScalarGridSpec(
            num_scalar_prefetch=1,
            grid=(2 * HEAD_STEPS,),
            in_specs=[
                pl.BlockSpec((ROWS, HEAD_BLOCK), lambda i, c: (0, jnp.minimum(i, HEAD_STEPS - 1))),
                pl.BlockSpec((ROWS, HEAD_BLOCK), lambda i, c: (0, jnp.maximum(i - HEAD_STEPS, 0))),
                pl.BlockSpec((ROWS, LOCAL), lambda i, c: (0, 0)),
                pl.BlockSpec((ROWS, LOCAL), lambda i, c: (0, 0)),
            ],
            out_specs=pl.BlockSpec((HEAD_BLOCK * LOCAL // 128, 128), place),
        ),
        out_shape=jax.ShapeDtypeStruct((D * LOCAL // 128, 128), F32),
        compiler_params=PARAMS,
        cost_estimate=pl.CostEstimate(
            flops=4 * ROWS * D * LOCAL, bytes_accessed=12 * 1024 * 1024, transcendentals=0
        ),
    )(c, own, other, high, low)


PAIR = [(i, i ^ 1) for i in range(SHARDS)]
RIGHT = [(i, (i + 2) % SHARDS) for i in range(SHARDS)]
LEFT = [(i, (i - 2) % SHARDS) for i in range(SHARDS)]


def along_z(k):
    return [(i, (i // Y + k) % Z * Y + i % Y) for i in range(TRAINERS)]


def along_y(k):
    return [(i, i // Y * Y + (i + k) % Y) for i in range(TRAINERS)]


def gather_pieces(half):
    near = [half] + [lax.ppermute(half, "trainer", along_z(k)) for k in range(1, Z)]
    low0 = jnp.stack(near[: Z // 2])
    high0 = jnp.stack(near[Z // 2 :])
    low1 = lax.ppermute(low0, "trainer", along_y(1))
    high3 = lax.ppermute(high0, "trainer", along_y(-1))
    high1 = lax.ppermute(high0, "trainer", along_y(1))
    low3 = lax.ppermute(low0, "trainer", along_y(-1))
    low2 = lax.ppermute(low1, "trainer", along_y(1))
    high2 = lax.ppermute(high3, "trainer", along_y(-1))
    return low0, high0, low1, high1, low2, high2, low3, high3


def on_device(hidden_table, head_weight, targets, counts, dest, token):
    me = lax.axis_index("vocab")
    trainer = lax.axis_index("trainer")
    c = lax.rem(me, 2)
    x = me // 2
    at = jnp.stack([c, lax.rem(trainer, Y), trainer // Y]).astype(jnp.int32)
    c1 = c.reshape(1).astype(jnp.int32)
    x1 = x.reshape(1).astype(jnp.int32)
    weight = head_weight[:, 0, :]

    half = lax.dynamic_slice(hidden_table, (0, c * HALF), (SLOTS, HALF))
    pieces = gather_pieces(half)
    pieces += tuple(lax.ppermute(p, "vocab", PAIR) for p in pieces)

    moved = lax.all_to_all(
        split_targets(targets[:, 0, :]), "trainer", split_axis=0, concat_axis=0, tiled=True
    )
    probs = moved.reshape(ROWS, LOCAL)

    blocks = weight.reshape(4, 2, LOCAL, LOCAL)
    w_own = lax.dynamic_index_in_dim(blocks, c, axis=1, keepdims=False)
    w_give = lax.dynamic_index_in_dim(blocks, 1 - c, axis=1, keepdims=False)
    weights = pair_weights(x1, w_own, lax.ppermute(w_give, "vocab", PAIR))

    gid = dest * SLOTS + token
    index = jnp.arange(ROWS, dtype=jnp.int32)
    live = (index % SLOTS < jnp.repeat(counts, SLOTS)).astype(F32).reshape(1, ROWS)
    psum, mass = target_sums(gid.reshape(1, ROWS), live, probs)

    own, other, logits, stats = logits_and_stats(at, pieces, weight, psum, mass)
    stats = lax.all_to_all(stats, "vocab", split_axis=0, concat_axis=0, tiled=True)
    stats = lax.all_to_all(merge_stats(stats), "trainer", split_axis=0, concat_axis=0, tiled=True)

    high, low, loss = gradients(stats, logits, probs, gid.astype(F32).reshape(1, ROWS), live)
    mean_loss = loss[0, 0] / jnp.sum(counts).astype(F32)

    t0, l1, h1, l2, h2, l3, h3 = terms(high, lax.ppermute(high, "vocab", PAIR), weights)
    low_r = lax.ppermute(l2, "vocab", RIGHT)
    high_l = lax.ppermute(h2, "vocab", LEFT)
    high_r = lax.ppermute(h1, "vocab", RIGHT)
    low_l = lax.ppermute(l3, "vocab", LEFT)
    low_r = lax.ppermute(l1 + low_r, "vocab", RIGHT)
    high_l = lax.ppermute(h3 + high_l, "vocab", LEFT)
    head = head_gradient(c1, own, other, high, low)
    total = t0 + jnp.concatenate([low_r + low_l, high_r + high_l], axis=0)
    got = lax.all_to_all(
        total.reshape(TRAINERS, SLOTS, LOCAL), "trainer", split_axis=0, concat_axis=0, tiled=True
    )
    table_grad = jnp.sum(got, axis=0)
    return head.reshape(D, 1, LOCAL), table_grad, mean_loss


def solution(mesh):
    return jax.shard_map(
        on_device,
        mesh=mesh,
        in_specs=(
            P("trainer", None),
            P(None, "vocab", "trainer"),
            P("trainer", "vocab", None),
            P(),
            P(),
            P(),
        ),
        out_specs=(P(None, "vocab", "trainer"), P("trainer", "vocab"), P()),
        check_vma=False,
    )
```

```python
import functools
import math

import jax
import jax.numpy as jnp
from jax import lax
from jax.experimental import pallas as pl
from jax.experimental.pallas import tpu as pltpu
from jax.sharding import PartitionSpec as P

D = 3072
VOCAB = 98304
ROWS = 1024
TRAINERS = 32
SLOTS = 32
SHARDS = 8
LOCAL = VOCAB // (TRAINERS * SHARDS)
HALF = D // 2
BLOCK = 256
BF16 = jnp.bfloat16
F32 = jnp.float32
PARAMS = pltpu.CompilerParams(vmem_limit_bytes=24 * 1024 * 1024)
VMEM = pl.BlockSpec(memory_space=pltpu.VMEM)
SMEM = pl.BlockSpec(memory_space=pltpu.SMEM)


def dot(a, b, dims=((1,), (0,))):
    return lax.dot_general(a, b, (dims, ((), ())), preferred_element_type=F32)


def split_kernel(x_ref, o_ref):
    for j in range(TRAINERS):
        o_ref[j] = x_ref[:, j * LOCAL : (j + 1) * LOCAL]


def split_targets(x):
    return pl.pallas_call(
        split_kernel,
        out_shape=jax.ShapeDtypeStruct((TRAINERS, SLOTS, LOCAL), BF16),
        in_specs=[VMEM],
        out_specs=VMEM,
        compiler_params=PARAMS,
    )(x)


Z = 8
Y = 4
PIECE = (Z // 2, SLOTS, HALF)


def logit_kernel(at_ref, *refs):
    pieces, refs = refs[:16], refs[16:]
    w_ref, own_ref, other_ref, logits_ref, o_ref = refs
    c, y, z = at_ref[0], at_ref[1], at_ref[2]
    for side, tab_ref in enumerate((own_ref, other_ref)):
        for dy in range(Y):
            for dz in range(Z):
                z_at = lax.rem(z + Z - dz, Z)
                y_at = lax.rem(y + Y - dy, Y)
                piece = pieces[side * 8 + dy * 2 + dz // 4]
                rows = pl.ds(pl.multiple_of((z_at * Y + y_at) * SLOTS, SLOTS), SLOTS)
                tab_ref[rows, :] = piece[dz % 4]
    near = pl.ds(pl.multiple_of(c * HALF, HALF), HALF)
    far = pl.ds(pl.multiple_of((1 - c) * HALF, HALF), HALF)
    block = 2 * BLOCK

    @pl.loop(0, ROWS // block)
    def _(i):
        rows = pl.ds(pl.multiple_of(i * block, block), block)
        logits = dot(own_ref[rows, :], w_ref[near, :])
        logits += dot(other_ref[rows, :], w_ref[far, :])
        logits_ref[rows, :] = logits
        top = jnp.max(logits, axis=1, keepdims=True)
        lse = top + jnp.log(jnp.sum(jnp.exp(logits - top), axis=1, keepdims=True))
        flat = jnp.broadcast_to(lse, (block, 128)).T
        for j in range(block // 128):
            row = flat[0:1, j * 128 : (j + 1) * 128]
            for k in range(SHARDS):
                o_ref[k, pl.ds(i * (block // 128) + j, 1), :] = row


def logits_and_stats(at, pieces, weight):
    table = jax.ShapeDtypeStruct((ROWS, HALF), BF16)
    return pl.pallas_call(
        logit_kernel,
        out_shape=(
            table,
            table,
            jax.ShapeDtypeStruct((ROWS, LOCAL), F32),
            jax.ShapeDtypeStruct((SHARDS, 8, 128), F32),
        ),
        in_specs=[SMEM] + [VMEM] * 17,
        out_specs=(VMEM,) * 4,
        compiler_params=PARAMS,
    )(at, *pieces, weight)


def merge(x):
    top = jnp.max(x, axis=0)
    return top + jnp.log(jnp.sum(jnp.exp(x - top[None]), axis=0))


def merge_kernel(x_ref, o_ref):
    lse = merge(x_ref[...])
    for k in range(TRAINERS):
        o_ref[k] = lse


def merge_stats(x):
    return pl.pallas_call(
        merge_kernel,
        out_shape=jax.ShapeDtypeStruct((TRAINERS, 8, 128), F32),
        in_specs=[VMEM],
        out_specs=VMEM,
        compiler_params=PARAMS,
    )(x)


def column(row):
    return jnp.broadcast_to(row, (128, row.shape[1])).T


def grad_kernel(
    x_ref, logits_ref, p_ref, gid_ref, live_ref, high_ref, low_ref, loss_ref, parts_ref, gp_ref, lse_ref
):
    lse = merge(x_ref[...])
    for j in range(8):
        lse_ref[pl.ds(j * 128, 128), :] = column(lse[j : j + 1])
    for j in range(LOCAL // 128):
        cols = pl.ds(j * 128, 128)
        p = jnp.exp(logits_ref[:, cols] - lse_ref[...])
        first = p.astype(BF16)
        p = p - first.astype(F32)
        second = p.astype(BF16)
        third = (p - second.astype(F32)).astype(BF16)
        parts_ref[:, pl.ds(j * 128, 128)] = first
        parts_ref[:, pl.ds(LOCAL + j * 128, 128)] = second
        parts_ref[:, pl.ds(2 * LOCAL + j * 128, 128)] = third
    scale = VOCAB / math.sqrt(ROWS)

    @pl.loop(0, ROWS // BLOCK)
    def _(i):
        rows = pl.ds(pl.multiple_of(i * BLOCK, BLOCK), BLOCK)
        gid = column(gid_ref[:, rows])
        factor = column(live_ref[:, rows]) * scale
        lane = lax.broadcasted_iota(jnp.int32, (BLOCK, 128), 1).astype(F32)
        hot = jnp.concatenate(
            [
                jnp.where(gid == lane + float(128 * k), 1.0, 0.0).astype(BF16)
                for k in range(ROWS // 128)
            ],
            axis=1,
        )
        sel = dot(hot, parts_ref[...])
        p = sel[:, 0:LOCAL] + sel[:, LOCAL : 2 * LOCAL] + sel[:, 2 * LOCAL :]
        targets = p_ref[rows, :]
        diff = p - targets.astype(F32)
        for j in range(LOCAL // 128):
            cols = slice(j * 128, (j + 1) * 128)
            gp_ref[rows, cols] = (factor * diff[:, cols]).astype(BF16)
        gp_ref[rows, LOCAL:] = targets

    def total(i, loss):
        rows = pl.ds(pl.multiple_of(i * BLOCK, BLOCK), BLOCK)
        row = lax.broadcasted_iota(jnp.int32, (BLOCK, ROWS), 0) + i * BLOCK
        hot = jnp.where(gid_ref[...] == row.astype(F32), live_ref[...], 0.0).astype(BF16)
        sums = dot(hot, gp_ref[...])
        high = sums[:, 0:LOCAL].astype(BF16)
        high_ref[rows, :] = high
        low_ref[rows, :] = (sums[:, 0:LOCAL] - high.astype(F32)).astype(BF16)
        for j in range(LOCAL // 128):
            cols = pl.ds(j * 128, 128)
            gap = lse_ref[rows, :] - logits_ref[rows, cols]
            loss += jnp.sum(sums[:, LOCAL + j * 128 : LOCAL + (j + 1) * 128] * gap)
        return loss

    loss_ref[0, 0] = lax.fori_loop(0, ROWS // BLOCK, total, jnp.float32(0))


def gradients(x, logits, probs, gid, live):
    return pl.pallas_call(
        grad_kernel,
        out_shape=(
            jax.ShapeDtypeStruct((ROWS, LOCAL), BF16),
            jax.ShapeDtypeStruct((ROWS, LOCAL), BF16),
            jax.ShapeDtypeStruct((1, 1), F32),
        ),
        in_specs=[VMEM] * 5,
        out_specs=(VMEM, VMEM, SMEM),
        scratch_shapes=[
            pltpu.VMEM((ROWS, 3 * LOCAL), BF16),
            pltpu.VMEM((ROWS, 2 * LOCAL), BF16),
            pltpu.VMEM((ROWS, 128), F32),
        ],
        compiler_params=PARAMS,
    )(x, logits, probs, gid, live)


TOP = 32700.0
ROWS2 = ROWS // 2
TAIL = 16
I16 = jnp.int16


def exponent(x):
    return jnp.ceil(jnp.log(jnp.maximum(x, 1e-30) / TOP) * (256.0 / math.log(2.0)))


def power(e):
    return jnp.exp2(e * (1.0 / 256.0))


def to16(x):
    return x.astype(jnp.int32).astype(I16)


def from16(x):
    return x.astype(jnp.int32).astype(F32)


def encode(val):
    e = exponent(jnp.max(jnp.abs(val), axis=1, keepdims=True))
    return to16(jnp.round(val * power(-e))), jnp.broadcast_to(e, (128, 128)).T[0:1]


def write_message(out_ref, block_of):
    tail = []
    for j in range(ROWS2 // 128):
        code, e = encode(block_of(j))
        out_ref[pl.ds(j * 128, 128), :] = code
        tail.append(e)
    tail.append(jnp.zeros((TAIL - len(tail), 128), F32))
    tail = jnp.concatenate(tail, axis=0)
    tail = jnp.concatenate([tail] + [jnp.zeros_like(tail)] * (LOCAL // 128 - 1), axis=1)
    out_ref[pl.ds(ROWS2, TAIL), :] = to16(tail)


def read_message(ref, j):
    tail = from16(ref[pl.ds(ROWS2, TAIL), 0:128])
    scale = power(column(tail[j : j + 1]))
    rows = pl.ds(j * 128, 128)
    return [from16(ref[rows, k * 128 : (k + 1) * 128]) * scale for k in range(LOCAL // 128)]


MESSAGE = jax.ShapeDtypeStruct((ROWS2 + TAIL, LOCAL), I16)


def weight_kernel(x_ref, own_ref, other_ref, o_ref):
    for k in range(4):
        at = lax.rem(x_ref[0] + k, 4)
        cols = pl.ds(k * LOCAL, LOCAL)
        o_ref[0:LOCAL, cols] = own_ref[at].T
        o_ref[LOCAL : 2 * LOCAL, cols] = other_ref[at].T


def pair_weights(x, own, other):
    return pl.pallas_call(
        weight_kernel,
        out_shape=jax.ShapeDtypeStruct((2 * LOCAL, 4 * LOCAL), BF16),
        in_specs=[SMEM, VMEM, VMEM],
        out_specs=VMEM,
        compiler_params=PARAMS,
    )(x, own, other)


def term_kernel(own_ref, other_ref, w_ref, c0, l1, h1, l2, h2, l3, h3, g_ref, val_ref):
    g_ref[:, 0:LOCAL] = own_ref[...]
    g_ref[:, LOCAL:] = other_ref[...]
    outs = {2: (l2, h2), 1: (l1, h1), 3: (l3, h3)}
    for i in range(2):
        rows = pl.ds(i * ROWS2, ROWS2)
        val_ref[...] = dot(g_ref[rows, :], w_ref[...])
        c0[rows, :] = val_ref[:, 0:LOCAL]
        for k in (1, 2, 3):
            out, cols = outs[k][i], slice(k * LOCAL, (k + 1) * LOCAL)
            if out.dtype == F32:
                out[...] = val_ref[:, cols]
            else:
                write_message(out, lambda j: val_ref[pl.ds(j * 128, 128), cols])


def terms(own, other, weights):
    part = jax.ShapeDtypeStruct((ROWS2, LOCAL), F32)
    return pl.pallas_call(
        term_kernel,
        out_shape=(
            jax.ShapeDtypeStruct((ROWS, LOCAL), F32),
            part,
            MESSAGE,
            MESSAGE,
            MESSAGE,
            MESSAGE,
            part,
        ),
        in_specs=[VMEM] * 3,
        out_specs=(VMEM,) * 7,
        scratch_shapes=[
            pltpu.VMEM((ROWS, 2 * LOCAL), BF16),
            pltpu.VMEM((ROWS2, 4 * LOCAL), F32),
        ],
        compiler_params=PARAMS,
    )(own, other, weights)


def relay_kernel(own_ref, got_ref, out_ref):
    def block(j):
        got = jnp.concatenate(read_message(got_ref, j), axis=1)
        return own_ref[pl.ds(j * 128, 128), :] + got

    write_message(out_ref, block)


def relay(own, got):
    return pl.pallas_call(
        relay_kernel,
        out_shape=MESSAGE,
        in_specs=[VMEM] * 2,
        out_specs=VMEM,
        compiler_params=PARAMS,
    )(own, got)


PACKED = 3 * SLOTS + TAIL


def pack_kernel(loss_ref, own_ref, low_r, low_l, high_r, high_l, o_ref):
    loss = jnp.full((1, 128), loss_ref[0, 0], F32)
    e = exponent(jnp.abs(loss))
    whole = loss * power(-e)
    first = jnp.round(whole)
    rest = jnp.round((whole - first) * TOP)
    lane = lax.broadcasted_iota(jnp.int32, (1, 128), 1)
    loss = jnp.where(lane == 0, e, jnp.where(lane == 1, first, jnp.where(lane == 2, rest, 0.0)))
    pad = jnp.zeros((TAIL - 2, 128), F32)
    for i, (right, left) in enumerate(((low_r, low_l), (high_r, high_l))):
        for j in range(ROWS2 // 128):
            a, b = read_message(right, j), read_message(left, j)
            val = jnp.concatenate([p + q for p, q in zip(a, b)], axis=1)
            at = i * (ROWS2 // 128) + j
            code, e = encode(own_ref[pl.ds(at * 128, 128), :] + val)
            tail = to16(jnp.concatenate([e, loss, pad], axis=0))
            for n in range(128 // SLOTS):
                for k in range(3):
                    o_ref[at * 4 + n, k * SLOTS : (k + 1) * SLOTS, :] = code[
                        n * SLOTS : (n + 1) * SLOTS, k * 128 : (k + 1) * 128
                    ]
                o_ref[at * 4 + n, 3 * SLOTS :, :] = tail


def pack(loss, own, low_r, low_l, high_r, high_l):
    return pl.pallas_call(
        pack_kernel,
        out_shape=jax.ShapeDtypeStruct((TRAINERS, PACKED, 128), I16),
        in_specs=[SMEM] + [VMEM] * 5,
        out_specs=VMEM,
        compiler_params=PARAMS,
    )(loss, own, low_r, low_l, high_r, high_l)


def finish_kernel(at_ref, x_ref, grad_ref, loss_ref, e_ref):
    tail = from16(x_ref[:, 3 * SLOTS :, :])
    e = tail[:, 0, :]
    e_ref[...] = jnp.concatenate([e, jnp.zeros((128 - TRAINERS, 128), F32)], axis=0).T
    scale = power(e_ref[pl.ds(pl.multiple_of(at_ref[0] * SLOTS, SLOTS), SLOTS), :])
    total = [jnp.zeros((SLOTS, 128), F32)] * 3
    for s in range(TRAINERS):
        for k in range(3):
            total[k] += from16(x_ref[s, k * SLOTS : (k + 1) * SLOTS, :]) * scale[:, s : s + 1]
    for k in range(3):
        grad_ref[:, k * 128 : (k + 1) * 128] = total[k]
    loss = tail[:, 1, :]
    loss_ref[0, 0] = jnp.sum((loss[:, 1:2] + loss[:, 2:3] * (1.0 / TOP)) * power(loss[:, 0:1]))


def finish(at, x):
    return pl.pallas_call(
        finish_kernel,
        out_shape=(
            jax.ShapeDtypeStruct((SLOTS, LOCAL), F32),
            jax.ShapeDtypeStruct((1, 1), F32),
        ),
        in_specs=[SMEM, VMEM],
        out_specs=(VMEM, SMEM),
        scratch_shapes=[pltpu.VMEM((128, 128), F32)],
        compiler_params=PARAMS,
    )(at, x)


HEAD_BLOCK = 256
HEAD_STEPS = HALF // HEAD_BLOCK


def head_kernel(c_ref, own_ref, other_ref, high_ref, low_ref, o_ref):
    i = pl.program_id(0)

    def work(t_ref):
        both = dot(t_ref[...], high_ref[...], ((0,), (0,)))
        both += dot(t_ref[...], low_ref[...], ((0,), (0,)))
        for j in range(LOCAL // 128):
            o_ref[pl.ds(j, HEAD_BLOCK, stride=LOCAL // 128), :] = both[:, j * 128 : (j + 1) * 128]

    @pl.when(i < HEAD_STEPS)
    def _():
        work(own_ref)

    @pl.when(i >= HEAD_STEPS)
    def _():
        work(other_ref)


def head_gradient(c, own, other, high, low):
    def place(i, c):
        mine = i < HEAD_STEPS
        side = jnp.where(mine, c[0], 1 - c[0])
        return (side * HEAD_STEPS + jnp.where(mine, i, i - HEAD_STEPS), 0)

    return pl.pallas_call(
        head_kernel,
        grid_spec=pltpu.PrefetchScalarGridSpec(
            num_scalar_prefetch=1,
            grid=(2 * HEAD_STEPS,),
            in_specs=[
                pl.BlockSpec((ROWS, HEAD_BLOCK), lambda i, c: (0, jnp.minimum(i, HEAD_STEPS - 1))),
                pl.BlockSpec((ROWS, HEAD_BLOCK), lambda i, c: (0, jnp.maximum(i - HEAD_STEPS, 0))),
                pl.BlockSpec((ROWS, LOCAL), lambda i, c: (0, 0)),
                pl.BlockSpec((ROWS, LOCAL), lambda i, c: (0, 0)),
            ],
            out_specs=pl.BlockSpec((HEAD_BLOCK * LOCAL // 128, 128), place),
        ),
        out_shape=jax.ShapeDtypeStruct((D * LOCAL // 128, 128), F32),
        compiler_params=PARAMS,
        cost_estimate=pl.CostEstimate(
            flops=4 * ROWS * D * LOCAL, bytes_accessed=12 * 1024 * 1024, transcendentals=0
        ),
    )(c, own, other, high, low)


PAIR = [(i, i ^ 1) for i in range(SHARDS)]
RIGHT = [(i, (i + 2) % SHARDS) for i in range(SHARDS)]
LEFT = [(i, (i - 2) % SHARDS) for i in range(SHARDS)]


def along_z(k):
    return [(i, (i // Y + k) % Z * Y + i % Y) for i in range(TRAINERS)]


def along_y(k):
    return [(i, i // Y * Y + (i + k) % Y) for i in range(TRAINERS)]


def gather_pieces(half, targets):
    near = [half] + [lax.ppermute(half, "trainer", along_z(k)) for k in range(1, Z)]
    low0 = jnp.stack(near[: Z // 2])
    high0 = jnp.stack(near[Z // 2 :])
    low1 = lax.ppermute(low0, "trainer", along_y(1))
    high3 = lax.ppermute(high0, "trainer", along_y(-1))
    high1 = lax.ppermute(high0, "trainer", along_y(1))
    low3 = lax.ppermute(low0, "trainer", along_y(-1))
    targets, _ = lax.optimization_barrier((targets, high0))
    probs = lax.all_to_all(targets, "trainer", split_axis=0, concat_axis=0, tiled=True)
    low2 = lax.ppermute(low1, "trainer", along_y(1))
    high2 = lax.ppermute(high3, "trainer", along_y(-1))
    return (low0, high0, low1, high1, low2, high2, low3, high3), probs.reshape(ROWS, LOCAL)


def on_device(hidden_table, head_weight, targets, counts, dest, token):
    me = lax.axis_index("vocab")
    trainer = lax.axis_index("trainer")
    c = lax.rem(me, 2)
    x = me // 2
    at = jnp.stack([c, lax.rem(trainer, Y), trainer // Y]).astype(jnp.int32)
    c1 = c.reshape(1).astype(jnp.int32)
    x1 = x.reshape(1).astype(jnp.int32)
    weight = head_weight[:, 0, :]

    half = lax.dynamic_slice(hidden_table, (0, c * HALF), (SLOTS, HALF))
    pieces, probs = gather_pieces(half, split_targets(targets[:, 0, :]))
    pieces += tuple(lax.ppermute(p, "vocab", PAIR) for p in pieces)

    blocks = weight.reshape(4, 2, LOCAL, LOCAL)
    w_own = lax.dynamic_index_in_dim(blocks, c, axis=1, keepdims=False)
    w_give = lax.dynamic_index_in_dim(blocks, 1 - c, axis=1, keepdims=False)
    weights = pair_weights(x1, w_own, lax.ppermute(w_give, "vocab", PAIR))

    gid = dest * SLOTS + token
    index = jnp.arange(ROWS, dtype=jnp.int32)
    live = (index % SLOTS < jnp.repeat(counts, SLOTS)).astype(F32).reshape(1, ROWS)

    at, weights = lax.optimization_barrier((at, weights))
    own, other, logits, stats = logits_and_stats(at, pieces, weight)
    stats = lax.all_to_all(stats, "vocab", split_axis=0, concat_axis=0, tiled=True)
    stats = lax.all_to_all(merge_stats(stats), "trainer", split_axis=0, concat_axis=0, tiled=True)

    high, low, loss = gradients(stats, logits, probs, gid.astype(F32).reshape(1, ROWS), live)

    t0, l1, h1, l2, h2, l3, h3 = terms(high, lax.ppermute(high, "vocab", PAIR), weights)
    low_r = lax.ppermute(l2, "vocab", RIGHT)
    high_l = lax.ppermute(h2, "vocab", LEFT)
    high_r = lax.ppermute(h1, "vocab", RIGHT)
    low_l = lax.ppermute(l3, "vocab", LEFT)
    low_r = lax.ppermute(relay(l1, low_r), "vocab", RIGHT)
    high_l = lax.ppermute(relay(h3, high_l), "vocab", LEFT)
    head = head_gradient(c1, own, other, high, low)
    loss = lax.psum(loss, "vocab")
    packed = pack(loss, t0, low_r, low_l, high_r, high_l)
    packed = lax.all_to_all(packed, "trainer", split_axis=0, concat_axis=0, tiled=True)
    table_grad, loss = finish(lax.rem(trainer, 4).reshape(1).astype(jnp.int32), packed)
    mean_loss = loss[0, 0] / jnp.sum(counts).astype(F32)
    return head.reshape(D, 1, LOCAL), table_grad, mean_loss


def solution(mesh):
    return jax.shard_map(
        on_device,
        mesh=mesh,
        in_specs=(
            P("trainer", None),
            P(None, "vocab", "trainer"),
            P("trainer", "vocab", None),
            P(),
            P(),
            P(),
        ),
        out_specs=(P(None, "vocab", "trainer"), P("trainer", "vocab"), P()),
        check_vma=False,
    )
```

```python
import functools
import math

import jax
import jax.numpy as jnp
from jax import lax
from jax.experimental import pallas as pl
from jax.experimental.pallas import tpu as pltpu
from jax.sharding import PartitionSpec as P

D = 3072
VOCAB = 98304
ROWS = 1024
TRAINERS = 32
SLOTS = 32
SHARDS = 8
LOCAL = VOCAB // (TRAINERS * SHARDS)
HALF = D // 2
BLOCK = 256
BF16 = jnp.bfloat16
F32 = jnp.float32
PARAMS = pltpu.CompilerParams(vmem_limit_bytes=24 * 1024 * 1024)
FULL = pltpu.CompilerParams(vmem_limit_bytes=60 * 1024 * 1024)
VMEM = pl.BlockSpec(memory_space=pltpu.VMEM)
SMEM = pl.BlockSpec(memory_space=pltpu.SMEM)
ANY = pl.BlockSpec(memory_space=pl.ANY)


def dot(a, b, dims=((1,), (0,))):
    return lax.dot_general(a, b, (dims, ((), ())), preferred_element_type=F32)


def split_kernel(x_ref, o_ref):
    for j in range(TRAINERS):
        o_ref[j] = x_ref[:, j * LOCAL : (j + 1) * LOCAL]


def split_targets(x):
    return pl.pallas_call(
        split_kernel,
        out_shape=jax.ShapeDtypeStruct((TRAINERS, SLOTS, LOCAL), BF16),
        in_specs=[VMEM],
        out_specs=VMEM,
        compiler_params=FULL,
    )(x)


Z = 8
Y = 4


def order_kernel(z_ref, *refs):
    pieces, (low_ref, high_ref, sems) = refs[:Z], refs[Z:]
    for start in (True, False):
        for k, piece in enumerate(pieces):
            at = lax.rem(z_ref[0] + Z - k, Z)
            for side, out in enumerate((low_ref, high_ref)):

                @pl.when(at // (Z // 2) == side)
                def _():
                    copy = pltpu.make_async_copy(piece, out.at[lax.rem(at, Z // 2)], sems.at[k])
                    copy.start() if start else copy.wait()


def in_order(z, pieces):
    half = jax.ShapeDtypeStruct((Z // 2, SLOTS, HALF), BF16)
    return pl.pallas_call(
        order_kernel,
        out_shape=(half, half),
        in_specs=[SMEM] + [ANY] * Z,
        out_specs=(ANY, ANY),
        scratch_shapes=[pltpu.SemaphoreType.DMA((Z,))],
        compiler_params=FULL,
    )(z, *pieces)


def logit_kernel(at_ref, *refs):
    pieces, refs = refs[:16], refs[16:]
    far_ref, own_ref, other_ref, logits_ref, o_ref, tabs, w_ref, logit_buf, in_sems, out_sems = refs
    c, y = at_ref[0], at_ref[1]
    copies = [[], []]
    for side in range(2):
        rows = pl.ds(pl.multiple_of((c + side) % 2 * HALF, HALF), HALF)
        copies[side].append(
            pltpu.make_async_copy(far_ref.at[rows], w_ref.at[side], in_sems.at[16 + side])
        )
        for dy in range(Y):
            y_at = lax.rem(y + Y - dy, Y)
            for high in range(2):
                n = side * 8 + dy * 2 + high
                place = tabs.at[side, pl.ds(high * (Z // 2), Z // 2), y_at]
                copies[side].append(pltpu.make_async_copy(pieces[n], place, in_sems.at[n]))
        for copy in copies[side]:
            copy.start()
    block = 2 * BLOCK
    step = block // (Y * SLOTS)
    stores = []
    for side, out in enumerate((own_ref, other_ref)):
        for copy in copies[side]:
            copy.wait()
        stores.append(pltpu.make_async_copy(tabs.at[side], out, out_sems.at[side]))
        stores[-1].start()
        for i in range(ROWS // block):
            rows = pl.ds(i * block, block)
            part = dot(tabs[side, pl.ds(i * step, step)].reshape(block, HALF), w_ref[side])
            if side == 0:
                logit_buf[rows, :] = part
                continue
            logits = logit_buf[rows, :] + part
            logit_buf[rows, :] = logits
            stores.append(
                pltpu.make_async_copy(logit_buf.at[rows], logits_ref.at[rows], out_sems.at[2 + i])
            )
            stores[-1].start()
            top = jnp.max(logits, axis=1, keepdims=True)
            lse = top + jnp.log(jnp.sum(jnp.exp(logits - top), axis=1, keepdims=True))
            flat = jnp.broadcast_to(lse, (block, 128)).T
            for j in range(block // 128):
                row = flat[0:1, j * 128 : (j + 1) * 128]
                o_ref[pl.ds(i * (block // 128) + j, 1), :] = row
    for store in stores:
        store.wait()


def logits_and_stats(at, pieces, weight):
    table = jax.ShapeDtypeStruct((Z, Y, SLOTS, HALF), BF16)
    own, other, logits, stats = pl.pallas_call(
        logit_kernel,
        out_shape=(
            table,
            table,
            jax.ShapeDtypeStruct((ROWS, LOCAL), F32),
            jax.ShapeDtypeStruct((8, 128), F32),
        ),
        in_specs=[SMEM] + [ANY] * 17,
        out_specs=(ANY, ANY, ANY, VMEM),
        scratch_shapes=[
            pltpu.VMEM((2, Z, Y, SLOTS, HALF), BF16),
            pltpu.VMEM((2, HALF, LOCAL), BF16),
            pltpu.VMEM((ROWS, LOCAL), F32),
            pltpu.SemaphoreType.DMA((18,)),
            pltpu.SemaphoreType.DMA((4,)),
        ],
        compiler_params=FULL,
    )(at, *pieces, weight)
    return own.reshape(ROWS, HALF), other.reshape(ROWS, HALF), logits, stats


def merge(x):
    top = jnp.max(x, axis=0)
    return top + jnp.log(jnp.sum(jnp.exp(x - top[None]), axis=0))


def merge_kernel(copies, *refs):
    lse = merge(jnp.stack([ref[...] for ref in refs[:-1]]))
    if copies == 1:
        refs[-1][...] = lse
    for k in range(copies if copies > 1 else 0):
        refs[-1][k] = lse


def merge_stats(parts, copies=1):
    shape = (8, 128) if copies == 1 else (copies, 8, 128)
    return pl.pallas_call(
        functools.partial(merge_kernel, copies),
        out_shape=jax.ShapeDtypeStruct(shape, F32),
        in_specs=[VMEM] * len(parts),
        out_specs=VMEM,
        compiler_params=PARAMS if copies == 1 else FULL,
    )(*parts)


def column(row):
    return jnp.broadcast_to(row, (128, row.shape[1])).T


def grad_kernel(
    x_ref, far_ref, targets_ref, gid_ref, live_ref, high_ref, both_ref, loss_ref, *scratch
):
    parts_ref, gp_ref, lse_ref, logits_ref, p_ref, sums_ref, sems = scratch
    fetch = pltpu.make_async_copy(far_ref, logits_ref, sems.at[0])
    fetch.start()
    fetch_targets = pltpu.make_async_copy(targets_ref, p_ref, sems.at[1])
    fetch_targets.start()
    lse = merge(x_ref[...])
    for j in range(8):
        lse_ref[pl.ds(j * 128, 128), :] = column(lse[j : j + 1])
    fetch.wait()
    for j in range(LOCAL // 128):
        cols = pl.ds(j * 128, 128)
        p = jnp.exp(logits_ref[:, cols] - lse_ref[...])
        first = p.astype(BF16)
        p = p - first.astype(F32)
        second = p.astype(BF16)
        third = (p - second.astype(F32)).astype(BF16)
        parts_ref[:, pl.ds(j * 128, 128)] = first
        parts_ref[:, pl.ds(LOCAL + j * 128, 128)] = second
        parts_ref[:, pl.ds(2 * LOCAL + j * 128, 128)] = third
    scale = VOCAB / math.sqrt(ROWS)
    fetch_targets.wait()

    @pl.loop(0, ROWS // BLOCK)
    def _(i):
        rows = pl.ds(pl.multiple_of(i * BLOCK, BLOCK), BLOCK)
        gid = column(gid_ref[:, rows])
        factor = column(live_ref[:, rows]) * scale
        lane = lax.broadcasted_iota(jnp.int32, (BLOCK, 128), 1).astype(F32)
        hot = jnp.concatenate(
            [
                jnp.where(gid == lane + float(128 * k), 1.0, 0.0).astype(BF16)
                for k in range(ROWS // 128)
            ],
            axis=1,
        )
        sel = dot(hot, parts_ref[...])
        p = sel[:, 0:LOCAL] + sel[:, LOCAL : 2 * LOCAL] + sel[:, 2 * LOCAL :]
        targets = p_ref[rows, :]
        diff = p - targets.astype(F32)
        for j in range(LOCAL // 128):
            cols = slice(j * 128, (j + 1) * 128)
            gp_ref[rows, cols] = (factor * diff[:, cols]).astype(BF16)
        gp_ref[rows, LOCAL:] = targets

    def stores(rows, i):
        high = sums_ref.at[rows, pl.ds(0, LOCAL)]
        yield pltpu.make_async_copy(high, high_ref.at[rows], sems.at[2 + i])
        yield pltpu.make_async_copy(sums_ref.at[rows], both_ref.at[rows], sems.at[6 + i])

    def total(i, loss):
        rows = pl.ds(pl.multiple_of(i * BLOCK, BLOCK), BLOCK)
        row = lax.broadcasted_iota(jnp.int32, (BLOCK, ROWS), 0) + i * BLOCK
        hot = jnp.where(gid_ref[...] == row.astype(F32), live_ref[...], 0.0).astype(BF16)
        sums = dot(hot, gp_ref[...])
        high = sums[:, 0:LOCAL].astype(BF16)
        sums_ref[rows, 0:LOCAL] = high
        sums_ref[rows, LOCAL:] = (sums[:, 0:LOCAL] - high.astype(F32)).astype(BF16)
        for store in stores(rows, i):
            store.start()
        for j in range(LOCAL // 128):
            cols = pl.ds(j * 128, 128)
            gap = lse_ref[rows, :] - logits_ref[rows, cols]
            loss += jnp.sum(sums[:, LOCAL + j * 128 : LOCAL + (j + 1) * 128] * gap)
        return loss

    loss_ref[0, 0] = lax.fori_loop(0, ROWS // BLOCK, total, jnp.float32(0))
    for i in range(ROWS // BLOCK):
        for store in stores(pl.ds(i * BLOCK, BLOCK), i):
            store.wait()


def gradients(x, logits, probs, gid, live):
    return pl.pallas_call(
        grad_kernel,
        out_shape=(
            jax.ShapeDtypeStruct((ROWS, LOCAL), BF16),
            jax.ShapeDtypeStruct((ROWS, 2 * LOCAL), BF16),
            jax.ShapeDtypeStruct((1, 1), F32),
        ),
        in_specs=[VMEM, ANY, ANY, VMEM, VMEM],
        out_specs=(ANY, ANY, SMEM),
        scratch_shapes=[
            pltpu.VMEM((ROWS, 3 * LOCAL), BF16),
            pltpu.VMEM((ROWS, 2 * LOCAL), BF16),
            pltpu.VMEM((ROWS, 128), F32),
            pltpu.VMEM((ROWS, LOCAL), F32),
            pltpu.VMEM((ROWS, LOCAL), BF16),
            pltpu.VMEM((ROWS, 2 * LOCAL), BF16),
            pltpu.SemaphoreType.DMA((10,)),
        ],
        compiler_params=FULL,
    )(x, logits, probs, gid, live)


TOP = 32700.0
ROWS2 = ROWS // 2
TAIL = 16
I16 = jnp.int16


def exponent(x):
    return jnp.ceil(jnp.log(jnp.maximum(x, 1e-30) / TOP) * (256.0 / math.log(2.0)))


def power(e):
    return jnp.exp2(e * (1.0 / 256.0))


def to16(x):
    return x.astype(jnp.int32).astype(I16)


def from16(x):
    return x.astype(jnp.int32).astype(F32)


def encode(val):
    e = exponent(jnp.max(jnp.abs(val), axis=1, keepdims=True))
    return to16(jnp.round(val * power(-e))), jnp.broadcast_to(e, (128, 128)).T[0:1]


def wide(row):
    return jnp.concatenate([row] + [jnp.zeros_like(row)] * (LOCAL // 128 - 1), axis=1)


def write_message(out_ref, block_of, loss):
    tail = []
    for j in range(ROWS2 // 128):
        code, e = encode(block_of(j))
        out_ref[pl.ds(j * 128, 128), :] = code
        tail.append(e)
    tail += [loss, jnp.zeros((TAIL - len(tail) - 1, 128), F32)]
    out_ref[pl.ds(ROWS2, TAIL), :] = to16(wide(jnp.concatenate(tail, axis=0)))


def encode_loss(loss):
    e = exponent(jnp.abs(loss))
    whole = loss * power(-e)
    first = jnp.round(whole)
    rest = jnp.round((whole - first) * TOP)
    lane = lax.broadcasted_iota(jnp.int32, (1, 128), 1)
    return jnp.where(lane == 0, e, jnp.where(lane == 1, first, jnp.where(lane == 2, rest, 0.0)))


def decode_loss(code):
    return (code[:, 1:2] + code[:, 2:3] * (1.0 / TOP)) * power(code[:, 0:1])


def message_loss(ref):
    return from16(ref[pl.ds(ROWS2, TAIL), 0:128])[ROWS2 // 128 : ROWS2 // 128 + 1]


def read_message(ref, j):
    tail = from16(ref[pl.ds(ROWS2, TAIL), 0:128])
    scale = power(column(tail[j : j + 1]))
    rows = pl.ds(j * 128, 128)
    return [from16(ref[rows, k * 128 : (k + 1) * 128]) * scale for k in range(LOCAL // 128)]


MESSAGE = jax.ShapeDtypeStruct((ROWS2 + TAIL, LOCAL), I16)


def weight_kernel(at_ref, all_ref, other_ref, o_ref, own_ref, sems):
    c, x = at_ref[0], at_ref[1]
    fetches = [
        pltpu.make_async_copy(all_ref.at[lax.rem(x + k, 4), c], own_ref.at[k], sems.at[k])
        for k in range(4)
    ]
    for fetch in fetches:
        fetch.start()
    for k in range(4):
        o_ref[LOCAL : 2 * LOCAL, k * LOCAL : (k + 1) * LOCAL] = other_ref[lax.rem(x + k, 4)].T
    for k in range(4):
        fetches[k].wait()
        o_ref[0:LOCAL, k * LOCAL : (k + 1) * LOCAL] = own_ref[k].T


def pair_weights(at, blocks, other):
    return pl.pallas_call(
        weight_kernel,
        out_shape=jax.ShapeDtypeStruct((2 * LOCAL, 4 * LOCAL), BF16),
        in_specs=[SMEM, ANY, VMEM],
        out_specs=VMEM,
        scratch_shapes=[
            pltpu.VMEM((4, LOCAL, LOCAL), BF16),
            pltpu.SemaphoreType.DMA((4,)),
        ],
        compiler_params=FULL,
    )(at, blocks, other)


def term_kernel(
    loss_ref, more_ref, own_ref, other_ref, w_ref, c0, l1, h1, l2, h2, l3, h3, sum_ref, *scratch
):
    g_ref, val_ref, sems = scratch
    fetches = [
        pltpu.make_async_copy(ref, g_ref.at[:, pl.ds(k * LOCAL, LOCAL)], sems.at[k])
        for k, ref in enumerate((own_ref, other_ref))
    ]
    for fetch in fetches:
        fetch.start()
    loss = encode_loss(jnp.full((1, 128), loss_ref[0, 0] + more_ref[0, 0], F32))
    sum_ref[...] = loss
    for fetch in fetches:
        fetch.wait()
    outs = {2: (l2, h2), 1: (l1, h1), 3: (l3, h3)}
    for i in range(2):
        rows = pl.ds(i * ROWS2, ROWS2)
        val_ref[...] = dot(g_ref[rows, :], w_ref[...])
        c0[rows, :] = val_ref[:, 0:LOCAL]
        for k in (1, 2, 3):
            out, cols = outs[k][i], slice(k * LOCAL, (k + 1) * LOCAL)
            if out.dtype == F32:
                out[...] = val_ref[:, cols]
            else:
                write_message(out, lambda j: val_ref[pl.ds(j * 128, 128), cols], loss)


def terms(loss, more, own, other, weights):
    part = jax.ShapeDtypeStruct((ROWS2, LOCAL), F32)
    return pl.pallas_call(
        term_kernel,
        out_shape=(
            jax.ShapeDtypeStruct((ROWS, LOCAL), F32),
            part,
            MESSAGE,
            MESSAGE,
            MESSAGE,
            MESSAGE,
            part,
            jax.ShapeDtypeStruct((1, 128), F32),
        ),
        in_specs=[SMEM, SMEM, ANY, ANY, VMEM],
        out_specs=(VMEM,) * 8,
        scratch_shapes=[
            pltpu.VMEM((ROWS, 2 * LOCAL), BF16),
            pltpu.VMEM((ROWS2, 4 * LOCAL), F32),
            pltpu.SemaphoreType.DMA((2,)),
        ],
        compiler_params=PARAMS,
    )(loss, more, own, other, weights)


def relay_kernel(own_ref, got_ref, out_ref):
    def block(j):
        got = jnp.concatenate(read_message(got_ref, j), axis=1)
        return own_ref[pl.ds(j * 128, 128), :] + got

    write_message(out_ref, block, message_loss(got_ref))


def relay(own, got):
    return pl.pallas_call(
        relay_kernel,
        out_shape=MESSAGE,
        in_specs=[VMEM] * 2,
        out_specs=VMEM,
        compiler_params=PARAMS,
    )(own, got)


PACKED = 3 * SLOTS + TAIL


def pack_kernel(loss_ref, own_ref, low_r, low_l, high_r, high_l, o_ref):
    codes = [loss_ref[...]] + [message_loss(ref) for ref in (low_r, low_l, high_r)]
    loss = decode_loss(jnp.concatenate(codes, axis=0))
    loss = (loss[0:1] + loss[1:2]) + (loss[2:3] + loss[3:4])
    loss = encode_loss(jnp.broadcast_to(loss, (1, 128)))
    pad = jnp.zeros((TAIL - 2, 128), F32)
    for i, (right, left) in enumerate(((low_r, low_l), (high_r, high_l))):
        for j in range(ROWS2 // 128):
            a, b = read_message(right, j), read_message(left, j)
            val = jnp.concatenate([p + q for p, q in zip(a, b)], axis=1)
            at = i * (ROWS2 // 128) + j
            code, e = encode(own_ref[pl.ds(at * 128, 128), :] + val)
            tail = to16(jnp.concatenate([e, loss, pad], axis=0))
            for n in range(128 // SLOTS):
                for k in range(3):
                    o_ref[at * 4 + n, k * SLOTS : (k + 1) * SLOTS, :] = code[
                        n * SLOTS : (n + 1) * SLOTS, k * 128 : (k + 1) * 128
                    ]
                o_ref[at * 4 + n, 3 * SLOTS :, :] = tail


def pack(loss, own, low_r, low_l, high_r, high_l):
    return pl.pallas_call(
        pack_kernel,
        out_shape=jax.ShapeDtypeStruct((TRAINERS, PACKED, 128), I16),
        in_specs=[VMEM] * 6,
        out_specs=VMEM,
        compiler_params=PARAMS,
    )(loss, own, low_r, low_l, high_r, high_l)


def finish_kernel(at_ref, x_ref, grad_ref, loss_ref, e_ref):
    tail = from16(x_ref[:, 3 * SLOTS :, :])
    e = tail[:, 0, :]
    e_ref[...] = jnp.concatenate([e, jnp.zeros((128 - TRAINERS, 128), F32)], axis=0).T
    scale = power(e_ref[pl.ds(pl.multiple_of(at_ref[0] * SLOTS, SLOTS), SLOTS), :])
    total = [jnp.zeros((SLOTS, 128), F32)] * 3
    for s in range(TRAINERS):
        for k in range(3):
            total[k] += from16(x_ref[s, k * SLOTS : (k + 1) * SLOTS, :]) * scale[:, s : s + 1]
    for k in range(3):
        grad_ref[:, k * 128 : (k + 1) * 128] = total[k]
    loss_ref[0, 0] = jnp.sum(decode_loss(tail[:, 1, :]))


def finish(at, x):
    return pl.pallas_call(
        finish_kernel,
        out_shape=(
            jax.ShapeDtypeStruct((SLOTS, LOCAL), F32),
            jax.ShapeDtypeStruct((1, 1), F32),
        ),
        in_specs=[SMEM, VMEM],
        out_specs=(VMEM, SMEM),
        scratch_shapes=[pltpu.VMEM((128, 128), F32)],
        compiler_params=PARAMS,
    )(at, x)


HEAD_BLOCK = 256
HEAD_STEPS = HALF // HEAD_BLOCK


def head_kernel(c_ref, own_ref, other_ref, sums_ref, o_ref):
    i = pl.program_id(0)

    def work(t_ref):
        both = dot(t_ref[...], sums_ref[...], ((0,), (0,)))
        both = both[:, 0:LOCAL] + both[:, LOCAL:]
        for j in range(LOCAL // 128):
            o_ref[pl.ds(j, HEAD_BLOCK, stride=LOCAL // 128), :] = both[:, j * 128 : (j + 1) * 128]

    @pl.when(i < HEAD_STEPS)
    def _():
        work(own_ref)

    @pl.when(i >= HEAD_STEPS)
    def _():
        work(other_ref)


def head_gradient(c, own, other, sums):
    def place(i, c):
        mine = i < HEAD_STEPS
        side = jnp.where(mine, c[0], 1 - c[0])
        return (side * HEAD_STEPS + jnp.where(mine, i, i - HEAD_STEPS), 0)

    return pl.pallas_call(
        head_kernel,
        grid_spec=pltpu.PrefetchScalarGridSpec(
            num_scalar_prefetch=1,
            grid=(2 * HEAD_STEPS,),
            in_specs=[
                pl.BlockSpec((ROWS, HEAD_BLOCK), lambda i, c: (0, jnp.minimum(i, HEAD_STEPS - 1))),
                pl.BlockSpec((ROWS, HEAD_BLOCK), lambda i, c: (0, jnp.maximum(i - HEAD_STEPS, 0))),
                pl.BlockSpec((ROWS, 2 * LOCAL), lambda i, c: (0, 0)),
            ],
            out_specs=pl.BlockSpec((HEAD_BLOCK * LOCAL // 128, 128), place),
        ),
        out_shape=jax.ShapeDtypeStruct((D * LOCAL // 128, 128), F32),
        compiler_params=PARAMS,
        cost_estimate=pl.CostEstimate(
            flops=4 * ROWS * D * LOCAL, bytes_accessed=12 * 1024 * 1024, transcendentals=0
        ),
    )(c, own, other, sums)


PAIR = [(i, i ^ 1) for i in range(SHARDS)]


def along_x(k):
    return [(i, (i + 2 * k) % SHARDS) for i in range(SHARDS)]


RIGHT, LEFT = along_x(1), along_x(-1)


def along_z(k):
    return [(i, (i // Y + k) % Z * Y + i % Y) for i in range(TRAINERS)]


def along_y(k):
    return [(i, i // Y * Y + (i + k) % Y) for i in range(TRAINERS)]


def on_device(hidden_table, head_weight, targets, counts, dest, token):
    me = lax.axis_index("vocab")
    trainer = lax.axis_index("trainer")
    c = lax.rem(me, 2)
    x = me // 2
    y = lax.rem(trainer, Y)
    c1 = c.reshape(1).astype(jnp.int32)
    at_cx = jnp.stack([c, x]).astype(jnp.int32)
    at_cy = jnp.stack([c, y]).astype(jnp.int32)
    z1 = (trainer // Y).reshape(1).astype(jnp.int32)
    weight = head_weight[:, 0, :]

    half = lax.dynamic_slice(hidden_table, (0, c * HALF), (SLOTS, HALF))
    near = [half] + [lax.ppermute(half, "trainer", along_z(k)) for k in range(1, Z)]

    split = split_targets(targets[:, 0, :])

    gid = dest * SLOTS + token
    index = jnp.arange(ROWS, dtype=jnp.int32)
    live = (index % SLOTS < jnp.repeat(counts, SLOTS)).astype(F32).reshape(1, ROWS)
    gid = gid.astype(F32).reshape(1, ROWS)

    z1, split, gid, live = lax.optimization_barrier((z1, split, gid, live))
    low0, high0 = in_order(z1, near)
    low1 = lax.ppermute(low0, "trainer", along_y(1))
    high3 = lax.ppermute(high0, "trainer", along_y(-1))
    high1 = lax.ppermute(high0, "trainer", along_y(1))
    low3 = lax.ppermute(low0, "trainer", along_y(-1))
    low2 = lax.ppermute(low1, "trainer", along_y(1))
    high2 = lax.ppermute(high3, "trainer", along_y(-1))
    pieces = (low0, high0, low1, high1, low2, high2, low3, high3)
    pieces += tuple(lax.ppermute(p, "vocab", PAIR) for p in pieces)
    blocks = weight.reshape(4, 2, LOCAL, LOCAL)
    c, _ = lax.optimization_barrier((c, low1))
    give = lax.dynamic_index_in_dim(blocks, 1 - c, axis=1, keepdims=False)
    weights = pair_weights(at_cx, blocks, lax.ppermute(give, "vocab", PAIR))
    at_cy, weights = lax.optimization_barrier((at_cy, weights))
    split, _ = lax.optimization_barrier((split, (low1, high1, low3, high3)))
    probs = lax.all_to_all(split, "trainer", split_axis=0, concat_axis=0, tiled=True)

    own, other, logits, stats = logits_and_stats(at_cy, pieces, weight)
    stats = merge_stats([stats, lax.ppermute(stats, "vocab", PAIR)])
    stats = [stats] + [lax.ppermute(stats, "vocab", along_x(k)) for k in (1, 2, 3)]
    stats = merge_stats(stats, TRAINERS)
    stats, probs = lax.optimization_barrier((stats, probs.reshape(ROWS, LOCAL)))
    stats = lax.all_to_all(stats, "trainer", split_axis=0, concat_axis=0, tiled=True)

    high, sums, loss = gradients(stats, logits, probs, gid, live)

    more = lax.ppermute(loss, "vocab", PAIR)
    far = lax.ppermute(high, "vocab", PAIR)
    t0, l1, h1, l2, h2, l3, h3, loss = terms(loss, more, high, far, weights)
    low_r = lax.ppermute(l2, "vocab", RIGHT)
    high_l = lax.ppermute(h2, "vocab", LEFT)
    high_r = lax.ppermute(h1, "vocab", RIGHT)
    low_l = lax.ppermute(l3, "vocab", LEFT)
    low_r = lax.ppermute(relay(l1, low_r), "vocab", RIGHT)
    high_l = lax.ppermute(relay(h3, high_l), "vocab", LEFT)
    head = head_gradient(c1, own, other, sums)
    packed = pack(loss, t0, low_r, low_l, high_r, high_l)
    packed = lax.all_to_all(packed, "trainer", split_axis=0, concat_axis=0, tiled=True)
    table_grad, loss = finish(lax.rem(trainer, 4).reshape(1).astype(jnp.int32), packed)
    mean_loss = loss[0, 0] / jnp.sum(counts).astype(F32)
    return head.reshape(D, 1, LOCAL), table_grad, mean_loss


def solution(mesh):
    return jax.shard_map(
        on_device,
        mesh=mesh,
        in_specs=(
            P("trainer", None),
            P(None, "vocab", "trainer"),
            P("trainer", "vocab", None),
            P(),
            P(),
            P(),
        ),
        out_specs=(P(None, "vocab", "trainer"), P("trainer", "vocab"), P()),
        check_vma=False,
    )
```

```python
import functools
import math

import jax
import jax.numpy as jnp
from jax import lax
from jax.experimental import pallas as pl
from jax.experimental.pallas import tpu as pltpu
from jax.sharding import PartitionSpec as P

D = 3072
VOCAB = 98304
ROWS = 1024
TRAINERS = 32
SLOTS = 32
SHARDS = 8
LOCAL = VOCAB // (TRAINERS * SHARDS)
HALF = D // 2
BLOCK = 256
BF16 = jnp.bfloat16
F32 = jnp.float32
PARAMS = pltpu.CompilerParams(vmem_limit_bytes=24 * 1024 * 1024)
FULL = pltpu.CompilerParams(vmem_limit_bytes=60 * 1024 * 1024)
VMEM = pl.BlockSpec(memory_space=pltpu.VMEM)
SMEM = pl.BlockSpec(memory_space=pltpu.SMEM)
ANY = pl.BlockSpec(memory_space=pl.ANY)


def dot(a, b, dims=((1,), (0,))):
    return lax.dot_general(a, b, (dims, ((), ())), preferred_element_type=F32)


def split_kernel(x_ref, o_ref):
    for j in range(TRAINERS):
        o_ref[j] = x_ref[:, j * LOCAL : (j + 1) * LOCAL]


def split_targets(x):
    return pl.pallas_call(
        split_kernel,
        out_shape=jax.ShapeDtypeStruct((TRAINERS, SLOTS, LOCAL), BF16),
        in_specs=[VMEM],
        out_specs=VMEM,
        compiler_params=FULL,
    )(x)


Z = 8
Y = 4


def order_kernel(z_ref, *refs):
    pieces, outs = refs[:Z], refs[Z:]
    for k, piece in enumerate(pieces):
        at = lax.rem(z_ref[0] + Z - k, Z)
        for side, out in enumerate(outs):

            @pl.when(at // (Z // 2) == side)
            def _():
                out[lax.rem(at, Z // 2)] = piece[...]


def in_order(z, pieces):
    half = jax.ShapeDtypeStruct((Z // 2, SLOTS, HALF), BF16)
    return pl.pallas_call(
        order_kernel,
        out_shape=(half, half),
        in_specs=[SMEM] + [VMEM] * Z,
        out_specs=(VMEM, VMEM),
        compiler_params=PARAMS,
    )(z, *pieces)


def logit_kernel(at_ref, *refs):
    pieces, refs = refs[:16], refs[16:]
    far_ref, own_ref, other_ref, logits_ref, lse_ref, top_ref, *refs = refs
    tabs, w_ref, logit_buf, in_sems, out_sems = refs
    c, y = at_ref[0], at_ref[1]
    copies = [[], []]
    for side in range(2):
        rows = pl.ds(pl.multiple_of((c + side) % 2 * HALF, HALF), HALF)
        copies[side].append(
            pltpu.make_async_copy(far_ref.at[rows], w_ref.at[side], in_sems.at[16 + side])
        )
        for dy in range(Y):
            y_at = lax.rem(y + Y - dy, Y)
            for high in range(2):
                n = side * 8 + dy * 2 + high
                place = tabs.at[side, pl.ds(high * (Z // 2), Z // 2), y_at]
                copies[side].append(pltpu.make_async_copy(pieces[n], place, in_sems.at[n]))
        for copy in copies[side]:
            copy.start()
    block = 2 * BLOCK
    step = block // (Y * SLOTS)
    stores = []
    for side, out in enumerate((own_ref, other_ref)):
        for copy in copies[side]:
            copy.wait()
        stores.append(pltpu.make_async_copy(tabs.at[side], out, out_sems.at[side]))
        stores[-1].start()
        for i in range(ROWS // block):
            rows = pl.ds(i * block, block)
            part = dot(tabs[side, pl.ds(i * step, step)].reshape(block, HALF), w_ref[side])
            if side == 0:
                logit_buf[rows, :] = part
                continue
            logits = logit_buf[rows, :] + part
            logit_buf[rows, :] = logits
            stores.append(
                pltpu.make_async_copy(logit_buf.at[rows], logits_ref.at[rows], out_sems.at[2 + i])
            )
            stores[-1].start()
            top = jnp.max(logits, axis=1, keepdims=True)
            lse = top + jnp.log(jnp.sum(jnp.exp(logits - top), axis=1, keepdims=True))
            for value, out in ((lse, lse_ref), (top, top_ref)):
                flat = jnp.broadcast_to(value, (block, 128)).T
                for j in range(block // 128):
                    row = flat[0:1, j * 128 : (j + 1) * 128]
                    out[pl.ds(i * (block // 128) + j, 1), :] = row
    for store in stores:
        store.wait()


def logits_and_stats(at, pieces, weight):
    table = jax.ShapeDtypeStruct((Z, Y, SLOTS, HALF), BF16)
    own, other, logits, lse, top = pl.pallas_call(
        logit_kernel,
        out_shape=(
            table,
            table,
            jax.ShapeDtypeStruct((ROWS, LOCAL), F32),
            jax.ShapeDtypeStruct((8, 128), F32),
            jax.ShapeDtypeStruct((8, 128), F32),
        ),
        in_specs=[SMEM] + [ANY] * 17,
        out_specs=(ANY, ANY, ANY, VMEM, VMEM),
        scratch_shapes=[
            pltpu.VMEM((2, Z, Y, SLOTS, HALF), BF16),
            pltpu.VMEM((2, HALF, LOCAL), BF16),
            pltpu.VMEM((ROWS, LOCAL), F32),
            pltpu.SemaphoreType.DMA((18,)),
            pltpu.SemaphoreType.DMA((4,)),
        ],
        compiler_params=FULL,
    )(at, *pieces, weight)
    return own.reshape(ROWS, HALF), other.reshape(ROWS, HALF), logits, lse, top


def merge(x):
    top = jnp.max(x, axis=0)
    return top + jnp.log(jnp.sum(jnp.exp(x - top[None]), axis=0))


def merge_kernel(copies, *refs):
    lse = merge(jnp.stack([ref[...] for ref in refs[:-1]]))
    if copies == 1:
        refs[-1][...] = lse
    for k in range(copies if copies > 1 else 0):
        refs[-1][k] = lse


def merge_stats(parts, copies=1):
    shape = (8, 128) if copies == 1 else (copies, 8, 128)
    return pl.pallas_call(
        functools.partial(merge_kernel, copies),
        out_shape=jax.ShapeDtypeStruct(shape, F32),
        in_specs=[VMEM] * len(parts),
        out_specs=VMEM,
        compiler_params=PARAMS if copies == 1 else FULL,
    )(*parts)


def column(row):
    return jnp.broadcast_to(row, (128, row.shape[1])).T


def select_kernel(
    top_ref, far_ref, targets_ref, gid_ref, live_ref, e_ref, mass_ref, cross_ref, *scratch
):
    logits_ref, p_ref, top_col, parts_ref, out_ref, sems = scratch
    fetch = pltpu.make_async_copy(far_ref, logits_ref, sems.at[0])
    fetch.start()
    fetch_targets = pltpu.make_async_copy(targets_ref, p_ref, sems.at[1])
    fetch_targets.start()
    for j in range(8):
        top_col[pl.ds(j * 128, 128), :] = column(top_ref[j : j + 1, :])
    fetch.wait()
    for j in range(LOCAL // 128):
        p = jnp.exp(logits_ref[:, pl.ds(j * 128, 128)] - top_col[...])
        first = p.astype(BF16)
        p = p - first.astype(F32)
        second = p.astype(BF16)
        third = (p - second.astype(F32)).astype(BF16)
        parts_ref[:, pl.ds(j * 128, 128)] = first
        parts_ref[:, pl.ds(LOCAL + j * 128, 128)] = second
        parts_ref[:, pl.ds(2 * LOCAL + j * 128, 128)] = third

    def store(i):
        rows = pl.ds(pl.multiple_of(i * BLOCK, BLOCK), BLOCK)
        return pltpu.make_async_copy(out_ref.at[rows], e_ref.at[rows], sems.at[2 + i])

    @pl.loop(0, ROWS // BLOCK)
    def _(i):
        rows = pl.ds(pl.multiple_of(i * BLOCK, BLOCK), BLOCK)
        gid = column(gid_ref[:, rows])
        lane = lax.broadcasted_iota(jnp.int32, (BLOCK, 128), 1).astype(F32)
        hot = jnp.concatenate(
            [
                jnp.where(gid == lane + float(128 * k), 1.0, 0.0).astype(BF16)
                for k in range(ROWS // 128)
            ],
            axis=1,
        )
        sel = dot(hot, parts_ref[...])
        out_ref[rows, :] = sel[:, 0:LOCAL] + sel[:, LOCAL : 2 * LOCAL] + sel[:, 2 * LOCAL :]
        store(i).start()

    fetch_targets.wait()

    def total(i, cross):
        rows = pl.ds(pl.multiple_of(i * BLOCK, BLOCK), BLOCK)
        row = lax.broadcasted_iota(jnp.int32, (BLOCK, ROWS), 0) + i * BLOCK
        hot = jnp.where(gid_ref[...] == row.astype(F32), live_ref[...], 0.0).astype(BF16)
        sums = dot(hot, p_ref[...])
        mass = jnp.broadcast_to(jnp.sum(sums, axis=1, keepdims=True), (BLOCK, 128)).T[0:1]
        for j in range(BLOCK // 128):
            mass_ref[pl.ds(i * (BLOCK // 128) + j, 1), :] = mass[:, j * 128 : (j + 1) * 128]
        return cross + jnp.sum(sums * logits_ref[rows, :])

    cross_ref[0, 0] = lax.fori_loop(0, ROWS // BLOCK, total, jnp.float32(0))
    for i in range(ROWS // BLOCK):
        store(i).wait()


def select_rows(top, logits, probs, gid, live):
    return pl.pallas_call(
        select_kernel,
        out_shape=(
            jax.ShapeDtypeStruct((ROWS, LOCAL), F32),
            jax.ShapeDtypeStruct((8, 128), F32),
            jax.ShapeDtypeStruct((1, 1), F32),
        ),
        in_specs=[VMEM, ANY, ANY, VMEM, VMEM],
        out_specs=(ANY, VMEM, SMEM),
        scratch_shapes=[
            pltpu.VMEM((ROWS, LOCAL), F32),
            pltpu.VMEM((ROWS, LOCAL), BF16),
            pltpu.VMEM((ROWS, 128), F32),
            pltpu.VMEM((ROWS, 3 * LOCAL), BF16),
            pltpu.VMEM((ROWS, LOCAL), F32),
            pltpu.SemaphoreType.DMA((6,)),
        ],
        compiler_params=FULL,
        cost_estimate=pl.CostEstimate(
            flops=4 * 2 * ROWS * ROWS * LOCAL, bytes_accessed=8 * 1024 * 1024, transcendentals=0
        ),
    )(top, logits, probs, gid, live)


def grad_kernel(
    x_ref, top_ref, mass_ref, cross_ref, far_ref, targets_ref, gid_ref, live_ref, *refs
):
    high_ref, both_ref, loss_ref, e_ref, p_ref, g_ref, sums_ref, sems = refs
    fetch = pltpu.make_async_copy(far_ref, e_ref, sems.at[0])
    fetch.start()
    fetch_targets = pltpu.make_async_copy(targets_ref, p_ref, sems.at[1])
    fetch_targets.start()
    lse = merge(x_ref[...])
    loss_ref[0, 0] = jnp.sum(lse * mass_ref[...]) - cross_ref[0, 0]
    share = jnp.exp(top_ref[...] - lse)
    scale = VOCAB / math.sqrt(ROWS)
    fetch.wait()
    fetch_targets.wait()
    lane = lax.broadcasted_iota(jnp.int32, (128, 128), 1).astype(F32)
    for i in range(ROWS // 128):
        rows = pl.ds(i * 128, 128)
        gid = column(gid_ref[:, rows])
        factor = column(live_ref[:, rows]) * scale
        found = jnp.zeros((128, 128), F32)
        for k in range(ROWS // 128):
            found += jnp.where(gid == lane + float(128 * k), share[k : k + 1], 0.0)
        found = jnp.sum(found, axis=1, keepdims=True)
        for j in range(LOCAL // 128):
            cols = pl.ds(j * 128, 128)
            diff = e_ref[rows, cols] * found - p_ref[rows, cols].astype(F32)
            g_ref[rows, cols] = (factor * diff).astype(BF16)

    def stores(i):
        rows = pl.ds(pl.multiple_of(i * BLOCK, BLOCK), BLOCK)
        high = sums_ref.at[rows, pl.ds(0, LOCAL)]
        yield pltpu.make_async_copy(high, high_ref.at[rows], sems.at[2 + i])
        yield pltpu.make_async_copy(sums_ref.at[rows], both_ref.at[rows], sems.at[6 + i])

    @pl.loop(0, ROWS // BLOCK)
    def _(i):
        rows = pl.ds(pl.multiple_of(i * BLOCK, BLOCK), BLOCK)
        row = lax.broadcasted_iota(jnp.int32, (BLOCK, ROWS), 0) + i * BLOCK
        hot = jnp.where(gid_ref[...] == row.astype(F32), 1.0, 0.0).astype(BF16)
        sums = dot(hot, g_ref[...])
        high = sums.astype(BF16)
        sums_ref[rows, 0:LOCAL] = high
        sums_ref[rows, LOCAL:] = (sums - high.astype(F32)).astype(BF16)
        for store in stores(i):
            store.start()

    for i in range(ROWS // BLOCK):
        for store in stores(i):
            store.wait()


def gradients(x, top, mass, cross, e, probs, gid, live):
    return pl.pallas_call(
        grad_kernel,
        out_shape=(
            jax.ShapeDtypeStruct((ROWS, LOCAL), BF16),
            jax.ShapeDtypeStruct((ROWS, 2 * LOCAL), BF16),
            jax.ShapeDtypeStruct((1, 1), F32),
        ),
        in_specs=[VMEM, VMEM, VMEM, SMEM, ANY, ANY, VMEM, VMEM],
        out_specs=(ANY, ANY, SMEM),
        scratch_shapes=[
            pltpu.VMEM((ROWS, LOCAL), F32),
            pltpu.VMEM((ROWS, LOCAL), BF16),
            pltpu.VMEM((ROWS, LOCAL), BF16),
            pltpu.VMEM((ROWS, 2 * LOCAL), BF16),
            pltpu.SemaphoreType.DMA((10,)),
        ],
        compiler_params=FULL,
    )(x, top, mass, cross, e, probs, gid, live)


TOP = 32700.0
ROWS2 = ROWS // 2
TAIL = 16
I16 = jnp.int16


def exponent(x):
    return jnp.ceil(jnp.log(jnp.maximum(x, 1e-30) / TOP) * (256.0 / math.log(2.0)))


def power(e):
    return jnp.exp2(e * (1.0 / 256.0))


def to16(x):
    return x.astype(jnp.int32).astype(I16)


def from16(x):
    return x.astype(jnp.int32).astype(F32)


def encode(val):
    e = exponent(jnp.max(jnp.abs(val), axis=1, keepdims=True))
    return to16(jnp.round(val * power(-e))), jnp.broadcast_to(e, (128, 128)).T[0:1]


def wide(row):
    return jnp.concatenate([row] + [jnp.zeros_like(row)] * (LOCAL // 128 - 1), axis=1)


def write_message(out_ref, block_of, loss):
    tail = []
    for j in range(ROWS2 // 128):
        code, e = encode(block_of(j))
        out_ref[pl.ds(j * 128, 128), :] = code
        tail.append(e)
    tail += [loss, jnp.zeros((TAIL - len(tail) - 1, 128), F32)]
    out_ref[pl.ds(ROWS2, TAIL), :] = to16(wide(jnp.concatenate(tail, axis=0)))


def encode_loss(loss):
    e = exponent(jnp.abs(loss))
    whole = loss * power(-e)
    first = jnp.round(whole)
    rest = jnp.round((whole - first) * TOP)
    lane = lax.broadcasted_iota(jnp.int32, (1, 128), 1)
    return jnp.where(lane == 0, e, jnp.where(lane == 1, first, jnp.where(lane == 2, rest, 0.0)))


def decode_loss(code):
    return (code[:, 1:2] + code[:, 2:3] * (1.0 / TOP)) * power(code[:, 0:1])


def message_loss(ref):
    return from16(ref[pl.ds(ROWS2, TAIL), 0:128])[ROWS2 // 128 : ROWS2 // 128 + 1]


def read_message(ref, j):
    tail = from16(ref[pl.ds(ROWS2, TAIL), 0:128])
    scale = power(column(tail[j : j + 1]))
    rows = pl.ds(j * 128, 128)
    return [from16(ref[rows, k * 128 : (k + 1) * 128]) * scale for k in range(LOCAL // 128)]


MESSAGE = jax.ShapeDtypeStruct((ROWS2 + TAIL, LOCAL), I16)


def weight_kernel(at_ref, all_ref, other_ref, o_ref, own_ref, sems):
    c, x = at_ref[0], at_ref[1]
    fetches = [
        pltpu.make_async_copy(all_ref.at[lax.rem(x + k, 4), c], own_ref.at[k], sems.at[k])
        for k in range(4)
    ]
    for fetch in fetches:
        fetch.start()
    for k in range(4):
        o_ref[LOCAL : 2 * LOCAL, k * LOCAL : (k + 1) * LOCAL] = other_ref[lax.rem(x + k, 4)].T
    for k in range(4):
        fetches[k].wait()
        o_ref[0:LOCAL, k * LOCAL : (k + 1) * LOCAL] = own_ref[k].T


def pair_weights(at, blocks, other):
    return pl.pallas_call(
        weight_kernel,
        out_shape=jax.ShapeDtypeStruct((2 * LOCAL, 4 * LOCAL), BF16),
        in_specs=[SMEM, ANY, VMEM],
        out_specs=VMEM,
        scratch_shapes=[
            pltpu.VMEM((4, LOCAL, LOCAL), BF16),
            pltpu.SemaphoreType.DMA((4,)),
        ],
        compiler_params=FULL,
    )(at, blocks, other)


def term_kernel(
    loss_ref, more_ref, own_ref, other_ref, w_ref, c0, l1, h1, l2, h2, l3, h3, sum_ref, *scratch
):
    g_ref, val_ref, sems = scratch
    fetches = [
        pltpu.make_async_copy(ref, g_ref.at[:, pl.ds(k * LOCAL, LOCAL)], sems.at[k])
        for k, ref in enumerate((own_ref, other_ref))
    ]
    for fetch in fetches:
        fetch.start()
    loss = encode_loss(jnp.full((1, 128), loss_ref[0, 0] + more_ref[0, 0], F32))
    sum_ref[...] = loss
    for fetch in fetches:
        fetch.wait()
    outs = {2: (l2, h2), 1: (l1, h1), 3: (l3, h3)}
    for i in range(2):
        rows = pl.ds(i * ROWS2, ROWS2)
        val_ref[...] = dot(g_ref[rows, :], w_ref[...])
        c0[rows, :] = val_ref[:, 0:LOCAL]
        for k in (1, 2, 3):
            out, cols = outs[k][i], slice(k * LOCAL, (k + 1) * LOCAL)
            if out.dtype == F32:
                out[...] = val_ref[:, cols]
            else:
                write_message(out, lambda j: val_ref[pl.ds(j * 128, 128), cols], loss)


def terms(loss, more, own, other, weights):
    part = jax.ShapeDtypeStruct((ROWS2, LOCAL), F32)
    return pl.pallas_call(
        term_kernel,
        out_shape=(
            jax.ShapeDtypeStruct((ROWS, LOCAL), F32),
            part,
            MESSAGE,
            MESSAGE,
            MESSAGE,
            MESSAGE,
            part,
            jax.ShapeDtypeStruct((1, 128), F32),
        ),
        in_specs=[SMEM, SMEM, ANY, ANY, VMEM],
        out_specs=(VMEM,) * 8,
        scratch_shapes=[
            pltpu.VMEM((ROWS, 2 * LOCAL), BF16),
            pltpu.VMEM((ROWS2, 4 * LOCAL), F32),
            pltpu.SemaphoreType.DMA((2,)),
        ],
        compiler_params=PARAMS,
    )(loss, more, own, other, weights)


def relay_kernel(own_ref, got_ref, out_ref):
    def block(j):
        got = jnp.concatenate(read_message(got_ref, j), axis=1)
        return own_ref[pl.ds(j * 128, 128), :] + got

    write_message(out_ref, block, message_loss(got_ref))


def relay(own, got):
    return pl.pallas_call(
        relay_kernel,
        out_shape=MESSAGE,
        in_specs=[VMEM] * 2,
        out_specs=VMEM,
        compiler_params=PARAMS,
    )(own, got)


PACKED = 3 * SLOTS + TAIL


def pack_kernel(loss_ref, own_ref, low_r, low_l, high_r, high_l, o_ref):
    codes = [loss_ref[...]] + [message_loss(ref) for ref in (low_r, low_l, high_r)]
    loss = decode_loss(jnp.concatenate(codes, axis=0))
    loss = (loss[0:1] + loss[1:2]) + (loss[2:3] + loss[3:4])
    loss = encode_loss(jnp.broadcast_to(loss, (1, 128)))
    pad = jnp.zeros((TAIL - 2, 128), F32)
    for i, (right, left) in enumerate(((low_r, low_l), (high_r, high_l))):
        for j in range(ROWS2 // 128):
            a, b = read_message(right, j), read_message(left, j)
            val = jnp.concatenate([p + q for p, q in zip(a, b)], axis=1)
            at = i * (ROWS2 // 128) + j
            code, e = encode(own_ref[pl.ds(at * 128, 128), :] + val)
            tail = to16(jnp.concatenate([e, loss, pad], axis=0))
            for n in range(128 // SLOTS):
                for k in range(3):
                    o_ref[at * 4 + n, k * SLOTS : (k + 1) * SLOTS, :] = code[
                        n * SLOTS : (n + 1) * SLOTS, k * 128 : (k + 1) * 128
                    ]
                o_ref[at * 4 + n, 3 * SLOTS :, :] = tail


def pack(loss, own, low_r, low_l, high_r, high_l):
    return pl.pallas_call(
        pack_kernel,
        out_shape=jax.ShapeDtypeStruct((TRAINERS, PACKED, 128), I16),
        in_specs=[VMEM] * 6,
        out_specs=VMEM,
        compiler_params=PARAMS,
    )(loss, own, low_r, low_l, high_r, high_l)


def finish_kernel(at_ref, x_ref, grad_ref, loss_ref, e_ref):
    tail = from16(x_ref[:, 3 * SLOTS :, :])
    e = tail[:, 0, :]
    e_ref[...] = jnp.concatenate([e, jnp.zeros((128 - TRAINERS, 128), F32)], axis=0).T
    scale = power(e_ref[pl.ds(pl.multiple_of(at_ref[0] * SLOTS, SLOTS), SLOTS), :])
    total = [jnp.zeros((SLOTS, 128), F32)] * 3
    for s in range(TRAINERS):
        for k in range(3):
            total[k] += from16(x_ref[s, k * SLOTS : (k + 1) * SLOTS, :]) * scale[:, s : s + 1]
    for k in range(3):
        grad_ref[:, k * 128 : (k + 1) * 128] = total[k]
    loss_ref[0, 0] = jnp.sum(decode_loss(tail[:, 1, :]))


def finish(at, x):
    return pl.pallas_call(
        finish_kernel,
        out_shape=(
            jax.ShapeDtypeStruct((SLOTS, LOCAL), F32),
            jax.ShapeDtypeStruct((1, 1), F32),
        ),
        in_specs=[SMEM, VMEM],
        out_specs=(VMEM, SMEM),
        scratch_shapes=[pltpu.VMEM((128, 128), F32)],
        compiler_params=PARAMS,
    )(at, x)


HEAD_BLOCK = 256
HEAD_STEPS = HALF // HEAD_BLOCK


def head_kernel(c_ref, own_ref, other_ref, sums_ref, o_ref):
    i = pl.program_id(0)

    def work(t_ref):
        both = dot(t_ref[...], sums_ref[...], ((0,), (0,)))
        both = both[:, 0:LOCAL] + both[:, LOCAL:]
        for j in range(LOCAL // 128):
            o_ref[pl.ds(j, HEAD_BLOCK, stride=LOCAL // 128), :] = both[:, j * 128 : (j + 1) * 128]

    @pl.when(i < HEAD_STEPS)
    def _():
        work(own_ref)

    @pl.when(i >= HEAD_STEPS)
    def _():
        work(other_ref)


def head_gradient(c, own, other, sums):
    def place(i, c):
        mine = i < HEAD_STEPS
        side = jnp.where(mine, c[0], 1 - c[0])
        return (side * HEAD_STEPS + jnp.where(mine, i, i - HEAD_STEPS), 0)

    return pl.pallas_call(
        head_kernel,
        grid_spec=pltpu.PrefetchScalarGridSpec(
            num_scalar_prefetch=1,
            grid=(2 * HEAD_STEPS,),
            in_specs=[
                pl.BlockSpec((ROWS, HEAD_BLOCK), lambda i, c: (0, jnp.minimum(i, HEAD_STEPS - 1))),
                pl.BlockSpec((ROWS, HEAD_BLOCK), lambda i, c: (0, jnp.maximum(i - HEAD_STEPS, 0))),
                pl.BlockSpec((ROWS, 2 * LOCAL), lambda i, c: (0, 0)),
            ],
            out_specs=pl.BlockSpec((HEAD_BLOCK * LOCAL // 128, 128), place),
        ),
        out_shape=jax.ShapeDtypeStruct((D * LOCAL // 128, 128), F32),
        compiler_params=PARAMS,
        cost_estimate=pl.CostEstimate(
            flops=4 * ROWS * D * LOCAL, bytes_accessed=12 * 1024 * 1024, transcendentals=0
        ),
    )(c, own, other, sums)


PAIR = [(i, i ^ 1) for i in range(SHARDS)]


def along_x(k):
    return [(i, (i + 2 * k) % SHARDS) for i in range(SHARDS)]


RIGHT, LEFT = along_x(1), along_x(-1)


def along_z(k):
    return [(i, (i // Y + k) % Z * Y + i % Y) for i in range(TRAINERS)]


def along_y(k):
    return [(i, i // Y * Y + (i + k) % Y) for i in range(TRAINERS)]


def on_device(hidden_table, head_weight, targets, counts, dest, token):
    me = lax.axis_index("vocab")
    trainer = lax.axis_index("trainer")
    c = lax.rem(me, 2)
    x = me // 2
    y = lax.rem(trainer, Y)
    c1 = c.reshape(1).astype(jnp.int32)
    at_cx = jnp.stack([c, x]).astype(jnp.int32)
    at_cy = jnp.stack([c, y]).astype(jnp.int32)
    z1 = (trainer // Y).reshape(1).astype(jnp.int32)
    weight = head_weight[:, 0, :]

    half = lax.dynamic_slice(hidden_table, (0, c * HALF), (SLOTS, HALF))
    near = [half] + [lax.ppermute(half, "trainer", along_z(k)) for k in range(1, Z)]

    split = split_targets(targets[:, 0, :])

    gid = dest * SLOTS + token
    index = jnp.arange(ROWS, dtype=jnp.int32)
    live = (index % SLOTS < jnp.repeat(counts, SLOTS)).astype(F32).reshape(1, ROWS)
    gid = gid.astype(F32).reshape(1, ROWS)

    z1, split, gid, live = lax.optimization_barrier((z1, split, gid, live))
    low0, high0 = in_order(z1, near)
    low1 = lax.ppermute(low0, "trainer", along_y(1))
    high3 = lax.ppermute(high0, "trainer", along_y(-1))
    high1 = lax.ppermute(high0, "trainer", along_y(1))
    low3 = lax.ppermute(low0, "trainer", along_y(-1))
    low2 = lax.ppermute(low1, "trainer", along_y(1))
    high2 = lax.ppermute(high3, "trainer", along_y(-1))
    pieces = (low0, high0, low1, high1, low2, high2, low3, high3)
    pieces += tuple(lax.ppermute(p, "vocab", PAIR) for p in pieces)
    split, _ = lax.optimization_barrier((split, (low2, high2) + pieces[8:12] + pieces[14:]))
    probs = lax.all_to_all(split, "trainer", split_axis=0, concat_axis=0, tiled=True)

    own, other, logits, stats, top = logits_and_stats(at_cy, pieces, weight)
    stats = merge_stats([stats, lax.ppermute(stats, "vocab", PAIR)])
    stats = [stats] + [lax.ppermute(stats, "vocab", along_x(k)) for k in (1, 2, 3)]
    stats = merge_stats(stats, TRAINERS)
    stats, probs = lax.optimization_barrier((stats, probs.reshape(ROWS, LOCAL)))
    stats = lax.all_to_all(stats, "trainer", split_axis=0, concat_axis=0, tiled=True)

    blocks = weight.reshape(4, 2, LOCAL, LOCAL)
    c, _ = lax.optimization_barrier((c, top))
    give = lax.dynamic_index_in_dim(blocks, 1 - c, axis=1, keepdims=False)
    weights = pair_weights(at_cx, blocks, lax.ppermute(give, "vocab", PAIR))
    e, mass, cross = select_rows(top, logits, probs, gid, live)
    mass, weights = lax.optimization_barrier((mass, weights))
    high, sums, loss = gradients(stats, top, mass, cross, e, probs, gid, live)

    more = lax.ppermute(loss, "vocab", PAIR)
    far = lax.ppermute(high, "vocab", PAIR)
    t0, l1, h1, l2, h2, l3, h3, loss = terms(loss, more, high, far, weights)
    low_r = lax.ppermute(l2, "vocab", RIGHT)
    high_l = lax.ppermute(h2, "vocab", LEFT)
    high_r = lax.ppermute(h1, "vocab", RIGHT)
    low_l = lax.ppermute(l3, "vocab", LEFT)
    low_r = lax.ppermute(relay(l1, low_r), "vocab", RIGHT)
    high_l = lax.ppermute(relay(h3, high_l), "vocab", LEFT)
    head = head_gradient(c1, own, other, sums)
    packed = pack(loss, t0, low_r, low_l, high_r, high_l)
    packed = lax.all_to_all(packed, "trainer", split_axis=0, concat_axis=0, tiled=True)
    table_grad, loss = finish(lax.rem(trainer, 4).reshape(1).astype(jnp.int32), packed)
    mean_loss = loss[0, 0] / jnp.sum(counts).astype(F32)
    return head.reshape(D, 1, LOCAL), table_grad, mean_loss


def solution(mesh):
    return jax.shard_map(
        on_device,
        mesh=mesh,
        in_specs=(
            P("trainer", None),
            P(None, "vocab", "trainer"),
            P("trainer", "vocab", None),
            P(),
            P(),
            P(),
        ),
        out_specs=(P(None, "vocab", "trainer"), P("trainer", "vocab"), P()),
        check_vma=False,
    )
```

```python
import functools
import math

import jax
import jax.numpy as jnp
from jax import lax
from jax.experimental import pallas as pl
from jax.experimental.pallas import tpu as pltpu
from jax.sharding import PartitionSpec as P

D = 3072
VOCAB = 98304
ROWS = 1024
TRAINERS = 32
SLOTS = 32
SHARDS = 8
LOCAL = VOCAB // (TRAINERS * SHARDS)
HALF = D // 2
BLOCK = 256
BF16 = jnp.bfloat16
F32 = jnp.float32
PARAMS = pltpu.CompilerParams(vmem_limit_bytes=24 * 1024 * 1024)
FULL = pltpu.CompilerParams(vmem_limit_bytes=60 * 1024 * 1024)
VMEM = pl.BlockSpec(memory_space=pltpu.VMEM)
SMEM = pl.BlockSpec(memory_space=pltpu.SMEM)
ANY = pl.BlockSpec(memory_space=pl.ANY)


def dot(a, b, dims=((1,), (0,))):
    return lax.dot_general(a, b, (dims, ((), ())), preferred_element_type=F32)


Z = 8
Y = 4


def split_kernel(y_ref, x_ref, *outs):
    for k, out in enumerate(outs):
        for z in range(Z):
            trainer = z * Y + lax.rem(y_ref[0] + k, Y)
            out[z] = x_ref[:, pl.ds(pl.multiple_of(trainer * LOCAL, LOCAL), LOCAL)]


def split_targets(y, x):
    part = jax.ShapeDtypeStruct((Z, SLOTS, LOCAL), BF16)
    return pl.pallas_call(
        split_kernel,
        out_shape=(part,) * Y,
        in_specs=[SMEM, VMEM],
        out_specs=(VMEM,) * Y,
        compiler_params=PARAMS,
    )(y, x)


def turn_kernel(z_ref, *refs):
    for m, out in enumerate(refs[Y:]):
        for k in range(Y):
            out[k] = refs[k][lax.rem(z_ref[0] + m, Z)]


def turn_targets(z, parts):
    part = jax.ShapeDtypeStruct((Y, SLOTS, LOCAL), BF16)
    return pl.pallas_call(
        turn_kernel,
        out_shape=(part,) * Z,
        in_specs=[SMEM] + [VMEM] * Y,
        out_specs=(VMEM,) * Z,
        compiler_params=PARAMS,
    )(z, *parts)


def order_kernel(z_ref, *refs):
    pieces, outs = refs[:Z], refs[Z:]
    for k, piece in enumerate(pieces):
        at = lax.rem(z_ref[0] + Z - k, Z)
        for side, out in enumerate(outs):

            @pl.when(at // (Z // 2) == side)
            def _():
                out[lax.rem(at, Z // 2)] = piece[...]


def in_order(z, pieces):
    half = jax.ShapeDtypeStruct((Z // 2, SLOTS, HALF), BF16)
    return pl.pallas_call(
        order_kernel,
        out_shape=(half, half),
        in_specs=[SMEM] + [VMEM] * Z,
        out_specs=(VMEM, VMEM),
        compiler_params=PARAMS,
    )(z, *pieces)


def logit_kernel(at_ref, *refs):
    pieces, refs = refs[:16], refs[16:]
    far_ref, own_ref, other_ref, logits_ref, lse_ref, top_ref, *refs = refs
    tabs, w_ref, logit_buf, in_sems, out_sems = refs
    c, y = at_ref[0], at_ref[1]
    copies = [[], []]
    for side in range(2):
        rows = pl.ds(pl.multiple_of((c + side) % 2 * HALF, HALF), HALF)
        copies[side].append(
            pltpu.make_async_copy(far_ref.at[rows], w_ref.at[side], in_sems.at[16 + side])
        )
        for dy in range(Y):
            y_at = lax.rem(y + Y - dy, Y)
            for high in range(2):
                n = side * 8 + dy * 2 + high
                place = tabs.at[side, pl.ds(high * (Z // 2), Z // 2), y_at]
                copies[side].append(pltpu.make_async_copy(pieces[n], place, in_sems.at[n]))
        for copy in copies[side]:
            copy.start()
    block = 2 * BLOCK
    step = block // (Y * SLOTS)
    stores = []
    for side, out in enumerate((own_ref, other_ref)):
        for copy in copies[side]:
            copy.wait()
        stores.append(pltpu.make_async_copy(tabs.at[side], out, out_sems.at[side]))
        stores[-1].start()
        for i in range(ROWS // block):
            rows = pl.ds(i * block, block)
            part = dot(tabs[side, pl.ds(i * step, step)].reshape(block, HALF), w_ref[side])
            if side == 0:
                logit_buf[rows, :] = part
                continue
            logits = logit_buf[rows, :] + part
            logit_buf[rows, :] = logits
            stores.append(
                pltpu.make_async_copy(logit_buf.at[rows], logits_ref.at[rows], out_sems.at[2 + i])
            )
            stores[-1].start()
            top = jnp.max(logits, axis=1, keepdims=True)
            lse = top + jnp.log(jnp.sum(jnp.exp(logits - top), axis=1, keepdims=True))
            for value, out in ((lse, lse_ref), (top, top_ref)):
                flat = jnp.broadcast_to(value, (block, 128)).T
                for j in range(block // 128):
                    row = flat[0:1, j * 128 : (j + 1) * 128]
                    out[pl.ds(i * (block // 128) + j, 1), :] = row
    for store in stores:
        store.wait()


def logits_and_stats(at, pieces, weight):
    table = jax.ShapeDtypeStruct((Z, Y, SLOTS, HALF), BF16)
    own, other, logits, lse, top = pl.pallas_call(
        logit_kernel,
        out_shape=(
            table,
            table,
            jax.ShapeDtypeStruct((ROWS, LOCAL), F32),
            jax.ShapeDtypeStruct((8, 128), F32),
            jax.ShapeDtypeStruct((8, 128), F32),
        ),
        in_specs=[SMEM] + [ANY] * 17,
        out_specs=(ANY, ANY, ANY, VMEM, VMEM),
        scratch_shapes=[
            pltpu.VMEM((2, Z, Y, SLOTS, HALF), BF16),
            pltpu.VMEM((2, HALF, LOCAL), BF16),
            pltpu.VMEM((ROWS, LOCAL), F32),
            pltpu.SemaphoreType.DMA((18,)),
            pltpu.SemaphoreType.DMA((4,)),
        ],
        compiler_params=FULL,
    )(at, *pieces, weight)
    return own.reshape(ROWS, HALF), other.reshape(ROWS, HALF), logits, lse, top


def merge(x):
    top = jnp.max(x, axis=0)
    return top + jnp.log(jnp.sum(jnp.exp(x - top[None]), axis=0))


def merge_kernel(copies, *refs):
    lse = merge(jnp.stack([ref[...] for ref in refs[:-1]]))
    if copies == 1:
        refs[-1][...] = lse
    for k in range(copies if copies > 1 else 0):
        refs[-1][k] = lse


def merge_stats(parts, copies=1):
    shape = (8, 128) if copies == 1 else (copies, 8, 128)
    return pl.pallas_call(
        functools.partial(merge_kernel, copies),
        out_shape=jax.ShapeDtypeStruct(shape, F32),
        in_specs=[VMEM] * len(parts),
        out_specs=VMEM,
        compiler_params=PARAMS if copies == 1 else FULL,
    )(*parts)


def column(row):
    return jnp.broadcast_to(row, (128, row.shape[1])).T


def select_kernel(at_ref, top_ref, far_ref, gid_ref, live_ref, *refs):
    targets, refs = refs[:Z], refs[Z:]
    e_ref, probs_ref, mass_ref, cross_ref, *refs = refs
    logits_ref, p_ref, top_col, parts_ref, out_ref, sems, target_sems = refs
    fetch = pltpu.make_async_copy(far_ref, logits_ref, sems.at[0])
    fetch.start()
    y, z = at_ref[0], at_ref[1]
    fetches = []
    for m, part in enumerate(targets):
        for k in range(Y):
            source = lax.rem(z + Z - m, Z) * Y + lax.rem(y + Y - k, Y)
            rows = pl.ds(pl.multiple_of(source * SLOTS, SLOTS), SLOTS)
            sem = target_sems.at[m * Y + k]
            fetches.append(pltpu.make_async_copy(part.at[k], p_ref.at[rows], sem))
            fetches[-1].start()
    for j in range(8):
        top_col[pl.ds(j * 128, 128), :] = column(top_ref[j : j + 1, :])
    fetch.wait()
    for j in range(LOCAL // 128):
        p = jnp.exp(logits_ref[:, pl.ds(j * 128, 128)] - top_col[...])
        first = p.astype(BF16)
        p = p - first.astype(F32)
        second = p.astype(BF16)
        third = (p - second.astype(F32)).astype(BF16)
        parts_ref[:, pl.ds(j * 128, 128)] = first
        parts_ref[:, pl.ds(LOCAL + j * 128, 128)] = second
        parts_ref[:, pl.ds(2 * LOCAL + j * 128, 128)] = third

    def store(i):
        rows = pl.ds(pl.multiple_of(i * BLOCK, BLOCK), BLOCK)
        return pltpu.make_async_copy(out_ref.at[rows], e_ref.at[rows], sems.at[2 + i])

    @pl.loop(0, ROWS // BLOCK)
    def _(i):
        rows = pl.ds(pl.multiple_of(i * BLOCK, BLOCK), BLOCK)
        gid = column(gid_ref[:, rows])
        lane = lax.broadcasted_iota(jnp.int32, (BLOCK, 128), 1).astype(F32)
        hot = jnp.concatenate(
            [
                jnp.where(gid == lane + float(128 * k), 1.0, 0.0).astype(BF16)
                for k in range(ROWS // 128)
            ],
            axis=1,
        )
        sel = dot(hot, parts_ref[...])
        out_ref[rows, :] = sel[:, 0:LOCAL] + sel[:, LOCAL : 2 * LOCAL] + sel[:, 2 * LOCAL :]
        store(i).start()

    for copy in fetches:
        copy.wait()
    store_targets = pltpu.make_async_copy(p_ref, probs_ref, sems.at[1])
    store_targets.start()

    def total(i, cross):
        rows = pl.ds(pl.multiple_of(i * BLOCK, BLOCK), BLOCK)
        row = lax.broadcasted_iota(jnp.int32, (BLOCK, ROWS), 0) + i * BLOCK
        hot = jnp.where(gid_ref[...] == row.astype(F32), live_ref[...], 0.0).astype(BF16)
        sums = dot(hot, p_ref[...])
        mass = jnp.broadcast_to(jnp.sum(sums, axis=1, keepdims=True), (BLOCK, 128)).T[0:1]
        for j in range(BLOCK // 128):
            mass_ref[pl.ds(i * (BLOCK // 128) + j, 1), :] = mass[:, j * 128 : (j + 1) * 128]
        return cross + jnp.sum(sums * logits_ref[rows, :])

    cross_ref[0, 0] = lax.fori_loop(0, ROWS // BLOCK, total, jnp.float32(0))
    for i in range(ROWS // BLOCK):
        store(i).wait()
    store_targets.wait()


def select_rows(at, top, logits, targets, gid, live):
    return pl.pallas_call(
        select_kernel,
        out_shape=(
            jax.ShapeDtypeStruct((ROWS, LOCAL), F32),
            jax.ShapeDtypeStruct((ROWS, LOCAL), BF16),
            jax.ShapeDtypeStruct((8, 128), F32),
            jax.ShapeDtypeStruct((1, 1), F32),
        ),
        in_specs=[SMEM, VMEM, ANY, VMEM, VMEM] + [ANY] * Z,
        out_specs=(ANY, ANY, VMEM, SMEM),
        scratch_shapes=[
            pltpu.VMEM((ROWS, LOCAL), F32),
            pltpu.VMEM((ROWS, LOCAL), BF16),
            pltpu.VMEM((ROWS, 128), F32),
            pltpu.VMEM((ROWS, 3 * LOCAL), BF16),
            pltpu.VMEM((ROWS, LOCAL), F32),
            pltpu.SemaphoreType.DMA((6,)),
            pltpu.SemaphoreType.DMA((TRAINERS,)),
        ],
        compiler_params=FULL,
        cost_estimate=pl.CostEstimate(
            flops=4 * 2 * ROWS * ROWS * LOCAL, bytes_accessed=8 * 1024 * 1024, transcendentals=0
        ),
    )(at, top, logits, gid, live, *targets)


def grad_kernel(
    x_ref, top_ref, mass_ref, cross_ref, far_ref, targets_ref, gid_ref, live_ref, *refs
):
    high_ref, both_ref, loss_ref, e_ref, p_ref, g_ref, sums_ref, sems = refs
    fetch = pltpu.make_async_copy(far_ref, e_ref, sems.at[0])
    fetch.start()
    fetch_targets = pltpu.make_async_copy(targets_ref, p_ref, sems.at[1])
    fetch_targets.start()
    lse = merge(x_ref[...])
    loss_ref[0, 0] = jnp.sum(lse * mass_ref[...]) - cross_ref[0, 0]
    share = jnp.exp(top_ref[...] - lse)
    scale = VOCAB / math.sqrt(ROWS)
    fetch.wait()
    fetch_targets.wait()
    lane = lax.broadcasted_iota(jnp.int32, (128, 128), 1).astype(F32)
    for i in range(ROWS // 128):
        rows = pl.ds(i * 128, 128)
        gid = column(gid_ref[:, rows])
        factor = column(live_ref[:, rows]) * scale
        found = jnp.zeros((128, 128), F32)
        for k in range(ROWS // 128):
            found += jnp.where(gid == lane + float(128 * k), share[k : k + 1], 0.0)
        found = jnp.sum(found, axis=1, keepdims=True)
        for j in range(LOCAL // 128):
            cols = pl.ds(j * 128, 128)
            diff = e_ref[rows, cols] * found - p_ref[rows, cols].astype(F32)
            g_ref[rows, cols] = (factor * diff).astype(BF16)

    def stores(i):
        rows = pl.ds(pl.multiple_of(i * BLOCK, BLOCK), BLOCK)
        high = sums_ref.at[rows, pl.ds(0, LOCAL)]
        yield pltpu.make_async_copy(high, high_ref.at[rows], sems.at[2 + i])
        yield pltpu.make_async_copy(sums_ref.at[rows], both_ref.at[rows], sems.at[6 + i])

    @pl.loop(0, ROWS // BLOCK)
    def _(i):
        rows = pl.ds(pl.multiple_of(i * BLOCK, BLOCK), BLOCK)
        row = lax.broadcasted_iota(jnp.int32, (BLOCK, ROWS), 0) + i * BLOCK
        hot = jnp.where(gid_ref[...] == row.astype(F32), 1.0, 0.0).astype(BF16)
        sums = dot(hot, g_ref[...])
        high = sums.astype(BF16)
        sums_ref[rows, 0:LOCAL] = high
        sums_ref[rows, LOCAL:] = (sums - high.astype(F32)).astype(BF16)
        for store in stores(i):
            store.start()

    for i in range(ROWS // BLOCK):
        for store in stores(i):
            store.wait()


def gradients(x, top, mass, cross, e, probs, gid, live):
    return pl.pallas_call(
        grad_kernel,
        out_shape=(
            jax.ShapeDtypeStruct((ROWS, LOCAL), BF16),
            jax.ShapeDtypeStruct((ROWS, 2 * LOCAL), BF16),
            jax.ShapeDtypeStruct((1, 1), F32),
        ),
        in_specs=[VMEM, VMEM, VMEM, SMEM, ANY, ANY, VMEM, VMEM],
        out_specs=(ANY, ANY, SMEM),
        scratch_shapes=[
            pltpu.VMEM((ROWS, LOCAL), F32),
            pltpu.VMEM((ROWS, LOCAL), BF16),
            pltpu.VMEM((ROWS, LOCAL), BF16),
            pltpu.VMEM((ROWS, 2 * LOCAL), BF16),
            pltpu.SemaphoreType.DMA((10,)),
        ],
        compiler_params=FULL,
    )(x, top, mass, cross, e, probs, gid, live)


TOP = 32700.0
ROWS2 = ROWS // 2
TAIL = 16
I16 = jnp.int16


def exponent(x):
    return jnp.ceil(jnp.log(jnp.maximum(x, 1e-30) / TOP) * (256.0 / math.log(2.0)))


def power(e):
    return jnp.exp2(e * (1.0 / 256.0))


def to16(x):
    return x.astype(jnp.int32).astype(I16)


def from16(x):
    return x.astype(jnp.int32).astype(F32)


def encode(val):
    e = exponent(jnp.max(jnp.abs(val), axis=1, keepdims=True))
    return to16(jnp.round(val * power(-e))), jnp.broadcast_to(e, (128, 128)).T[0:1]


def wide(row):
    return jnp.concatenate([row] + [jnp.zeros_like(row)] * (LOCAL // 128 - 1), axis=1)


def write_message(out_ref, block_of, loss):
    tail = []
    for j in range(ROWS2 // 128):
        code, e = encode(block_of(j))
        out_ref[pl.ds(j * 128, 128), :] = code
        tail.append(e)
    tail += [loss, jnp.zeros((TAIL - len(tail) - 1, 128), F32)]
    out_ref[pl.ds(ROWS2, TAIL), :] = to16(wide(jnp.concatenate(tail, axis=0)))


def encode_loss(loss):
    e = exponent(jnp.abs(loss))
    whole = loss * power(-e)
    first = jnp.round(whole)
    rest = jnp.round((whole - first) * TOP)
    lane = lax.broadcasted_iota(jnp.int32, (1, 128), 1)
    return jnp.where(lane == 0, e, jnp.where(lane == 1, first, jnp.where(lane == 2, rest, 0.0)))


def decode_loss(code):
    return (code[:, 1:2] + code[:, 2:3] * (1.0 / TOP)) * power(code[:, 0:1])


def message_loss(ref):
    return from16(ref[pl.ds(ROWS2, TAIL), 0:128])[ROWS2 // 128 : ROWS2 // 128 + 1]


def read_message(ref, j):
    tail = from16(ref[pl.ds(ROWS2, TAIL), 0:128])
    scale = power(column(tail[j : j + 1]))
    rows = pl.ds(j * 128, 128)
    return [from16(ref[rows, k * 128 : (k + 1) * 128]) * scale for k in range(LOCAL // 128)]


MESSAGE = jax.ShapeDtypeStruct((ROWS2 + TAIL, LOCAL), I16)


def weight_kernel(at_ref, all_ref, keep_ref, give_ref, block_ref, sems):
    c, x = at_ref[0], at_ref[1]
    fetches = []
    for n in range(8):
        source = all_ref.at[lax.rem(x + n % 4, 4), (c + n // 4) % 2]
        fetches.append(pltpu.make_async_copy(source, block_ref.at[n], sems.at[n]))
        fetches[-1].start()
    for n in range(8):
        fetches[n].wait()
        out = (keep_ref, give_ref)[n // 4]
        out[:, n % 4 * LOCAL : (n % 4 + 1) * LOCAL] = block_ref[n].T


def turn_weights(at, blocks):
    half = jax.ShapeDtypeStruct((LOCAL, 4 * LOCAL), BF16)
    return pl.pallas_call(
        weight_kernel,
        out_shape=(half, half),
        in_specs=[SMEM, ANY],
        out_specs=(VMEM, VMEM),
        scratch_shapes=[
            pltpu.VMEM((8, LOCAL, LOCAL), BF16),
            pltpu.SemaphoreType.DMA((8,)),
        ],
        compiler_params=FULL,
    )(at, blocks)


def term_kernel(
    loss_ref, more_ref, own_ref, other_ref, w_own, w_other, c0, l1, h1, l2, h2, l3, h3, sum_ref, *refs
):
    g_ref, w_ref, val_ref, sems = refs
    fetches = [
        pltpu.make_async_copy(ref, g_ref.at[:, pl.ds(k * LOCAL, LOCAL)], sems.at[k])
        for k, ref in enumerate((own_ref, other_ref))
    ] + [
        pltpu.make_async_copy(ref, w_ref.at[pl.ds(k * LOCAL, LOCAL)], sems.at[2 + k])
        for k, ref in enumerate((w_own, w_other))
    ]
    for fetch in fetches:
        fetch.start()
    loss = encode_loss(jnp.full((1, 128), loss_ref[0, 0] + more_ref[0, 0], F32))
    sum_ref[...] = loss
    for fetch in fetches:
        fetch.wait()
    outs = {2: (l2, h2), 1: (l1, h1), 3: (l3, h3)}
    for i in range(2):
        rows = pl.ds(i * ROWS2, ROWS2)
        val_ref[...] = dot(g_ref[rows, :], w_ref[...])
        c0[rows, :] = val_ref[:, 0:LOCAL]
        for k in (1, 2, 3):
            out, cols = outs[k][i], slice(k * LOCAL, (k + 1) * LOCAL)
            if out.dtype == F32:
                out[...] = val_ref[:, cols]
            else:
                write_message(out, lambda j: val_ref[pl.ds(j * 128, 128), cols], loss)


def terms(loss, more, own, other, w_own, w_other):
    part = jax.ShapeDtypeStruct((ROWS2, LOCAL), F32)
    return pl.pallas_call(
        term_kernel,
        out_shape=(
            jax.ShapeDtypeStruct((ROWS, LOCAL), F32),
            part,
            MESSAGE,
            MESSAGE,
            MESSAGE,
            MESSAGE,
            part,
            jax.ShapeDtypeStruct((1, 128), F32),
        ),
        in_specs=[SMEM, SMEM] + [ANY] * 4,
        out_specs=(VMEM,) * 8,
        scratch_shapes=[
            pltpu.VMEM((ROWS, 2 * LOCAL), BF16),
            pltpu.VMEM((2 * LOCAL, 4 * LOCAL), BF16),
            pltpu.VMEM((ROWS2, 4 * LOCAL), F32),
            pltpu.SemaphoreType.DMA((4,)),
        ],
        compiler_params=PARAMS,
    )(loss, more, own, other, w_own, w_other)


def relay_kernel(own_ref, got_ref, out_ref):
    def block(j):
        got = jnp.concatenate(read_message(got_ref, j), axis=1)
        return own_ref[pl.ds(j * 128, 128), :] + got

    write_message(out_ref, block, message_loss(got_ref))


def relay(own, got):
    return pl.pallas_call(
        relay_kernel,
        out_shape=MESSAGE,
        in_specs=[VMEM] * 2,
        out_specs=VMEM,
        compiler_params=PARAMS,
    )(own, got)


PACKED = 3 * SLOTS + TAIL


def pack_kernel(loss_ref, own_ref, low_r, low_l, high_r, high_l, o_ref):
    codes = [loss_ref[...]] + [message_loss(ref) for ref in (low_r, low_l, high_r)]
    loss = decode_loss(jnp.concatenate(codes, axis=0))
    loss = (loss[0:1] + loss[1:2]) + (loss[2:3] + loss[3:4])
    loss = encode_loss(jnp.broadcast_to(loss, (1, 128)))
    pad = jnp.zeros((TAIL - 2, 128), F32)
    for i, (right, left) in enumerate(((low_r, low_l), (high_r, high_l))):
        for j in range(ROWS2 // 128):
            a, b = read_message(right, j), read_message(left, j)
            val = jnp.concatenate([p + q for p, q in zip(a, b)], axis=1)
            at = i * (ROWS2 // 128) + j
            code, e = encode(own_ref[pl.ds(at * 128, 128), :] + val)
            tail = to16(jnp.concatenate([e, loss, pad], axis=0))
            for n in range(128 // SLOTS):
                for k in range(3):
                    o_ref[at * 4 + n, k * SLOTS : (k + 1) * SLOTS, :] = code[
                        n * SLOTS : (n + 1) * SLOTS, k * 128 : (k + 1) * 128
                    ]
                o_ref[at * 4 + n, 3 * SLOTS :, :] = tail


def pack(loss, own, low_r, low_l, high_r, high_l):
    return pl.pallas_call(
        pack_kernel,
        out_shape=jax.ShapeDtypeStruct((TRAINERS, PACKED, 128), I16),
        in_specs=[VMEM] * 6,
        out_specs=VMEM,
        compiler_params=PARAMS,
    )(loss, own, low_r, low_l, high_r, high_l)


def finish_kernel(at_ref, x_ref, grad_ref, loss_ref, e_ref):
    tail = from16(x_ref[:, 3 * SLOTS :, :])
    e = tail[:, 0, :]
    e_ref[...] = jnp.concatenate([e, jnp.zeros((128 - TRAINERS, 128), F32)], axis=0).T
    scale = power(e_ref[pl.ds(pl.multiple_of(at_ref[0] * SLOTS, SLOTS), SLOTS), :])
    total = [jnp.zeros((SLOTS, 128), F32)] * 3
    for s in range(TRAINERS):
        for k in range(3):
            total[k] += from16(x_ref[s, k * SLOTS : (k + 1) * SLOTS, :]) * scale[:, s : s + 1]
    for k in range(3):
        grad_ref[:, k * 128 : (k + 1) * 128] = total[k]
    loss_ref[0, 0] = jnp.sum(decode_loss(tail[:, 1, :]))


def finish(at, x):
    return pl.pallas_call(
        finish_kernel,
        out_shape=(
            jax.ShapeDtypeStruct((SLOTS, LOCAL), F32),
            jax.ShapeDtypeStruct((1, 1), F32),
        ),
        in_specs=[SMEM, VMEM],
        out_specs=(VMEM, SMEM),
        scratch_shapes=[pltpu.VMEM((128, 128), F32)],
        compiler_params=PARAMS,
    )(at, x)


HEAD_BLOCK = 256
HEAD_STEPS = HALF // HEAD_BLOCK


def head_kernel(c_ref, own_ref, other_ref, sums_ref, o_ref):
    i = pl.program_id(0)

    def work(t_ref):
        both = dot(t_ref[...], sums_ref[...], ((0,), (0,)))
        both = both[:, 0:LOCAL] + both[:, LOCAL:]
        for j in range(LOCAL // 128):
            o_ref[pl.ds(j, HEAD_BLOCK, stride=LOCAL // 128), :] = both[:, j * 128 : (j + 1) * 128]

    @pl.when(i < HEAD_STEPS)
    def _():
        work(own_ref)

    @pl.when(i >= HEAD_STEPS)
    def _():
        work(other_ref)


def head_gradient(c, own, other, sums):
    def place(i, c):
        mine = i < HEAD_STEPS
        side = jnp.where(mine, c[0], 1 - c[0])
        return (side * HEAD_STEPS + jnp.where(mine, i, i - HEAD_STEPS), 0)

    return pl.pallas_call(
        head_kernel,
        grid_spec=pltpu.PrefetchScalarGridSpec(
            num_scalar_prefetch=1,
            grid=(2 * HEAD_STEPS,),
            in_specs=[
                pl.BlockSpec((ROWS, HEAD_BLOCK), lambda i, c: (0, jnp.minimum(i, HEAD_STEPS - 1))),
                pl.BlockSpec((ROWS, HEAD_BLOCK), lambda i, c: (0, jnp.maximum(i - HEAD_STEPS, 0))),
                pl.BlockSpec((ROWS, 2 * LOCAL), lambda i, c: (0, 0)),
            ],
            out_specs=pl.BlockSpec((HEAD_BLOCK * LOCAL // 128, 128), place),
        ),
        out_shape=jax.ShapeDtypeStruct((D * LOCAL // 128, 128), F32),
        compiler_params=PARAMS,
        cost_estimate=pl.CostEstimate(
            flops=4 * ROWS * D * LOCAL, bytes_accessed=12 * 1024 * 1024, transcendentals=0
        ),
    )(c, own, other, sums)


PAIR = [(i, i ^ 1) for i in range(SHARDS)]


def along_x(k):
    return [(i, (i + 2 * k) % SHARDS) for i in range(SHARDS)]


RIGHT, LEFT = along_x(1), along_x(-1)


def along_z(k):
    return [(i, (i // Y + k) % Z * Y + i % Y) for i in range(TRAINERS)]


def along_y(k):
    return [(i, i // Y * Y + (i + k) % Y) for i in range(TRAINERS)]


def on_device(hidden_table, head_weight, targets, counts, dest, token):
    me = lax.axis_index("vocab")
    trainer = lax.axis_index("trainer")
    c = lax.rem(me, 2)
    x = me // 2
    y = lax.rem(trainer, Y)
    c1 = c.reshape(1).astype(jnp.int32)
    at_cx = jnp.stack([c, x]).astype(jnp.int32)
    at_cy = jnp.stack([c, y]).astype(jnp.int32)
    z1 = (trainer // Y).reshape(1).astype(jnp.int32)
    y1 = y.reshape(1).astype(jnp.int32)
    at_yz = jnp.stack([y, trainer // Y]).astype(jnp.int32)
    weight = head_weight[:, 0, :]

    half = lax.dynamic_slice(hidden_table, (0, c * HALF), (SLOTS, HALF))
    near = [half] + [lax.ppermute(half, "trainer", along_z(k)) for k in range(1, Z)]

    y1, _ = lax.optimization_barrier((y1, (near[1], near[2])))
    split = split_targets(y1, targets[:, 0, :])
    split = [split[0]] + [lax.ppermute(split[k], "trainer", along_y(k)) for k in range(1, Y)]

    gid = dest * SLOTS + token
    index = jnp.arange(ROWS, dtype=jnp.int32)
    live = (index % SLOTS < jnp.repeat(counts, SLOTS)).astype(F32).reshape(1, ROWS)
    gid = gid.astype(F32).reshape(1, ROWS)

    w_own, w_give = turn_weights(at_cx, weight.reshape(4, 2, LOCAL, LOCAL))
    z1, gid, live, split, w_own, w_give = lax.optimization_barrier(
        (z1, gid, live, split, w_own, w_give)
    )
    low0, high0 = in_order(z1, near)
    low1 = lax.ppermute(low0, "trainer", along_y(1))
    high3 = lax.ppermute(high0, "trainer", along_y(-1))
    high1 = lax.ppermute(high0, "trainer", along_y(1))
    low3 = lax.ppermute(low0, "trainer", along_y(-1))
    low2 = lax.ppermute(low1, "trainer", along_y(1))
    high2 = lax.ppermute(high3, "trainer", along_y(-1))

    z1, _ = lax.optimization_barrier((z1, (low1, high1, low3, high3)))
    turned = turn_targets(z1, split)
    turned = [turned[0]] + [lax.ppermute(turned[k], "trainer", along_z(k)) for k in range(1, Z)]
    at_cy, _ = lax.optimization_barrier((at_cy, turned[:4]))
    pieces = (low0, high0, low1, high1, low2, high2, low3, high3)
    pieces += tuple(lax.ppermute(p, "vocab", PAIR) for p in pieces)

    own, other, logits, stats, top = logits_and_stats(at_cy, pieces, weight)
    stats = merge_stats([stats, lax.ppermute(stats, "vocab", PAIR)])
    stats = [stats] + [lax.ppermute(stats, "vocab", along_x(k)) for k in (1, 2, 3)]
    stats = merge_stats(stats, TRAINERS)
    stats = lax.all_to_all(stats, "trainer", split_axis=0, concat_axis=0, tiled=True)
    w_give, _ = lax.optimization_barrier((w_give, top))
    w_other = lax.ppermute(w_give, "vocab", PAIR)

    e, probs, mass, cross = select_rows(at_yz, top, logits, turned, gid, live)
    high, sums, loss = gradients(stats, top, mass, cross, e, probs, gid, live)

    more = lax.ppermute(loss, "vocab", PAIR)
    far = lax.ppermute(high, "vocab", PAIR)
    t0, l1, h1, l2, h2, l3, h3, loss = terms(loss, more, high, far, w_own, w_other)
    low_r = lax.ppermute(l2, "vocab", RIGHT)
    high_l = lax.ppermute(h2, "vocab", LEFT)
    high_r = lax.ppermute(h1, "vocab", RIGHT)
    low_l = lax.ppermute(l3, "vocab", LEFT)
    low_r = lax.ppermute(relay(l1, low_r), "vocab", RIGHT)
    high_l = lax.ppermute(relay(h3, high_l), "vocab", LEFT)
    head = head_gradient(c1, own, other, sums)
    packed = pack(loss, t0, low_r, low_l, high_r, high_l)
    packed = lax.all_to_all(packed, "trainer", split_axis=0, concat_axis=0, tiled=True)
    table_grad, loss = finish(lax.rem(trainer, 4).reshape(1).astype(jnp.int32), packed)
    mean_loss = loss[0, 0] / jnp.sum(counts).astype(F32)
    return head.reshape(D, 1, LOCAL), table_grad, mean_loss


def solution(mesh):
    return jax.shard_map(
        on_device,
        mesh=mesh,
        in_specs=(
            P("trainer", None),
            P(None, "vocab", "trainer"),
            P("trainer", "vocab", None),
            P(),
            P(),
            P(),
        ),
        out_specs=(P(None, "vocab", "trainer"), P("trainer", "vocab"), P()),
        check_vma=False,
    )
```

```python
import functools
import math

import jax
import jax.numpy as jnp
from jax import lax
from jax.experimental import pallas as pl
from jax.experimental.pallas import tpu as pltpu
from jax.sharding import PartitionSpec as P

D = 3072
VOCAB = 98304
ROWS = 1024
TRAINERS = 32
SLOTS = 32
SHARDS = 8
LOCAL = VOCAB // (TRAINERS * SHARDS)
HALF = D // 2
BLOCK = 256
BF16 = jnp.bfloat16
F32 = jnp.float32
PARAMS = pltpu.CompilerParams(vmem_limit_bytes=24 * 1024 * 1024)
FULL = pltpu.CompilerParams(vmem_limit_bytes=60 * 1024 * 1024)
VMEM = pl.BlockSpec(memory_space=pltpu.VMEM)
SMEM = pl.BlockSpec(memory_space=pltpu.SMEM)
ANY = pl.BlockSpec(memory_space=pl.ANY)


def dot(a, b, dims=((1,), (0,))):
    return lax.dot_general(a, b, (dims, ((), ())), preferred_element_type=F32)


def split_kernel(x_ref, o_ref):
    for j in range(TRAINERS):
        o_ref[j] = x_ref[:, j * LOCAL : (j + 1) * LOCAL]


def split_targets(x):
    return pl.pallas_call(
        split_kernel,
        out_shape=jax.ShapeDtypeStruct((TRAINERS, SLOTS, LOCAL), BF16),
        in_specs=[VMEM],
        out_specs=VMEM,
        compiler_params=FULL,
    )(x)


Z = 8
Y = 4


def order_kernel(z_ref, *refs):
    pieces, outs = refs[:Z], refs[Z:]
    for k, piece in enumerate(pieces):
        at = lax.rem(z_ref[0] + Z - k, Z)
        for side, out in enumerate(outs):

            @pl.when(at // (Z // 2) == side)
            def _():
                out[lax.rem(at, Z // 2)] = piece[...]


def in_order(z, pieces):
    half = jax.ShapeDtypeStruct((Z // 2, SLOTS, HALF), BF16)
    return pl.pallas_call(
        order_kernel,
        out_shape=(half, half),
        in_specs=[SMEM] + [VMEM] * Z,
        out_specs=(VMEM, VMEM),
        compiler_params=PARAMS,
    )(z, *pieces)


def logit_kernel(at_ref, *refs):
    pieces, refs = refs[:16], refs[16:]
    far_ref, own_ref, other_ref, logits_ref, lse_ref, top_ref, *refs = refs
    tabs, w_ref, logit_buf, in_sems, out_sems = refs
    c, y = at_ref[0], at_ref[1]
    copies = [[], []]
    for side in range(2):
        rows = pl.ds(pl.multiple_of((c + side) % 2 * HALF, HALF), HALF)
        copies[side].append(
            pltpu.make_async_copy(far_ref.at[rows], w_ref.at[side], in_sems.at[16 + side])
        )
        for dy in range(Y):
            y_at = lax.rem(y + Y - dy, Y)
            for high in range(2):
                n = side * 8 + dy * 2 + high
                place = tabs.at[side, pl.ds(high * (Z // 2), Z // 2), y_at]
                copies[side].append(pltpu.make_async_copy(pieces[n], place, in_sems.at[n]))
        for copy in copies[side]:
            copy.start()
    step = BLOCK // (Y * SLOTS)

    def part(side, i):
        block = tabs[side, pl.ds(i * step, step)].reshape(BLOCK, HALF)
        return dot(block, w_ref[side])

    def store(i):
        rows = pl.ds(pl.multiple_of(i * BLOCK, BLOCK), BLOCK)
        return pltpu.make_async_copy(logit_buf.at[rows], logits_ref.at[rows], out_sems.at[2 + i])

    stores = []
    for side, out in enumerate((own_ref, other_ref)):
        for copy in copies[side]:
            copy.wait()
        stores.append(pltpu.make_async_copy(tabs.at[side], out, out_sems.at[side]))
        stores[-1].start()

        @pl.loop(0, ROWS // BLOCK)
        def _(i):
            rows = pl.ds(pl.multiple_of(i * BLOCK, BLOCK), BLOCK)
            if side == 0:
                logit_buf[rows, :] = part(side, i)
                return
            logits = logit_buf[rows, :] + part(side, i)
            logit_buf[rows, :] = logits
            store(i).start()
            top = jnp.max(logits, axis=1, keepdims=True)
            lse = top + jnp.log(jnp.sum(jnp.exp(logits - top), axis=1, keepdims=True))
            for value, out in ((lse, lse_ref), (top, top_ref)):
                flat = jnp.broadcast_to(value, (BLOCK, 128)).T
                for j in range(BLOCK // 128):
                    row = flat[0:1, j * 128 : (j + 1) * 128]
                    out[pl.ds(i * (BLOCK // 128) + j, 1), :] = row

    for copy in stores + [store(i) for i in range(ROWS // BLOCK)]:
        copy.wait()


def logits_and_stats(at, pieces, weight):
    table = jax.ShapeDtypeStruct((Z, Y, SLOTS, HALF), BF16)
    own, other, logits, lse, top = pl.pallas_call(
        logit_kernel,
        out_shape=(
            table,
            table,
            jax.ShapeDtypeStruct((ROWS, LOCAL), F32),
            jax.ShapeDtypeStruct((8, 128), F32),
            jax.ShapeDtypeStruct((8, 128), F32),
        ),
        in_specs=[SMEM] + [ANY] * 17,
        out_specs=(ANY, ANY, ANY, VMEM, VMEM),
        scratch_shapes=[
            pltpu.VMEM((2, Z, Y, SLOTS, HALF), BF16),
            pltpu.VMEM((2, HALF, LOCAL), BF16),
            pltpu.VMEM((ROWS, LOCAL), F32),
            pltpu.SemaphoreType.DMA((18,)),
            pltpu.SemaphoreType.DMA((6,)),
        ],
        compiler_params=FULL,
    )(at, *pieces, weight)
    return own.reshape(ROWS, HALF), other.reshape(ROWS, HALF), logits, lse, top


def merge(x):
    top = jnp.max(x, axis=0)
    return top + jnp.log(jnp.sum(jnp.exp(x - top[None]), axis=0))


def merge_kernel(copies, *refs):
    lse = merge(jnp.stack([ref[...] for ref in refs[:-1]]))
    if copies == 1:
        refs[-1][...] = lse
    for k in range(copies if copies > 1 else 0):
        refs[-1][k] = lse


def merge_stats(parts, copies=1):
    shape = (8, 128) if copies == 1 else (copies, 8, 128)
    return pl.pallas_call(
        functools.partial(merge_kernel, copies),
        out_shape=jax.ShapeDtypeStruct(shape, F32),
        in_specs=[VMEM] * len(parts),
        out_specs=VMEM,
        compiler_params=PARAMS if copies == 1 else FULL,
    )(*parts)


def column(row):
    return jnp.broadcast_to(row, (128, row.shape[1])).T


def select_kernel(
    top_ref, far_ref, targets_ref, gid_ref, live_ref, e_ref, mass_ref, cross_ref, *scratch
):
    logits_ref, p_ref, top_col, parts_ref, out_ref, sems = scratch
    fetch = pltpu.make_async_copy(far_ref, logits_ref, sems.at[0])
    fetch.start()
    fetch_targets = pltpu.make_async_copy(targets_ref, p_ref, sems.at[1])
    fetch_targets.start()
    for j in range(8):
        top_col[pl.ds(j * 128, 128), :] = column(top_ref[j : j + 1, :])
    fetch.wait()

    @pl.loop(0, ROWS // 128)
    def _(i):
        rows = pl.ds(pl.multiple_of(i * 128, 128), 128)
        for j in range(LOCAL // 128):
            p = jnp.exp(logits_ref[rows, pl.ds(j * 128, 128)] - top_col[rows, :])
            first = p.astype(BF16)
            p = p - first.astype(F32)
            second = p.astype(BF16)
            third = (p - second.astype(F32)).astype(BF16)
            parts_ref[rows, pl.ds(j * 128, 128)] = first
            parts_ref[rows, pl.ds(LOCAL + j * 128, 128)] = second
            parts_ref[rows, pl.ds(2 * LOCAL + j * 128, 128)] = third

    def store(i):
        rows = pl.ds(pl.multiple_of(i * BLOCK, BLOCK), BLOCK)
        return pltpu.make_async_copy(out_ref.at[rows], e_ref.at[rows], sems.at[2 + i])

    @pl.loop(0, ROWS // BLOCK)
    def _(i):
        rows = pl.ds(pl.multiple_of(i * BLOCK, BLOCK), BLOCK)
        gid = column(gid_ref[:, rows])
        lane = lax.broadcasted_iota(jnp.int32, (BLOCK, 128), 1).astype(F32)
        hot = jnp.concatenate(
            [
                jnp.where(gid == lane + float(128 * k), 1.0, 0.0).astype(BF16)
                for k in range(ROWS // 128)
            ],
            axis=1,
        )
        sel = dot(hot, parts_ref[...])
        out_ref[rows, :] = sel[:, 0:LOCAL] + sel[:, LOCAL : 2 * LOCAL] + sel[:, 2 * LOCAL :]
        store(i).start()

    fetch_targets.wait()

    def total(i, cross):
        rows = pl.ds(pl.multiple_of(i * BLOCK, BLOCK), BLOCK)
        row = lax.broadcasted_iota(jnp.int32, (BLOCK, ROWS), 0) + i * BLOCK
        hot = jnp.where(gid_ref[...] == row.astype(F32), live_ref[...], 0.0).astype(BF16)
        sums = dot(hot, p_ref[...])
        mass = jnp.broadcast_to(jnp.sum(sums, axis=1, keepdims=True), (BLOCK, 128)).T[0:1]
        for j in range(BLOCK // 128):
            mass_ref[pl.ds(i * (BLOCK // 128) + j, 1), :] = mass[:, j * 128 : (j + 1) * 128]
        return cross + jnp.sum(sums * logits_ref[rows, :])

    cross_ref[0, 0] = lax.fori_loop(0, ROWS // BLOCK, total, jnp.float32(0))
    for i in range(ROWS // BLOCK):
        store(i).wait()


def select_rows(top, logits, probs, gid, live):
    return pl.pallas_call(
        select_kernel,
        out_shape=(
            jax.ShapeDtypeStruct((ROWS, LOCAL), F32),
            jax.ShapeDtypeStruct((8, 128), F32),
            jax.ShapeDtypeStruct((1, 1), F32),
        ),
        in_specs=[VMEM, ANY, ANY, VMEM, VMEM],
        out_specs=(ANY, VMEM, SMEM),
        scratch_shapes=[
            pltpu.VMEM((ROWS, LOCAL), F32),
            pltpu.VMEM((ROWS, LOCAL), BF16),
            pltpu.VMEM((ROWS, 128), F32),
            pltpu.VMEM((ROWS, 3 * LOCAL), BF16),
            pltpu.VMEM((ROWS, LOCAL), F32),
            pltpu.SemaphoreType.DMA((6,)),
        ],
        compiler_params=FULL,
        cost_estimate=pl.CostEstimate(
            flops=4 * 2 * ROWS * ROWS * LOCAL, bytes_accessed=8 * 1024 * 1024, transcendentals=0
        ),
    )(top, logits, probs, gid, live)


def grad_kernel(
    x_ref, top_ref, mass_ref, cross_ref, far_ref, targets_ref, gid_ref, live_ref, *refs
):
    high_ref, both_ref, loss_ref, e_ref, p_ref, g_ref, sums_ref, sems = refs
    fetch = pltpu.make_async_copy(far_ref, e_ref, sems.at[0])
    fetch.start()
    fetch_targets = pltpu.make_async_copy(targets_ref, p_ref, sems.at[1])
    fetch_targets.start()
    lse = merge(x_ref[...])
    loss_ref[0, 0] = jnp.sum(lse * mass_ref[...]) - cross_ref[0, 0]
    share = jnp.exp(top_ref[...] - lse)
    scale = VOCAB / math.sqrt(ROWS)
    fetch.wait()
    fetch_targets.wait()
    lane = lax.broadcasted_iota(jnp.int32, (128, 128), 1).astype(F32)

    @pl.loop(0, ROWS // 128)
    def _(i):
        rows = pl.ds(pl.multiple_of(i * 128, 128), 128)
        gid = column(gid_ref[:, rows])
        factor = column(live_ref[:, rows]) * scale
        found = jnp.zeros((128, 128), F32)
        for k in range(ROWS // 128):
            found += jnp.where(gid == lane + float(128 * k), share[k : k + 1], 0.0)
        found = jnp.sum(found, axis=1, keepdims=True)
        for j in range(LOCAL // 128):
            cols = pl.ds(j * 128, 128)
            diff = e_ref[rows, cols] * found - p_ref[rows, cols].astype(F32)
            g_ref[rows, cols] = (factor * diff).astype(BF16)

    def stores(i):
        rows = pl.ds(pl.multiple_of(i * BLOCK, BLOCK), BLOCK)
        high = sums_ref.at[rows, pl.ds(0, LOCAL)]
        yield pltpu.make_async_copy(high, high_ref.at[rows], sems.at[2 + i])
        yield pltpu.make_async_copy(sums_ref.at[rows], both_ref.at[rows], sems.at[6 + i])

    @pl.loop(0, ROWS // BLOCK)
    def _(i):
        rows = pl.ds(pl.multiple_of(i * BLOCK, BLOCK), BLOCK)
        row = lax.broadcasted_iota(jnp.int32, (BLOCK, ROWS), 0) + i * BLOCK
        hot = jnp.where(gid_ref[...] == row.astype(F32), 1.0, 0.0).astype(BF16)
        sums = dot(hot, g_ref[...])
        high = sums.astype(BF16)
        sums_ref[rows, 0:LOCAL] = high
        sums_ref[rows, LOCAL:] = (sums - high.astype(F32)).astype(BF16)
        for store in stores(i):
            store.start()

    for i in range(ROWS // BLOCK):
        for store in stores(i):
            store.wait()


def gradients(x, top, mass, cross, e, probs, gid, live):
    return pl.pallas_call(
        grad_kernel,
        out_shape=(
            jax.ShapeDtypeStruct((ROWS, LOCAL), BF16),
            jax.ShapeDtypeStruct((ROWS, 2 * LOCAL), BF16),
            jax.ShapeDtypeStruct((1, 1), F32),
        ),
        in_specs=[VMEM, VMEM, VMEM, SMEM, ANY, ANY, VMEM, VMEM],
        out_specs=(ANY, ANY, SMEM),
        scratch_shapes=[
            pltpu.VMEM((ROWS, LOCAL), F32),
            pltpu.VMEM((ROWS, LOCAL), BF16),
            pltpu.VMEM((ROWS, LOCAL), BF16),
            pltpu.VMEM((ROWS, 2 * LOCAL), BF16),
            pltpu.SemaphoreType.DMA((10,)),
        ],
        compiler_params=FULL,
    )(x, top, mass, cross, e, probs, gid, live)


TOP = 32700.0
ROWS2 = ROWS // 2
TAIL = 16
I16 = jnp.int16


def exponent(x):
    return jnp.ceil(jnp.log(jnp.maximum(x, 1e-30) / TOP) * (256.0 / math.log(2.0)))


def power(e):
    return jnp.exp2(e * (1.0 / 256.0))


def to16(x):
    return x.astype(jnp.int32).astype(I16)


def from16(x):
    return x.astype(jnp.int32).astype(F32)


def encode(val):
    e = exponent(jnp.max(jnp.abs(val), axis=1, keepdims=True))
    return to16(jnp.round(val * power(-e))), jnp.broadcast_to(e, (128, 128)).T[0:1]


def wide(row):
    return jnp.concatenate([row] + [jnp.zeros_like(row)] * (LOCAL // 128 - 1), axis=1)


def write_message(out_ref, block_of, loss, tail_ref):
    @pl.loop(0, ROWS2 // 128)
    def _(j):
        code, e = encode(block_of(j))
        out_ref[pl.ds(pl.multiple_of(j * 128, 128), 128), :] = code
        tail_ref[pl.ds(j, 1), :] = e

    tail = [tail_ref[0 : ROWS2 // 128, :], loss, jnp.zeros((TAIL - ROWS2 // 128 - 1, 128), F32)]
    tail = jnp.concatenate(tail, axis=0)
    zeros = [jnp.zeros_like(tail)] * (LOCAL // 128 - 1)
    out_ref[pl.ds(ROWS2, TAIL), :] = to16(jnp.concatenate([tail] + zeros, axis=1))


def encode_loss(loss):
    e = exponent(jnp.abs(loss))
    whole = loss * power(-e)
    first = jnp.round(whole)
    rest = jnp.round((whole - first) * TOP)
    lane = lax.broadcasted_iota(jnp.int32, (1, 128), 1)
    return jnp.where(lane == 0, e, jnp.where(lane == 1, first, jnp.where(lane == 2, rest, 0.0)))


def decode_loss(code):
    return (code[:, 1:2] + code[:, 2:3] * (1.0 / TOP)) * power(code[:, 0:1])


def read_tail(ref, tail_ref):
    tail_ref[...] = from16(ref[pl.ds(ROWS2, TAIL), 0:128])


def tail_loss(tail_ref):
    return tail_ref[ROWS2 // 128 : ROWS2 // 128 + 1, :]


def read_message(ref, tail_ref, j):
    scale = power(column(tail_ref[pl.ds(j, 1), :]))
    rows = pl.ds(pl.multiple_of(j * 128, 128), 128)
    parts = [from16(ref[rows, k * 128 : (k + 1) * 128]) * scale for k in range(LOCAL // 128)]
    return jnp.concatenate(parts, axis=1)


TAIL_REF = pltpu.VMEM((TAIL, 128), F32)
MESSAGE = jax.ShapeDtypeStruct((ROWS2 + TAIL, LOCAL), I16)


def weight_kernel(at_ref, all_ref, keep_ref, give_ref, block_ref, sems):
    c, x = at_ref[0], at_ref[1]

    def fetch(n):
        source = all_ref.at[lax.rem(x + n % 4, 4), lax.rem(c + n // 4, 2)]
        return pltpu.make_async_copy(source, block_ref.at[n], sems.at[n])

    for n in range(8):
        fetch(n).start()
    for n in range(8):
        fetch(n).wait()
        out = (keep_ref, give_ref)[n // 4]
        out[:, n % 4 * LOCAL : (n % 4 + 1) * LOCAL] = block_ref[n].T


def turn_weights(at, blocks):
    half = jax.ShapeDtypeStruct((LOCAL, 4 * LOCAL), BF16)
    return pl.pallas_call(
        weight_kernel,
        out_shape=(half, half),
        in_specs=[SMEM, ANY],
        out_specs=(VMEM, VMEM),
        scratch_shapes=[
            pltpu.VMEM((8, LOCAL, LOCAL), BF16),
            pltpu.SemaphoreType.DMA((8,)),
        ],
        compiler_params=FULL,
    )(at, blocks)


def term_kernel(
    loss_ref, more_ref, own_ref, other_ref, w_own, w_other, c0, l1, h1, l2, h2, l3, h3, sum_ref, *refs
):
    g_ref, w_ref, val_ref, tail_ref, sems = refs
    fetches = [
        pltpu.make_async_copy(ref, g_ref.at[:, pl.ds(k * LOCAL, LOCAL)], sems.at[k])
        for k, ref in enumerate((own_ref, other_ref))
    ] + [
        pltpu.make_async_copy(ref, w_ref.at[pl.ds(k * LOCAL, LOCAL)], sems.at[2 + k])
        for k, ref in enumerate((w_own, w_other))
    ]
    for fetch in fetches:
        fetch.start()
    loss = encode_loss(jnp.full((1, 128), loss_ref[0, 0] + more_ref[0, 0], F32))
    sum_ref[...] = loss
    for fetch in fetches:
        fetch.wait()

    @pl.loop(0, ROWS // BLOCK)
    def _(i):
        rows = pl.ds(pl.multiple_of(i * BLOCK, BLOCK), BLOCK)
        val_ref[rows, :] = dot(g_ref[rows, :], w_ref[...])

    c0[...] = val_ref[:, 0:LOCAL]
    for i, k, out in ((0, 2, l2), (1, 2, h2), (1, 1, h1), (0, 3, l3), (0, 1, l1), (1, 3, h3)):
        cols = slice(k * LOCAL, (k + 1) * LOCAL)
        if out.dtype == F32:
            out[...] = val_ref[i * ROWS2 : (i + 1) * ROWS2, cols]
        else:

            def block(j):
                at = pl.multiple_of(i * ROWS2 + j * 128, 128)
                return val_ref[pl.ds(at, 128), cols]

            write_message(out, block, loss, tail_ref)


def terms(loss, more, own, other, w_own, w_other):
    part = jax.ShapeDtypeStruct((ROWS2, LOCAL), F32)
    return pl.pallas_call(
        term_kernel,
        out_shape=(
            jax.ShapeDtypeStruct((ROWS, LOCAL), F32),
            part,
            MESSAGE,
            MESSAGE,
            MESSAGE,
            MESSAGE,
            part,
            jax.ShapeDtypeStruct((1, 128), F32),
        ),
        in_specs=[SMEM, SMEM] + [ANY] * 4,
        out_specs=(VMEM,) * 8,
        scratch_shapes=[
            pltpu.VMEM((ROWS, 2 * LOCAL), BF16),
            pltpu.VMEM((2 * LOCAL, 4 * LOCAL), BF16),
            pltpu.VMEM((ROWS, 4 * LOCAL), F32),
            TAIL_REF,
            pltpu.SemaphoreType.DMA((4,)),
        ],
        compiler_params=PARAMS,
    )(loss, more, own, other, w_own, w_other)


def relay_kernel(own_ref, got_ref, out_ref, got_tail, tail_ref):
    read_tail(got_ref, got_tail)

    def block(j):
        rows = pl.ds(pl.multiple_of(j * 128, 128), 128)
        return own_ref[rows, :] + read_message(got_ref, got_tail, j)

    write_message(out_ref, block, tail_loss(got_tail), tail_ref)


def relay(own, got):
    return pl.pallas_call(
        relay_kernel,
        out_shape=MESSAGE,
        in_specs=[VMEM] * 2,
        out_specs=VMEM,
        scratch_shapes=[TAIL_REF] * 2,
        compiler_params=PARAMS,
    )(own, got)


PACKED = 3 * SLOTS + TAIL


def pack_kernel(loss_ref, own_ref, low_r, low_l, high_r, high_l, o_ref, *tails):
    messages = (low_r, low_l, high_r, high_l)
    for ref, tail_ref in zip(messages, tails):
        read_tail(ref, tail_ref)
    codes = [loss_ref[...]] + [tail_loss(tail_ref) for tail_ref in tails[:3]]
    loss = decode_loss(jnp.concatenate(codes, axis=0))
    loss = (loss[0:1] + loss[1:2]) + (loss[2:3] + loss[3:4])
    loss = encode_loss(jnp.broadcast_to(loss, (1, 128)))
    pad = jnp.zeros((TAIL - 2, 128), F32)
    for i in range(2):

        @pl.loop(0, ROWS2 // 128)
        def _(j):
            at = i * (ROWS2 // 128) + j
            val = own_ref[pl.ds(pl.multiple_of(at * 128, 128), 128), :]
            got = [read_message(messages[n], tails[n], j) for n in (2 * i, 2 * i + 1)]
            code, e = encode(val + (got[0] + got[1]))
            tail = to16(jnp.concatenate([e, loss, pad], axis=0))
            for n in range(128 // SLOTS):
                for k in range(3):
                    o_ref[at * 4 + n, k * SLOTS : (k + 1) * SLOTS, :] = code[
                        n * SLOTS : (n + 1) * SLOTS, k * 128 : (k + 1) * 128
                    ]
                o_ref[at * 4 + n, 3 * SLOTS :, :] = tail


def pack(loss, own, low_r, low_l, high_r, high_l):
    return pl.pallas_call(
        pack_kernel,
        out_shape=jax.ShapeDtypeStruct((TRAINERS, PACKED, 128), I16),
        in_specs=[VMEM] * 6,
        out_specs=VMEM,
        scratch_shapes=[TAIL_REF] * 4,
        compiler_params=PARAMS,
    )(loss, own, low_r, low_l, high_r, high_l)


def finish_kernel(at_ref, x_ref, grad_ref, loss_ref, e_ref):
    tail = from16(x_ref[:, 3 * SLOTS :, :])
    e = tail[:, 0, :]
    e_ref[...] = jnp.concatenate([e, jnp.zeros((128 - TRAINERS, 128), F32)], axis=0).T
    scale = power(e_ref[pl.ds(pl.multiple_of(at_ref[0] * SLOTS, SLOTS), SLOTS), :])
    total = [jnp.zeros((SLOTS, 128), F32)] * 3
    for s in range(TRAINERS):
        for k in range(3):
            total[k] += from16(x_ref[s, k * SLOTS : (k + 1) * SLOTS, :]) * scale[:, s : s + 1]
    for k in range(3):
        grad_ref[:, k * 128 : (k + 1) * 128] = total[k]
    loss_ref[0, 0] = jnp.sum(decode_loss(tail[:, 1, :]))


def finish(at, x):
    return pl.pallas_call(
        finish_kernel,
        out_shape=(
            jax.ShapeDtypeStruct((SLOTS, LOCAL), F32),
            jax.ShapeDtypeStruct((1, 1), F32),
        ),
        in_specs=[SMEM, VMEM],
        out_specs=(VMEM, SMEM),
        scratch_shapes=[pltpu.VMEM((128, 128), F32)],
        compiler_params=PARAMS,
    )(at, x)


HEAD_BLOCK = 256
HEAD_STEPS = HALF // HEAD_BLOCK


def head_kernel(c_ref, own_ref, other_ref, sums_ref, o_ref):
    i = pl.program_id(0)

    def work(t_ref):
        both = dot(t_ref[...], sums_ref[...], ((0,), (0,)))
        both = both[:, 0:LOCAL] + both[:, LOCAL:]
        for j in range(LOCAL // 128):
            o_ref[pl.ds(j, HEAD_BLOCK, stride=LOCAL // 128), :] = both[:, j * 128 : (j + 1) * 128]

    @pl.when(i < HEAD_STEPS)
    def _():
        work(own_ref)

    @pl.when(i >= HEAD_STEPS)
    def _():
        work(other_ref)


def head_gradient(c, own, other, sums):
    def place(i, c):
        mine = i < HEAD_STEPS
        side = jnp.where(mine, c[0], 1 - c[0])
        return (side * HEAD_STEPS + jnp.where(mine, i, i - HEAD_STEPS), 0)

    return pl.pallas_call(
        head_kernel,
        grid_spec=pltpu.PrefetchScalarGridSpec(
            num_scalar_prefetch=1,
            grid=(2 * HEAD_STEPS,),
            in_specs=[
                pl.BlockSpec((ROWS, HEAD_BLOCK), lambda i, c: (0, jnp.minimum(i, HEAD_STEPS - 1))),
                pl.BlockSpec((ROWS, HEAD_BLOCK), lambda i, c: (0, jnp.maximum(i - HEAD_STEPS, 0))),
                pl.BlockSpec((ROWS, 2 * LOCAL), lambda i, c: (0, 0)),
            ],
            out_specs=pl.BlockSpec((HEAD_BLOCK * LOCAL // 128, 128), place),
        ),
        out_shape=jax.ShapeDtypeStruct((D * LOCAL // 128, 128), F32),
        compiler_params=PARAMS,
        cost_estimate=pl.CostEstimate(
            flops=4 * ROWS * D * LOCAL, bytes_accessed=12 * 1024 * 1024, transcendentals=0
        ),
    )(c, own, other, sums)


PAIR = [(i, i ^ 1) for i in range(SHARDS)]


def along_x(k):
    return [(i, (i + 2 * k) % SHARDS) for i in range(SHARDS)]


RIGHT, LEFT = along_x(1), along_x(-1)


def along_z(k):
    return [(i, (i // Y + k) % Z * Y + i % Y) for i in range(TRAINERS)]


def along_y(k):
    return [(i, i // Y * Y + (i + k) % Y) for i in range(TRAINERS)]


def on_device(hidden_table, head_weight, targets, counts, dest, token):
    me = lax.axis_index("vocab")
    trainer = lax.axis_index("trainer")
    c = lax.rem(me, 2)
    x = me // 2
    y = lax.rem(trainer, Y)
    c1 = c.reshape(1).astype(jnp.int32)
    at_cx = jnp.stack([c, x]).astype(jnp.int32)
    at_cy = jnp.stack([c, y]).astype(jnp.int32)
    z1 = (trainer // Y).reshape(1).astype(jnp.int32)
    weight = head_weight[:, 0, :]

    half = lax.dynamic_slice(hidden_table, (0, c * HALF), (SLOTS, HALF))
    near = [half] + [lax.ppermute(half, "trainer", along_z(k)) for k in range(1, Z)]

    split = split_targets(targets[:, 0, :])

    gid = dest * SLOTS + token
    index = jnp.arange(ROWS, dtype=jnp.int32)
    live = (index % SLOTS < jnp.repeat(counts, SLOTS)).astype(F32).reshape(1, ROWS)
    gid = gid.astype(F32).reshape(1, ROWS)

    w_own, w_give = turn_weights(at_cx, weight.reshape(4, 2, LOCAL, LOCAL))
    z1, split, gid, live, w_own, w_give = lax.optimization_barrier(
        (z1, split, gid, live, w_own, w_give)
    )
    low0, high0 = in_order(z1, near)
    low1 = lax.ppermute(low0, "trainer", along_y(1))
    high3 = lax.ppermute(high0, "trainer", along_y(-1))
    high1 = lax.ppermute(high0, "trainer", along_y(1))
    low3 = lax.ppermute(low0, "trainer", along_y(-1))
    low2 = lax.ppermute(low1, "trainer", along_y(1))
    high2 = lax.ppermute(high3, "trainer", along_y(-1))
    pieces = (low0, high0, low1, high1, low2, high2, low3, high3)
    pieces += tuple(lax.ppermute(p, "vocab", PAIR) for p in pieces)
    split, _ = lax.optimization_barrier((split, (low2, high2) + pieces[8:12] + pieces[14:]))
    probs = lax.all_to_all(split, "trainer", split_axis=0, concat_axis=0, tiled=True)

    own, other, logits, stats, top = logits_and_stats(at_cy, pieces, weight)
    stats = merge_stats([stats, lax.ppermute(stats, "vocab", PAIR)])
    stats = [stats] + [lax.ppermute(stats, "vocab", along_x(k)) for k in (1, 2, 3)]
    stats = merge_stats(stats, TRAINERS)
    stats, probs = lax.optimization_barrier((stats, probs.reshape(ROWS, LOCAL)))
    stats = lax.all_to_all(stats, "trainer", split_axis=0, concat_axis=0, tiled=True)

    w_give, _ = lax.optimization_barrier((w_give, top))
    w_other = lax.ppermute(w_give, "vocab", PAIR)
    e, mass, cross = select_rows(top, logits, probs, gid, live)
    high, sums, loss = gradients(stats, top, mass, cross, e, probs, gid, live)

    more = lax.ppermute(loss, "vocab", PAIR)
    far = lax.ppermute(high, "vocab", PAIR)
    t0, l1, h1, l2, h2, l3, h3, loss = terms(loss, more, high, far, w_own, w_other)
    low_r = lax.ppermute(l2, "vocab", RIGHT)
    high_l = lax.ppermute(h2, "vocab", LEFT)
    high_r = lax.ppermute(h1, "vocab", RIGHT)
    low_l = lax.ppermute(l3, "vocab", LEFT)
    low_r = lax.ppermute(relay(l1, low_r), "vocab", RIGHT)
    high_l = lax.ppermute(relay(h3, high_l), "vocab", LEFT)
    head = head_gradient(c1, own, other, sums)
    packed = pack(loss, t0, low_r, low_l, high_r, high_l)
    packed = lax.all_to_all(packed, "trainer", split_axis=0, concat_axis=0, tiled=True)
    table_grad, loss = finish(lax.rem(trainer, 4).reshape(1).astype(jnp.int32), packed)
    mean_loss = loss[0, 0] / jnp.sum(counts).astype(F32)
    return head.reshape(D, 1, LOCAL), table_grad, mean_loss


def solution(mesh):
    return jax.shard_map(
        on_device,
        mesh=mesh,
        in_specs=(
            P("trainer", None),
            P(None, "vocab", "trainer"),
            P("trainer", "vocab", None),
            P(),
            P(),
            P(),
        ),
        out_specs=(P(None, "vocab", "trainer"), P("trainer", "vocab"), P()),
        check_vma=False,
    )
```

```python
import functools
import math

import jax
import jax.numpy as jnp
from jax import lax
from jax.experimental import pallas as pl
from jax.experimental.pallas import tpu as pltpu
from jax.sharding import PartitionSpec as P

D = 3072
VOCAB = 98304
ROWS = 1024
TRAINERS = 32
SLOTS = 32
SHARDS = 8
LOCAL = VOCAB // (TRAINERS * SHARDS)
HALF = D // 2
BLOCK = 256
BF16 = jnp.bfloat16
F32 = jnp.float32
PARAMS = pltpu.CompilerParams(vmem_limit_bytes=24 * 1024 * 1024)
FULL = pltpu.CompilerParams(vmem_limit_bytes=60 * 1024 * 1024)
VMEM = pl.BlockSpec(memory_space=pltpu.VMEM)
SMEM = pl.BlockSpec(memory_space=pltpu.SMEM)
ANY = pl.BlockSpec(memory_space=pl.ANY)


def dot(a, b, dims=((1,), (0,))):
    return lax.dot_general(a, b, (dims, ((), ())), preferred_element_type=F32)


def split_kernel(x_ref, o_ref):
    for j in range(TRAINERS):
        o_ref[j] = x_ref[:, j * LOCAL : (j + 1) * LOCAL]


def split_targets(x):
    return pl.pallas_call(
        split_kernel,
        out_shape=jax.ShapeDtypeStruct((TRAINERS, SLOTS, LOCAL), BF16),
        in_specs=[VMEM],
        out_specs=VMEM,
        compiler_params=FULL,
    )(x)


Z = 8
Y = 4


PLACES = (((0, 0), (0, 4)), ((1, 0), (1, 8)), ((2, 0), (2, 4)), ((1, 12), (1, 4)))


def order_kernel(z_ref, *refs):
    for k, piece in enumerate(refs[:Z]):
        refs[Z][lax.rem(z_ref[0] + Z - k, Z)] = piece[...]


def in_order(z, pieces):
    return pl.pallas_call(
        order_kernel,
        out_shape=jax.ShapeDtypeStruct((Z, SLOTS, HALF), BF16),
        in_specs=[SMEM] + [VMEM] * Z,
        out_specs=VMEM,
        compiler_params=PARAMS,
    )(z, *pieces)


def logit_kernel(at_ref, *refs):
    pieces, refs = refs[:6], refs[6:]
    far_ref, table_ref, logits_ref, lse_ref, top_ref, *refs = refs
    tabs, w_ref, logit_buf, in_sems, out_sems = refs
    c, y = at_ref[0], at_ref[1]
    copies = [[], []]
    for side in range(2):
        rows = pl.ds(pl.multiple_of((c + side) % 2 * HALF, HALF), HALF)
        copies[side].append(
            pltpu.make_async_copy(far_ref.at[rows], w_ref.at[side], in_sems.at[16 + side])
        )
        for dy in range(Y):
            y_at = lax.rem(y + Y - dy, Y)
            for high in range(2):
                which, first = PLACES[dy][high]
                piece = pieces[side * 3 + which].at[pl.ds(first, Z // 2)]
                place = tabs.at[side, pl.ds(high * (Z // 2), Z // 2), y_at]
                sem = in_sems.at[side * 8 + dy * 2 + high]
                copies[side].append(pltpu.make_async_copy(piece, place, sem))
        for copy in copies[side]:
            copy.start()
    block = 2 * BLOCK
    step = block // (Y * SLOTS)

    def part(side, i):
        rows = tabs[side, pl.ds(i * step, step)].reshape(block, HALF)
        return dot(rows, w_ref[side])

    def store(i):
        rows = pl.ds(i * block, block)
        return pltpu.make_async_copy(logit_buf.at[rows], logits_ref.at[rows], out_sems.at[2 + i])

    stores = []
    for side in range(2):
        for copy in copies[side]:
            copy.wait()
        stores.append(
            pltpu.make_async_copy(tabs.at[side], table_ref.at[side], out_sems.at[side])
        )
        stores[-1].start()
        for i in range(ROWS // block):
            rows = pl.ds(i * block, block)
            if side == 0:
                logit_buf[rows, :] = part(side, i)
                continue
            logits = logit_buf[rows, :] + part(side, i)
            logit_buf[rows, :] = logits
            store(i).start()
            top = jnp.max(logits, axis=1, keepdims=True)
            lse = top + jnp.log(jnp.sum(jnp.exp(logits - top), axis=1, keepdims=True))
            for value, out in ((lse, lse_ref), (top, top_ref)):
                flat = jnp.broadcast_to(value, (block, 128)).T
                for j in range(block // 128):
                    row = flat[0:1, j * 128 : (j + 1) * 128]
                    out[pl.ds(i * (block // 128) + j, 1), :] = row

    for copy in stores + [store(i) for i in range(ROWS // block)]:
        copy.wait()


def logits_and_stats(at, pieces, weight):
    table, logits, lse, top = pl.pallas_call(
        logit_kernel,
        out_shape=(
            jax.ShapeDtypeStruct((2, Z, Y, SLOTS, HALF), BF16),
            jax.ShapeDtypeStruct((ROWS, LOCAL), F32),
            jax.ShapeDtypeStruct((8, 128), F32),
            jax.ShapeDtypeStruct((8, 128), F32),
        ),
        in_specs=[SMEM] + [ANY] * 7,
        out_specs=(ANY, ANY, VMEM, VMEM),
        scratch_shapes=[
            pltpu.VMEM((2, Z, Y, SLOTS, HALF), BF16),
            pltpu.VMEM((2, HALF, LOCAL), BF16),
            pltpu.VMEM((ROWS, LOCAL), F32),
            pltpu.SemaphoreType.DMA((18,)),
            pltpu.SemaphoreType.DMA((6,)),
        ],
        compiler_params=FULL,
    )(at, *pieces, weight)
    return table.reshape(2, ROWS, HALF), logits, lse, top


def merge(x):
    top = jnp.max(x, axis=0)
    return top + jnp.log(jnp.sum(jnp.exp(x - top[None]), axis=0))


def merge_kernel(copies, *refs):
    lse = merge(jnp.stack([ref[...] for ref in refs[:-1]]))
    if copies == 1:
        refs[-1][...] = lse
    for k in range(copies if copies > 1 else 0):
        refs[-1][k] = lse


def merge_stats(parts, copies=1):
    shape = (8, 128) if copies == 1 else (copies, 8, 128)
    return pl.pallas_call(
        functools.partial(merge_kernel, copies),
        out_shape=jax.ShapeDtypeStruct(shape, F32),
        in_specs=[VMEM] * len(parts),
        out_specs=VMEM,
        compiler_params=PARAMS if copies == 1 else FULL,
    )(*parts)


def column(row):
    return jnp.broadcast_to(row, (128, row.shape[1])).T


def select_kernel(
    top_ref, far_ref, targets_ref, gid_ref, live_ref, e_ref, mass_ref, cross_ref, *scratch
):
    logits_ref, p_ref, top_col, parts_ref, out_ref, sems = scratch
    fetch = pltpu.make_async_copy(far_ref, logits_ref, sems.at[0])
    fetch.start()
    fetch_targets = pltpu.make_async_copy(targets_ref, p_ref, sems.at[1])
    fetch_targets.start()
    for j in range(8):
        top_col[pl.ds(j * 128, 128), :] = column(top_ref[j : j + 1, :])
    fetch.wait()

    @pl.loop(0, ROWS // 128)
    def _(i):
        rows = pl.ds(pl.multiple_of(i * 128, 128), 128)
        for j in range(LOCAL // 128):
            p = jnp.exp(logits_ref[rows, pl.ds(j * 128, 128)] - top_col[rows, :])
            first = p.astype(BF16)
            p = p - first.astype(F32)
            second = p.astype(BF16)
            third = (p - second.astype(F32)).astype(BF16)
            parts_ref[rows, pl.ds(j * 128, 128)] = first
            parts_ref[rows, pl.ds(LOCAL + j * 128, 128)] = second
            parts_ref[rows, pl.ds(2 * LOCAL + j * 128, 128)] = third

    def store(i):
        rows = pl.ds(pl.multiple_of(i * BLOCK, BLOCK), BLOCK)
        return pltpu.make_async_copy(out_ref.at[rows], e_ref.at[rows], sems.at[2 + i])

    @pl.loop(0, ROWS // BLOCK)
    def _(i):
        rows = pl.ds(pl.multiple_of(i * BLOCK, BLOCK), BLOCK)
        gid = column(gid_ref[:, rows])
        lane = lax.broadcasted_iota(jnp.int32, (BLOCK, 128), 1).astype(F32)
        hot = jnp.concatenate(
            [
                jnp.where(gid == lane + float(128 * k), 1.0, 0.0).astype(BF16)
                for k in range(ROWS // 128)
            ],
            axis=1,
        )
        sel = dot(hot, parts_ref[...])
        out_ref[rows, :] = sel[:, 0:LOCAL] + sel[:, LOCAL : 2 * LOCAL] + sel[:, 2 * LOCAL :]
        store(i).start()

    fetch_targets.wait()

    def total(i, cross):
        rows = pl.ds(pl.multiple_of(i * BLOCK, BLOCK), BLOCK)
        row = lax.broadcasted_iota(jnp.int32, (BLOCK, ROWS), 0) + i * BLOCK
        hot = jnp.where(gid_ref[...] == row.astype(F32), live_ref[...], 0.0).astype(BF16)
        sums = dot(hot, p_ref[...])
        mass = jnp.broadcast_to(jnp.sum(sums, axis=1, keepdims=True), (BLOCK, 128)).T[0:1]
        for j in range(BLOCK // 128):
            mass_ref[pl.ds(i * (BLOCK // 128) + j, 1), :] = mass[:, j * 128 : (j + 1) * 128]
        return cross + jnp.sum(sums * logits_ref[rows, :])

    cross_ref[0, 0] = lax.fori_loop(0, ROWS // BLOCK, total, jnp.float32(0))
    for i in range(ROWS // BLOCK):
        store(i).wait()


def select_rows(top, logits, probs, gid, live):
    return pl.pallas_call(
        select_kernel,
        out_shape=(
            jax.ShapeDtypeStruct((ROWS, LOCAL), F32),
            jax.ShapeDtypeStruct((8, 128), F32),
            jax.ShapeDtypeStruct((1, 1), F32),
        ),
        in_specs=[VMEM, ANY, ANY, VMEM, VMEM],
        out_specs=(ANY, VMEM, SMEM),
        scratch_shapes=[
            pltpu.VMEM((ROWS, LOCAL), F32),
            pltpu.VMEM((ROWS, LOCAL), BF16),
            pltpu.VMEM((ROWS, 128), F32),
            pltpu.VMEM((ROWS, 3 * LOCAL), BF16),
            pltpu.VMEM((ROWS, LOCAL), F32),
            pltpu.SemaphoreType.DMA((6,)),
        ],
        compiler_params=FULL,
        cost_estimate=pl.CostEstimate(
            flops=4 * 2 * ROWS * ROWS * LOCAL, bytes_accessed=8 * 1024 * 1024, transcendentals=0
        ),
    )(top, logits, probs, gid, live)


def grad_kernel(
    x_ref, top_ref, mass_ref, cross_ref, far_ref, targets_ref, gid_ref, live_ref, *refs
):
    high_ref, both_ref, loss_ref, e_ref, p_ref, g_ref, sums_ref, sems = refs
    fetch = pltpu.make_async_copy(far_ref, e_ref, sems.at[0])
    fetch.start()
    fetch_targets = pltpu.make_async_copy(targets_ref, p_ref, sems.at[1])
    fetch_targets.start()
    lse = merge(x_ref[...])
    loss_ref[0, 0] = jnp.sum(lse * mass_ref[...]) - cross_ref[0, 0]
    share = jnp.exp(top_ref[...] - lse)
    scale = VOCAB / math.sqrt(ROWS)
    fetch.wait()
    fetch_targets.wait()
    lane = lax.broadcasted_iota(jnp.int32, (128, 128), 1).astype(F32)
    for i in range(ROWS // 128):
        rows = pl.ds(i * 128, 128)
        gid = column(gid_ref[:, rows])
        factor = column(live_ref[:, rows]) * scale
        found = jnp.zeros((128, 128), F32)
        for k in range(ROWS // 128):
            found += jnp.where(gid == lane + float(128 * k), share[k : k + 1], 0.0)
        found = jnp.sum(found, axis=1, keepdims=True)
        for j in range(LOCAL // 128):
            cols = pl.ds(j * 128, 128)
            diff = e_ref[rows, cols] * found - p_ref[rows, cols].astype(F32)
            g_ref[rows, cols] = (factor * diff).astype(BF16)

    def stores(i):
        rows = pl.ds(pl.multiple_of(i * BLOCK, BLOCK), BLOCK)
        high = sums_ref.at[rows, pl.ds(0, LOCAL)]
        yield pltpu.make_async_copy(high, high_ref.at[rows], sems.at[2 + i])
        yield pltpu.make_async_copy(sums_ref.at[rows], both_ref.at[rows], sems.at[6 + i])

    @pl.loop(0, ROWS // BLOCK)
    def _(i):
        rows = pl.ds(pl.multiple_of(i * BLOCK, BLOCK), BLOCK)
        row = lax.broadcasted_iota(jnp.int32, (BLOCK, ROWS), 0) + i * BLOCK
        hot = jnp.where(gid_ref[...] == row.astype(F32), 1.0, 0.0).astype(BF16)
        sums = dot(hot, g_ref[...])
        high = sums.astype(BF16)
        sums_ref[rows, 0:LOCAL] = high
        sums_ref[rows, LOCAL:] = (sums - high.astype(F32)).astype(BF16)
        for store in stores(i):
            store.start()

    for i in range(ROWS // BLOCK):
        for store in stores(i):
            store.wait()


def gradients(x, top, mass, cross, e, probs, gid, live):
    return pl.pallas_call(
        grad_kernel,
        out_shape=(
            jax.ShapeDtypeStruct((ROWS, LOCAL), BF16),
            jax.ShapeDtypeStruct((ROWS, 2 * LOCAL), BF16),
            jax.ShapeDtypeStruct((1, 1), F32),
        ),
        in_specs=[VMEM, VMEM, VMEM, SMEM, ANY, ANY, VMEM, VMEM],
        out_specs=(ANY, ANY, SMEM),
        scratch_shapes=[
            pltpu.VMEM((ROWS, LOCAL), F32),
            pltpu.VMEM((ROWS, LOCAL), BF16),
            pltpu.VMEM((ROWS, LOCAL), BF16),
            pltpu.VMEM((ROWS, 2 * LOCAL), BF16),
            pltpu.SemaphoreType.DMA((10,)),
        ],
        compiler_params=FULL,
    )(x, top, mass, cross, e, probs, gid, live)


TOP = 32700.0
ROWS2 = ROWS // 2
TAIL = 16
I16 = jnp.int16


def exponent(x):
    return jnp.ceil(jnp.log(jnp.maximum(x, 1e-30) / TOP) * (256.0 / math.log(2.0)))


def power(e):
    return jnp.exp2(e * (1.0 / 256.0))


def to16(x):
    return x.astype(jnp.int32).astype(I16)


def from16(x):
    return x.astype(jnp.int32).astype(F32)


def encode(val):
    e = exponent(jnp.max(jnp.abs(val), axis=1, keepdims=True))
    return to16(jnp.round(val * power(-e))), jnp.broadcast_to(e, (128, 128)).T[0:1]


def wide(row):
    return jnp.concatenate([row] + [jnp.zeros_like(row)] * (LOCAL // 128 - 1), axis=1)


def write_message(out_ref, block_of, loss, tail_ref):
    for j in range(ROWS2 // 128):
        code, e = encode(block_of(j))
        out_ref[pl.ds(j * 128, 128), :] = code
        tail_ref[pl.ds(j, 1), :] = e
    tail = [tail_ref[0 : ROWS2 // 128, :], loss, jnp.zeros((TAIL - ROWS2 // 128 - 1, 128), F32)]
    tail = jnp.concatenate(tail, axis=0)
    zeros = [jnp.zeros_like(tail)] * (LOCAL // 128 - 1)
    out_ref[pl.ds(ROWS2, TAIL), :] = to16(jnp.concatenate([tail] + zeros, axis=1))


def encode_loss(loss):
    e = exponent(jnp.abs(loss))
    whole = loss * power(-e)
    first = jnp.round(whole)
    rest = jnp.round((whole - first) * TOP)
    lane = lax.broadcasted_iota(jnp.int32, (1, 128), 1)
    return jnp.where(lane == 0, e, jnp.where(lane == 1, first, jnp.where(lane == 2, rest, 0.0)))


def decode_loss(code):
    return (code[:, 1:2] + code[:, 2:3] * (1.0 / TOP)) * power(code[:, 0:1])


def read_tail(ref, tail_ref):
    tail_ref[...] = from16(ref[pl.ds(ROWS2, TAIL), 0:128])


def tail_loss(tail_ref):
    return tail_ref[ROWS2 // 128 : ROWS2 // 128 + 1, :]


def read_message(ref, tail_ref, j):
    scale = power(column(tail_ref[pl.ds(j, 1), :]))
    rows = pl.ds(j * 128, 128)
    parts = [from16(ref[rows, k * 128 : (k + 1) * 128]) * scale for k in range(LOCAL // 128)]
    return jnp.concatenate(parts, axis=1)


TAIL_REF = pltpu.VMEM((TAIL, 128), F32)
MESSAGE = jax.ShapeDtypeStruct((ROWS2 + TAIL, LOCAL), I16)


def weight_kernel(at_ref, all_ref, keep_ref, give_ref, block_ref, sems):
    c, x = at_ref[0], at_ref[1]

    def fetch(n):
        source = all_ref.at[lax.rem(x + (2, 1, 3, 0)[n % 4], 4), lax.rem(c + n // 4, 2)]
        return pltpu.make_async_copy(source, block_ref.at[n], sems.at[n])

    for n in range(8):
        fetch(n).start()
    for n in range(8):
        fetch(n).wait()
        out = (keep_ref, give_ref)[n // 4]
        out[:, n % 4 * LOCAL : (n % 4 + 1) * LOCAL] = block_ref[n].T


def turn_weights(at, blocks):
    half = jax.ShapeDtypeStruct((LOCAL, 4 * LOCAL), BF16)
    return pl.pallas_call(
        weight_kernel,
        out_shape=(half, half),
        in_specs=[SMEM, ANY],
        out_specs=(VMEM, VMEM),
        scratch_shapes=[
            pltpu.VMEM((8, LOCAL, LOCAL), BF16),
            pltpu.SemaphoreType.DMA((8,)),
        ],
        compiler_params=FULL,
    )(at, blocks)


def fetch_pair(own_ref, other_ref, w_own, w_other, first, n, g_ref, w_ref, sems):
    cols = pl.ds(first * LOCAL, n * LOCAL)
    copies = [
        pltpu.make_async_copy(ref, g_ref.at[:, pl.ds(k * LOCAL, LOCAL)], sems.at[k])
        for k, ref in enumerate((own_ref, other_ref))
    ] + [
        pltpu.make_async_copy(ref.at[:, cols], w_ref.at[pl.ds(k * LOCAL, LOCAL)], sems.at[2 + k])
        for k, ref in enumerate((w_own, w_other))
    ]
    for copy in copies:
        copy.start()
    return copies


def far_kernel(
    loss_ref, more_ref, own_ref, other_ref, w_own, w_other, low, high, sum_ref, *refs
):
    g_ref, w_ref, val_ref, tail_ref, sems = refs
    copies = fetch_pair(own_ref, other_ref, w_own, w_other, 0, 1, g_ref, w_ref, sems)
    loss = encode_loss(jnp.full((1, 128), loss_ref[0, 0] + more_ref[0, 0], F32))
    sum_ref[...] = loss
    for copy in copies:
        copy.wait()
    for i, out in enumerate((low, high)):
        val_ref[...] = dot(g_ref[pl.ds(i * ROWS2, ROWS2), :], w_ref[...])
        write_message(out, lambda j: val_ref[pl.ds(j * 128, 128), :], loss, tail_ref)


def near_kernel(
    loss_ref, own_ref, other_ref, w_own, w_other, l1, h1, l3, h3, c0, g_ref, w_ref, val_ref, tail_ref, sems
):
    copies = fetch_pair(own_ref, other_ref, w_own, w_other, 1, 3, g_ref, w_ref, sems)
    for copy in copies:
        copy.wait()
    for i in range(2):
        rows = pl.ds(i * ROWS2, ROWS2)
        val_ref[...] = dot(g_ref[rows, :], w_ref[...])
        for k, out in enumerate(((l1, h1)[i], (l3, h3)[i])):
            cols = slice(k * LOCAL, (k + 1) * LOCAL)
            if out.dtype == F32:
                out[...] = val_ref[:, cols]
            else:
                write_message(
                    out, lambda j: val_ref[pl.ds(j * 128, 128), cols], loss_ref[...], tail_ref
                )
        c0[rows, :] = val_ref[:, 2 * LOCAL :]


def pair_scratch(n):
    return [
        pltpu.VMEM((ROWS, 2 * LOCAL), BF16),
        pltpu.VMEM((2 * LOCAL, n * LOCAL), BF16),
        pltpu.VMEM((ROWS2, n * LOCAL), F32),
        TAIL_REF,
        pltpu.SemaphoreType.DMA((4,)),
    ]


def far_terms(loss, more, own, other, w_own, w_other):
    return pl.pallas_call(
        far_kernel,
        out_shape=(MESSAGE, MESSAGE, jax.ShapeDtypeStruct((1, 128), F32)),
        in_specs=[SMEM, SMEM] + [ANY] * 4,
        out_specs=(VMEM,) * 3,
        scratch_shapes=pair_scratch(1),
        compiler_params=PARAMS,
    )(loss, more, own, other, w_own, w_other)


def near_terms(loss, own, other, w_own, w_other):
    part = jax.ShapeDtypeStruct((ROWS2, LOCAL), F32)
    return pl.pallas_call(
        near_kernel,
        out_shape=(part, MESSAGE, MESSAGE, part, jax.ShapeDtypeStruct((ROWS, LOCAL), F32)),
        in_specs=[VMEM] + [ANY] * 4,
        out_specs=(VMEM,) * 5,
        scratch_shapes=pair_scratch(3),
        compiler_params=PARAMS,
    )(loss, own, other, w_own, w_other)


def relay_kernel(own_ref, got_ref, out_ref, got_tail, tail_ref):
    read_tail(got_ref, got_tail)

    def block(j):
        rows = pl.ds(j * 128, 128)
        return own_ref[rows, :] + read_message(got_ref, got_tail, j)

    write_message(out_ref, block, tail_loss(got_tail), tail_ref)


def relay(own, got):
    return pl.pallas_call(
        relay_kernel,
        out_shape=MESSAGE,
        in_specs=[VMEM] * 2,
        out_specs=VMEM,
        scratch_shapes=[TAIL_REF] * 2,
        compiler_params=PARAMS,
    )(own, got)


PACKED = 3 * SLOTS + TAIL


def pack_kernel(loss_ref, own_ref, low_r, low_l, high_r, high_l, o_ref, *tails):
    messages = (low_r, low_l, high_r, high_l)
    for ref, tail_ref in zip(messages, tails):
        read_tail(ref, tail_ref)
    codes = [loss_ref[...]] + [tail_loss(tail_ref) for tail_ref in tails[:3]]
    loss = decode_loss(jnp.concatenate(codes, axis=0))
    loss = (loss[0:1] + loss[1:2]) + (loss[2:3] + loss[3:4])
    loss = encode_loss(jnp.broadcast_to(loss, (1, 128)))
    pad = jnp.zeros((TAIL - 2, 128), F32)
    for i in range(2):
        for j in range(ROWS2 // 128):
            at = i * (ROWS2 // 128) + j
            val = own_ref[pl.ds(at * 128, 128), :]
            got = [read_message(messages[n], tails[n], j) for n in (2 * i, 2 * i + 1)]
            code, e = encode(val + (got[0] + got[1]))
            tail = to16(jnp.concatenate([e, loss, pad], axis=0))
            for n in range(128 // SLOTS):
                for k in range(3):
                    o_ref[at * 4 + n, k * SLOTS : (k + 1) * SLOTS, :] = code[
                        n * SLOTS : (n + 1) * SLOTS, k * 128 : (k + 1) * 128
                    ]
                o_ref[at * 4 + n, 3 * SLOTS :, :] = tail


def pack(loss, own, low_r, low_l, high_r, high_l):
    return pl.pallas_call(
        pack_kernel,
        out_shape=jax.ShapeDtypeStruct((TRAINERS, PACKED, 128), I16),
        in_specs=[VMEM] * 6,
        out_specs=VMEM,
        scratch_shapes=[TAIL_REF] * 4,
        compiler_params=PARAMS,
    )(loss, own, low_r, low_l, high_r, high_l)


def finish_kernel(at_ref, x_ref, grad_ref, loss_ref, e_ref):
    tail = from16(x_ref[:, 3 * SLOTS :, :])
    e = tail[:, 0, :]
    e_ref[...] = jnp.concatenate([e, jnp.zeros((128 - TRAINERS, 128), F32)], axis=0).T
    scale = power(e_ref[pl.ds(pl.multiple_of(at_ref[0] * SLOTS, SLOTS), SLOTS), :])
    total = [jnp.zeros((SLOTS, 128), F32)] * 3
    for s in range(TRAINERS):
        for k in range(3):
            total[k] += from16(x_ref[s, k * SLOTS : (k + 1) * SLOTS, :]) * scale[:, s : s + 1]
    for k in range(3):
        grad_ref[:, k * 128 : (k + 1) * 128] = total[k]
    loss_ref[0, 0] = jnp.sum(decode_loss(tail[:, 1, :]))


def finish(at, x):
    return pl.pallas_call(
        finish_kernel,
        out_shape=(
            jax.ShapeDtypeStruct((SLOTS, LOCAL), F32),
            jax.ShapeDtypeStruct((1, 1), F32),
        ),
        in_specs=[SMEM, VMEM],
        out_specs=(VMEM, SMEM),
        scratch_shapes=[pltpu.VMEM((128, 128), F32)],
        compiler_params=PARAMS,
    )(at, x)


HEAD_BLOCK = 256
HEAD_STEPS = HALF // HEAD_BLOCK


def head_kernel(c_ref, table_ref, sums_ref, o_ref):
    both = dot(table_ref[0], sums_ref[...], ((0,), (0,)))
    both = both[:, 0:LOCAL] + both[:, LOCAL:]
    for j in range(LOCAL // 128):
        o_ref[pl.ds(j, HEAD_BLOCK, stride=LOCAL // 128), :] = both[:, j * 128 : (j + 1) * 128]


def head_gradient(c, table, sums):
    def place(i, c):
        side = lax.rem(c[0] + i // HEAD_STEPS, 2)
        return (side * HEAD_STEPS + i % HEAD_STEPS, 0)

    return pl.pallas_call(
        head_kernel,
        grid_spec=pltpu.PrefetchScalarGridSpec(
            num_scalar_prefetch=1,
            grid=(2 * HEAD_STEPS,),
            in_specs=[
                pl.BlockSpec(
                    (1, ROWS, HEAD_BLOCK), lambda i, c: (i // HEAD_STEPS, 0, i % HEAD_STEPS)
                ),
                pl.BlockSpec((ROWS, 2 * LOCAL), lambda i, c: (0, 0)),
            ],
            out_specs=pl.BlockSpec((HEAD_BLOCK * LOCAL // 128, 128), place),
        ),
        out_shape=jax.ShapeDtypeStruct((D * LOCAL // 128, 128), F32),
        compiler_params=PARAMS,
        cost_estimate=pl.CostEstimate(
            flops=4 * ROWS * D * LOCAL, bytes_accessed=12 * 1024 * 1024, transcendentals=0
        ),
    )(c, table, sums)


PAIR = [(i, i ^ 1) for i in range(SHARDS)]


def along_x(k):
    return [(i, (i + 2 * k) % SHARDS) for i in range(SHARDS)]


RIGHT, LEFT = along_x(1), along_x(-1)


def along_z(k):
    return [(i, (i // Y + k) % Z * Y + i % Y) for i in range(TRAINERS)]


def along_y(k):
    return [(i, i // Y * Y + (i + k) % Y) for i in range(TRAINERS)]


def on_device(hidden_table, head_weight, targets, counts, dest, token):
    me = lax.axis_index("vocab")
    trainer = lax.axis_index("trainer")
    c = lax.rem(me, 2)
    x = me // 2
    y = lax.rem(trainer, Y)
    c1 = c.reshape(1).astype(jnp.int32)
    at_cx = jnp.stack([c, x]).astype(jnp.int32)
    at_cy = jnp.stack([c, y]).astype(jnp.int32)
    z1 = (trainer // Y).reshape(1).astype(jnp.int32)
    weight = head_weight[:, 0, :]

    half = lax.dynamic_slice(hidden_table, (0, c * HALF), (SLOTS, HALF))
    near = [half] + [lax.ppermute(half, "trainer", along_z(k)) for k in range(1, Z)]

    gid = dest * SLOTS + token
    index = jnp.arange(ROWS, dtype=jnp.int32)
    live = (index % SLOTS < jnp.repeat(counts, SLOTS)).astype(F32).reshape(1, ROWS)
    gid = gid.astype(F32).reshape(1, ROWS)

    z1, gid, live = lax.optimization_barrier((z1, gid, live))
    plane = in_order(z1, near)
    low0, high0 = plane[: Z // 2], plane[Z // 2 :]
    low1 = lax.ppermute(low0, "trainer", along_y(1))
    high3 = lax.ppermute(high0, "trainer", along_y(-1))
    high1 = lax.ppermute(high0, "trainer", along_y(1))
    low3 = lax.ppermute(low0, "trainer", along_y(-1))
    low2 = lax.ppermute(low1, "trainer", along_y(1))
    high2 = lax.ppermute(high3, "trainer", along_y(-1))
    at_cx, targets, _ = lax.optimization_barrier((at_cx, targets, low1))
    split = split_targets(targets[:, 0, :])
    w_own, w_give = turn_weights(at_cx, weight.reshape(4, 2, LOCAL, LOCAL))
    high1, split, w_own, w_give = lax.optimization_barrier((high1, split, w_own, w_give))
    pieces = [plane, jnp.concatenate([low1, high3, high1, low3]), jnp.concatenate([low2, high2])]
    pieces += [lax.ppermute(p, "vocab", PAIR) for p in pieces]
    split, _ = lax.optimization_barrier((split, (pieces[2], pieces[3], pieces[4])))
    probs = lax.all_to_all(split, "trainer", split_axis=0, concat_axis=0, tiled=True)

    table, logits, stats, top = logits_and_stats(at_cy, pieces, weight)
    stats = merge_stats([stats, lax.ppermute(stats, "vocab", PAIR)])
    stats = [stats] + [lax.ppermute(stats, "vocab", along_x(k)) for k in (1, 2, 3)]
    stats = merge_stats(stats, TRAINERS)
    w_give, _ = lax.optimization_barrier((w_give, stats))
    w_other = lax.ppermute(w_give, "vocab", PAIR)
    stats, probs = lax.optimization_barrier((stats, probs.reshape(ROWS, LOCAL)))
    stats = lax.all_to_all(stats, "trainer", split_axis=0, concat_axis=0, tiled=True)

    e, mass, cross = select_rows(top, logits, probs, gid, live)
    high, sums, loss = gradients(stats, top, mass, cross, e, probs, gid, live)

    more = lax.ppermute(loss, "vocab", PAIR)
    far = lax.ppermute(high, "vocab", PAIR)
    l2, h2, loss = far_terms(loss, more, high, far, w_own, w_other)
    low_r = lax.ppermute(l2, "vocab", RIGHT)
    high_l = lax.ppermute(h2, "vocab", LEFT)
    l1, h1, l3, h3, t0 = near_terms(loss, high, far, w_own, w_other)
    high_r = lax.ppermute(h1, "vocab", RIGHT)
    low_l = lax.ppermute(l3, "vocab", LEFT)
    low_r = lax.ppermute(relay(l1, low_r), "vocab", RIGHT)
    high_l = lax.ppermute(relay(h3, high_l), "vocab", LEFT)
    head = head_gradient(c1, table, sums)
    packed = pack(loss, t0, low_r, low_l, high_r, high_l)
    packed = lax.all_to_all(packed, "trainer", split_axis=0, concat_axis=0, tiled=True)
    table_grad, loss = finish(lax.rem(trainer, 4).reshape(1).astype(jnp.int32), packed)
    mean_loss = loss[0, 0] / jnp.sum(counts).astype(F32)
    return head.reshape(D, 1, LOCAL), table_grad, mean_loss


def solution(mesh):
    return jax.shard_map(
        on_device,
        mesh=mesh,
        in_specs=(
            P("trainer", None),
            P(None, "vocab", "trainer"),
            P("trainer", "vocab", None),
            P(),
            P(),
            P(),
        ),
        out_specs=(P(None, "vocab", "trainer"), P("trainer", "vocab"), P()),
        check_vma=False,
    )
```

```python
import functools
import math

import jax
import jax.numpy as jnp
from jax import lax
from jax.experimental import pallas as pl
from jax.experimental.pallas import tpu as pltpu
from jax.sharding import PartitionSpec as P

D = 3072
VOCAB = 98304
ROWS = 1024
TRAINERS = 32
SLOTS = 32
SHARDS = 8
LOCAL = VOCAB // (TRAINERS * SHARDS)
HALF = D // 2
BLOCK = 256
BF16 = jnp.bfloat16
F32 = jnp.float32
PARAMS = pltpu.CompilerParams(vmem_limit_bytes=24 * 1024 * 1024)
FULL = pltpu.CompilerParams(vmem_limit_bytes=60 * 1024 * 1024)
VMEM = pl.BlockSpec(memory_space=pltpu.VMEM)
SMEM = pl.BlockSpec(memory_space=pltpu.SMEM)
ANY = pl.BlockSpec(memory_space=pl.ANY)


def dot(a, b, dims=((1,), (0,))):
    return lax.dot_general(a, b, (dims, ((), ())), preferred_element_type=F32)


def split_kernel(x_ref, o_ref):
    for j in range(TRAINERS):
        o_ref[j] = x_ref[:, j * LOCAL : (j + 1) * LOCAL]


def split_targets(x):
    return pl.pallas_call(
        split_kernel,
        out_shape=jax.ShapeDtypeStruct((TRAINERS, SLOTS, LOCAL), BF16),
        in_specs=[VMEM],
        out_specs=VMEM,
        compiler_params=FULL,
    )(x)


Z = 8
Y = 4


PLACES = (((0, 0), (0, 4)), ((1, 0), (1, 8)), ((2, 0), (2, 4)), ((1, 12), (1, 4)))


def order_kernel(z_ref, *refs):
    for k, piece in enumerate(refs[:Z]):
        refs[Z][lax.rem(z_ref[0] + Z - k, Z)] = piece[...]


def in_order(z, pieces):
    return pl.pallas_call(
        order_kernel,
        out_shape=jax.ShapeDtypeStruct((Z, SLOTS, HALF), BF16),
        in_specs=[SMEM] + [VMEM] * Z,
        out_specs=VMEM,
        compiler_params=PARAMS,
    )(z, *pieces)


def logit_kernel(at_ref, *refs):
    pieces, refs = refs[:6], refs[6:]
    far_ref, table_ref, logits_ref, lse_ref, top_ref, *refs = refs
    tabs, w_ref, logit_buf, in_sems, out_sems = refs
    c, y = at_ref[0], at_ref[1]
    copies = [[], []]
    for side in range(2):
        rows = pl.ds(pl.multiple_of((c + side) % 2 * HALF, HALF), HALF)
        copies[side].append(
            pltpu.make_async_copy(far_ref.at[rows], w_ref.at[side], in_sems.at[16 + side])
        )
        for dy in range(Y):
            y_at = lax.rem(y + Y - dy, Y)
            for high in range(2):
                which, first = PLACES[dy][high]
                piece = pieces[side * 3 + which].at[pl.ds(first, Z // 2)]
                place = tabs.at[side, pl.ds(high * (Z // 2), Z // 2), y_at]
                sem = in_sems.at[side * 8 + dy * 2 + high]
                copies[side].append(pltpu.make_async_copy(piece, place, sem))
        for copy in copies[side]:
            copy.start()
    block = 2 * BLOCK
    step = block // (Y * SLOTS)

    def part(side, i):
        rows = tabs[side, pl.ds(i * step, step)].reshape(block, HALF)
        return dot(rows, w_ref[side])

    def store(i):
        rows = pl.ds(i * block, block)
        return pltpu.make_async_copy(logit_buf.at[rows], logits_ref.at[rows], out_sems.at[2 + i])

    stores = []
    for side in range(2):
        for copy in copies[side]:
            copy.wait()
        stores.append(
            pltpu.make_async_copy(tabs.at[side], table_ref.at[side], out_sems.at[side])
        )
        stores[-1].start()
        for i in range(ROWS // block):
            rows = pl.ds(i * block, block)
            if side == 0:
                logit_buf[rows, :] = part(side, i)
                continue
            logits = logit_buf[rows, :] + part(side, i)
            logit_buf[rows, :] = logits
            store(i).start()
            top = jnp.max(logits, axis=1, keepdims=True)
            lse = top + jnp.log(jnp.sum(jnp.exp(logits - top), axis=1, keepdims=True))
            for value, out in ((lse, lse_ref), (top, top_ref)):
                flat = jnp.broadcast_to(value, (block, 128)).T
                for j in range(block // 128):
                    row = flat[0:1, j * 128 : (j + 1) * 128]
                    out[pl.ds(i * (block // 128) + j, 1), :] = row

    for copy in stores + [store(i) for i in range(ROWS // block)]:
        copy.wait()


def logits_and_stats(at, pieces, weight):
    table, logits, lse, top = pl.pallas_call(
        logit_kernel,
        out_shape=(
            jax.ShapeDtypeStruct((2, Z, Y, SLOTS, HALF), BF16),
            jax.ShapeDtypeStruct((ROWS, LOCAL), F32),
            jax.ShapeDtypeStruct((8, 128), F32),
            jax.ShapeDtypeStruct((8, 128), F32),
        ),
        in_specs=[SMEM] + [ANY] * 7,
        out_specs=(ANY, ANY, VMEM, VMEM),
        scratch_shapes=[
            pltpu.VMEM((2, Z, Y, SLOTS, HALF), BF16),
            pltpu.VMEM((2, HALF, LOCAL), BF16),
            pltpu.VMEM((ROWS, LOCAL), F32),
            pltpu.SemaphoreType.DMA((18,)),
            pltpu.SemaphoreType.DMA((6,)),
        ],
        compiler_params=FULL,
    )(at, *pieces, weight)
    return table.reshape(2, ROWS, HALF), logits, lse, top


def merge(x):
    top = jnp.max(x, axis=0)
    return top + jnp.log(jnp.sum(jnp.exp(x - top[None]), axis=0))


def merge_kernel(copies, *refs):
    lse = merge(jnp.stack([ref[...] for ref in refs[:-1]]))
    if copies == 1:
        refs[-1][...] = lse
    for k in range(copies if copies > 1 else 0):
        refs[-1][k] = lse


def merge_stats(parts, copies=1):
    shape = (8, 128) if copies == 1 else (copies, 8, 128)
    return pl.pallas_call(
        functools.partial(merge_kernel, copies),
        out_shape=jax.ShapeDtypeStruct(shape, F32),
        in_specs=[VMEM] * len(parts),
        out_specs=VMEM,
        compiler_params=PARAMS if copies == 1 else FULL,
    )(*parts)


def column(row):
    return jnp.broadcast_to(row, (128, row.shape[1])).T


def select_kernel(
    top_ref, far_ref, targets_ref, gid_ref, live_ref, e_ref, mass_ref, cross_ref, *scratch
):
    logits_ref, p_ref, top_col, parts_ref, out_ref, sems = scratch
    fetch = pltpu.make_async_copy(far_ref, logits_ref, sems.at[0])
    fetch.start()
    fetch_targets = pltpu.make_async_copy(targets_ref, p_ref, sems.at[1])
    fetch_targets.start()
    for j in range(8):
        top_col[pl.ds(j * 128, 128), :] = column(top_ref[j : j + 1, :])
    fetch.wait()

    @pl.loop(0, ROWS // 128)
    def _(i):
        rows = pl.ds(pl.multiple_of(i * 128, 128), 128)
        for j in range(LOCAL // 128):
            p = jnp.exp(logits_ref[rows, pl.ds(j * 128, 128)] - top_col[rows, :])
            first = p.astype(BF16)
            p = p - first.astype(F32)
            second = p.astype(BF16)
            third = (p - second.astype(F32)).astype(BF16)
            parts_ref[rows, pl.ds(j * 128, 128)] = first
            parts_ref[rows, pl.ds(LOCAL + j * 128, 128)] = second
            parts_ref[rows, pl.ds(2 * LOCAL + j * 128, 128)] = third

    def store(i):
        rows = pl.ds(pl.multiple_of(i * BLOCK, BLOCK), BLOCK)
        return pltpu.make_async_copy(out_ref.at[rows], e_ref.at[rows], sems.at[2 + i])

    @pl.loop(0, ROWS // BLOCK)
    def _(i):
        rows = pl.ds(pl.multiple_of(i * BLOCK, BLOCK), BLOCK)
        gid = column(gid_ref[:, rows])
        lane = lax.broadcasted_iota(jnp.int32, (BLOCK, 128), 1).astype(F32)
        hot = jnp.concatenate(
            [
                jnp.where(gid == lane + float(128 * k), 1.0, 0.0).astype(BF16)
                for k in range(ROWS // 128)
            ],
            axis=1,
        )
        sel = dot(hot, parts_ref[...])
        out_ref[rows, :] = sel[:, 0:LOCAL] + sel[:, LOCAL : 2 * LOCAL] + sel[:, 2 * LOCAL :]
        store(i).start()

    fetch_targets.wait()

    def total(i, cross):
        rows = pl.ds(pl.multiple_of(i * BLOCK, BLOCK), BLOCK)
        row = lax.broadcasted_iota(jnp.int32, (BLOCK, ROWS), 0) + i * BLOCK
        hot = jnp.where(gid_ref[...] == row.astype(F32), live_ref[...], 0.0).astype(BF16)
        sums = dot(hot, p_ref[...])
        mass = jnp.broadcast_to(jnp.sum(sums, axis=1, keepdims=True), (BLOCK, 128)).T[0:1]
        for j in range(BLOCK // 128):
            mass_ref[pl.ds(i * (BLOCK // 128) + j, 1), :] = mass[:, j * 128 : (j + 1) * 128]
        return cross + jnp.sum(sums * logits_ref[rows, :])

    cross_ref[0, 0] = lax.fori_loop(0, ROWS // BLOCK, total, jnp.float32(0))
    for i in range(ROWS // BLOCK):
        store(i).wait()


def select_rows(top, logits, probs, gid, live):
    return pl.pallas_call(
        select_kernel,
        out_shape=(
            jax.ShapeDtypeStruct((ROWS, LOCAL), F32),
            jax.ShapeDtypeStruct((8, 128), F32),
            jax.ShapeDtypeStruct((1, 1), F32),
        ),
        in_specs=[VMEM, ANY, ANY, VMEM, VMEM],
        out_specs=(ANY, VMEM, SMEM),
        scratch_shapes=[
            pltpu.VMEM((ROWS, LOCAL), F32),
            pltpu.VMEM((ROWS, LOCAL), BF16),
            pltpu.VMEM((ROWS, 128), F32),
            pltpu.VMEM((ROWS, 3 * LOCAL), BF16),
            pltpu.VMEM((ROWS, LOCAL), F32),
            pltpu.SemaphoreType.DMA((6,)),
        ],
        compiler_params=FULL,
        cost_estimate=pl.CostEstimate(
            flops=4 * 2 * ROWS * ROWS * LOCAL, bytes_accessed=8 * 1024 * 1024, transcendentals=0
        ),
    )(top, logits, probs, gid, live)


def grad_kernel(
    x_ref, top_ref, mass_ref, cross_ref, far_ref, targets_ref, gid_ref, live_ref, *refs
):
    high_ref, both_ref, loss_ref, e_ref, p_ref, g_ref, sums_ref, sems = refs
    fetch = pltpu.make_async_copy(far_ref, e_ref, sems.at[0])
    fetch.start()
    fetch_targets = pltpu.make_async_copy(targets_ref, p_ref, sems.at[1])
    fetch_targets.start()
    lse = merge(x_ref[...])
    loss_ref[0, 0] = jnp.sum(lse * mass_ref[...]) - cross_ref[0, 0]
    share = jnp.exp(top_ref[...] - lse)
    scale = VOCAB / math.sqrt(ROWS)
    fetch.wait()
    fetch_targets.wait()
    lane = lax.broadcasted_iota(jnp.int32, (128, 128), 1).astype(F32)
    for i in range(ROWS // 128):
        rows = pl.ds(i * 128, 128)
        gid = column(gid_ref[:, rows])
        factor = column(live_ref[:, rows]) * scale
        found = jnp.zeros((128, 128), F32)
        for k in range(ROWS // 128):
            found += jnp.where(gid == lane + float(128 * k), share[k : k + 1], 0.0)
        found = jnp.sum(found, axis=1, keepdims=True)
        for j in range(LOCAL // 128):
            cols = pl.ds(j * 128, 128)
            diff = e_ref[rows, cols] * found - p_ref[rows, cols].astype(F32)
            g_ref[rows, cols] = (factor * diff).astype(BF16)

    def stores(i):
        rows = pl.ds(pl.multiple_of(i * BLOCK, BLOCK), BLOCK)
        high = sums_ref.at[rows, pl.ds(0, LOCAL)]
        yield pltpu.make_async_copy(high, high_ref.at[rows], sems.at[2 + i])
        yield pltpu.make_async_copy(sums_ref.at[rows], both_ref.at[rows], sems.at[6 + i])

    @pl.loop(0, ROWS // BLOCK)
    def _(i):
        rows = pl.ds(pl.multiple_of(i * BLOCK, BLOCK), BLOCK)
        row = lax.broadcasted_iota(jnp.int32, (BLOCK, ROWS), 0) + i * BLOCK
        hot = jnp.where(gid_ref[...] == row.astype(F32), 1.0, 0.0).astype(BF16)
        sums = dot(hot, g_ref[...])
        high = sums.astype(BF16)
        sums_ref[rows, 0:LOCAL] = high
        sums_ref[rows, LOCAL:] = (sums - high.astype(F32)).astype(BF16)
        for store in stores(i):
            store.start()

    for i in range(ROWS // BLOCK):
        for store in stores(i):
            store.wait()


def gradients(x, top, mass, cross, e, probs, gid, live):
    return pl.pallas_call(
        grad_kernel,
        out_shape=(
            jax.ShapeDtypeStruct((ROWS, LOCAL), BF16),
            jax.ShapeDtypeStruct((ROWS, 2 * LOCAL), BF16),
            jax.ShapeDtypeStruct((1, 1), F32),
        ),
        in_specs=[VMEM, VMEM, VMEM, SMEM, ANY, ANY, VMEM, VMEM],
        out_specs=(ANY, ANY, SMEM),
        scratch_shapes=[
            pltpu.VMEM((ROWS, LOCAL), F32),
            pltpu.VMEM((ROWS, LOCAL), BF16),
            pltpu.VMEM((ROWS, LOCAL), BF16),
            pltpu.VMEM((ROWS, 2 * LOCAL), BF16),
            pltpu.SemaphoreType.DMA((10,)),
        ],
        compiler_params=FULL,
    )(x, top, mass, cross, e, probs, gid, live)


TOP = 32700.0
ROWS2 = ROWS // 2
TAIL = 16
I16 = jnp.int16


def exponent(x):
    return jnp.ceil(jnp.log(jnp.maximum(x, 1e-30) / TOP) * (256.0 / math.log(2.0)))


def power(e):
    return jnp.exp2(e * (1.0 / 256.0))


def to16(x):
    return x.astype(jnp.int32).astype(I16)


def from16(x):
    return x.astype(jnp.int32).astype(F32)


def encode(val):
    e = exponent(jnp.max(jnp.abs(val), axis=1, keepdims=True))
    return to16(jnp.round(val * power(-e))), jnp.broadcast_to(e, (128, 128)).T[0:1]


def wide(row):
    return jnp.concatenate([row] + [jnp.zeros_like(row)] * (LOCAL // 128 - 1), axis=1)


def write_message(out_ref, block_of, loss, tail_ref):
    for j in range(ROWS2 // 128):
        code, e = encode(block_of(j))
        out_ref[pl.ds(j * 128, 128), :] = code
        tail_ref[pl.ds(j, 1), :] = e
    tail = [tail_ref[0 : ROWS2 // 128, :], loss, jnp.zeros((TAIL - ROWS2 // 128 - 1, 128), F32)]
    tail = jnp.concatenate(tail, axis=0)
    zeros = [jnp.zeros_like(tail)] * (LOCAL // 128 - 1)
    out_ref[pl.ds(ROWS2, TAIL), :] = to16(jnp.concatenate([tail] + zeros, axis=1))


def encode_loss(loss):
    e = exponent(jnp.abs(loss))
    whole = loss * power(-e)
    first = jnp.round(whole)
    rest = jnp.round((whole - first) * TOP)
    lane = lax.broadcasted_iota(jnp.int32, (1, 128), 1)
    return jnp.where(lane == 0, e, jnp.where(lane == 1, first, jnp.where(lane == 2, rest, 0.0)))


def decode_loss(code):
    return (code[:, 1:2] + code[:, 2:3] * (1.0 / TOP)) * power(code[:, 0:1])


def read_tail(ref, tail_ref):
    tail_ref[...] = from16(ref[pl.ds(ROWS2, TAIL), 0:128])


def tail_loss(tail_ref):
    return tail_ref[ROWS2 // 128 : ROWS2 // 128 + 1, :]


def read_message(ref, tail_ref, j):
    scale = power(column(tail_ref[pl.ds(j, 1), :]))
    rows = pl.ds(j * 128, 128)
    parts = [from16(ref[rows, k * 128 : (k + 1) * 128]) * scale for k in range(LOCAL // 128)]
    return jnp.concatenate(parts, axis=1)


TAIL_REF = pltpu.VMEM((TAIL, 128), F32)
MESSAGE = jax.ShapeDtypeStruct((ROWS2 + TAIL, LOCAL), I16)


def weight_kernel(at_ref, all_ref, keep_ref, give_ref, block_ref, sems):
    c, x = at_ref[0], at_ref[1]

    def fetch(n):
        source = all_ref.at[lax.rem(x + (2, 1, 3, 0)[n % 4], 4), lax.rem(c + n // 4, 2)]
        return pltpu.make_async_copy(source, block_ref.at[n], sems.at[n])

    for n in range(8):
        fetch(n).start()
    for n in range(8):
        fetch(n).wait()
        out = (keep_ref, give_ref)[n // 4]
        out[:, n % 4 * LOCAL : (n % 4 + 1) * LOCAL] = block_ref[n].T


def turn_weights(at, blocks):
    half = jax.ShapeDtypeStruct((LOCAL, 4 * LOCAL), BF16)
    return pl.pallas_call(
        weight_kernel,
        out_shape=(half, half),
        in_specs=[SMEM, ANY],
        out_specs=(VMEM, VMEM),
        scratch_shapes=[
            pltpu.VMEM((8, LOCAL, LOCAL), BF16),
            pltpu.SemaphoreType.DMA((8,)),
        ],
        compiler_params=FULL,
    )(at, blocks)


def fetch_pair(own_ref, other_ref, w_own, w_other, first, n, g_ref, w_ref, sems):
    cols = pl.ds(first * LOCAL, n * LOCAL)
    copies = [
        pltpu.make_async_copy(ref, g_ref.at[:, pl.ds(k * LOCAL, LOCAL)], sems.at[k])
        for k, ref in enumerate((own_ref, other_ref))
    ] + [
        pltpu.make_async_copy(ref.at[:, cols], w_ref.at[pl.ds(k * LOCAL, LOCAL)], sems.at[2 + k])
        for k, ref in enumerate((w_own, w_other))
    ]
    for copy in copies:
        copy.start()
    return copies


def far_kernel(
    loss_ref, more_ref, own_ref, other_ref, w_own, w_other, low, high, sum_ref, *refs
):
    g_ref, w_ref, val_ref, tail_ref, sems = refs
    copies = fetch_pair(own_ref, other_ref, w_own, w_other, 0, 1, g_ref, w_ref, sems)
    loss = encode_loss(jnp.full((1, 128), loss_ref[0, 0] + more_ref[0, 0], F32))
    sum_ref[...] = loss
    for copy in copies:
        copy.wait()
    for i, out in enumerate((low, high)):
        val_ref[...] = dot(g_ref[pl.ds(i * ROWS2, ROWS2), :], w_ref[...])
        write_message(out, lambda j: val_ref[pl.ds(j * 128, 128), :], loss, tail_ref)


def near_kernel(
    loss_ref, own_ref, other_ref, w_own, w_other, l1, h1, l3, h3, c0, g_ref, w_ref, val_ref, tail_ref, sems
):
    copies = fetch_pair(own_ref, other_ref, w_own, w_other, 1, 3, g_ref, w_ref, sems)
    for copy in copies:
        copy.wait()
    for i in range(2):
        rows = pl.ds(i * ROWS2, ROWS2)
        val_ref[...] = dot(g_ref[rows, :], w_ref[...])
        for k, out in enumerate(((l1, h1)[i], (l3, h3)[i])):
            cols = slice(k * LOCAL, (k + 1) * LOCAL)
            if out.dtype == F32:
                out[...] = val_ref[:, cols]
            else:
                write_message(
                    out, lambda j: val_ref[pl.ds(j * 128, 128), cols], loss_ref[...], tail_ref
                )
        c0[rows, :] = val_ref[:, 2 * LOCAL :]


def pair_scratch(n):
    return [
        pltpu.VMEM((ROWS, 2 * LOCAL), BF16),
        pltpu.VMEM((2 * LOCAL, n * LOCAL), BF16),
        pltpu.VMEM((ROWS2, n * LOCAL), F32),
        TAIL_REF,
        pltpu.SemaphoreType.DMA((4,)),
    ]


def far_terms(loss, more, own, other, w_own, w_other):
    return pl.pallas_call(
        far_kernel,
        out_shape=(MESSAGE, MESSAGE, jax.ShapeDtypeStruct((1, 128), F32)),
        in_specs=[SMEM, SMEM] + [ANY] * 4,
        out_specs=(VMEM,) * 3,
        scratch_shapes=pair_scratch(1),
        compiler_params=PARAMS,
    )(loss, more, own, other, w_own, w_other)


def near_terms(loss, own, other, w_own, w_other):
    part = jax.ShapeDtypeStruct((ROWS2, LOCAL), F32)
    return pl.pallas_call(
        near_kernel,
        out_shape=(part, MESSAGE, MESSAGE, part, jax.ShapeDtypeStruct((ROWS, LOCAL), F32)),
        in_specs=[VMEM] + [ANY] * 4,
        out_specs=(VMEM,) * 5,
        scratch_shapes=pair_scratch(3),
        compiler_params=PARAMS,
    )(loss, own, other, w_own, w_other)


def relay_kernel(own_ref, got_ref, out_ref, got_tail, tail_ref):
    read_tail(got_ref, got_tail)

    def block(j):
        rows = pl.ds(j * 128, 128)
        return own_ref[rows, :] + read_message(got_ref, got_tail, j)

    write_message(out_ref, block, tail_loss(got_tail), tail_ref)


def relay(own, got):
    return pl.pallas_call(
        relay_kernel,
        out_shape=MESSAGE,
        in_specs=[VMEM] * 2,
        out_specs=VMEM,
        scratch_shapes=[TAIL_REF] * 2,
        compiler_params=PARAMS,
    )(own, got)


PACKED = 3 * SLOTS + TAIL


def pack_kernel(loss_ref, own_ref, low_r, low_l, high_r, high_l, o_ref, *tails):
    messages = (low_r, low_l, high_r, high_l)
    for ref, tail_ref in zip(messages, tails):
        read_tail(ref, tail_ref)
    codes = [loss_ref[...]] + [tail_loss(tail_ref) for tail_ref in tails[:3]]
    loss = decode_loss(jnp.concatenate(codes, axis=0))
    loss = (loss[0:1] + loss[1:2]) + (loss[2:3] + loss[3:4])
    loss = encode_loss(jnp.broadcast_to(loss, (1, 128)))
    pad = jnp.zeros((TAIL - 2, 128), F32)
    for i in range(2):
        for j in range(ROWS2 // 128):
            at = i * (ROWS2 // 128) + j
            val = own_ref[pl.ds(at * 128, 128), :]
            got = [read_message(messages[n], tails[n], j) for n in (2 * i, 2 * i + 1)]
            code, e = encode(val + (got[0] + got[1]))
            tail = to16(jnp.concatenate([e, loss, pad], axis=0))
            for n in range(128 // SLOTS):
                for k in range(3):
                    o_ref[at * 4 + n, k * SLOTS : (k + 1) * SLOTS, :] = code[
                        n * SLOTS : (n + 1) * SLOTS, k * 128 : (k + 1) * 128
                    ]
                o_ref[at * 4 + n, 3 * SLOTS :, :] = tail


def pack(loss, own, low_r, low_l, high_r, high_l):
    return pl.pallas_call(
        pack_kernel,
        out_shape=jax.ShapeDtypeStruct((TRAINERS, PACKED, 128), I16),
        in_specs=[VMEM] * 6,
        out_specs=VMEM,
        scratch_shapes=[TAIL_REF] * 4,
        compiler_params=PARAMS,
    )(loss, own, low_r, low_l, high_r, high_l)


def finish_kernel(at_ref, x_ref, grad_ref, loss_ref, e_ref):
    tail = from16(x_ref[:, 3 * SLOTS :, :])
    e = tail[:, 0, :]
    e_ref[...] = jnp.concatenate([e, jnp.zeros((128 - TRAINERS, 128), F32)], axis=0).T
    scale = power(e_ref[pl.ds(pl.multiple_of(at_ref[0] * SLOTS, SLOTS), SLOTS), :])
    total = [jnp.zeros((SLOTS, 128), F32)] * 3
    for s in range(TRAINERS):
        for k in range(3):
            total[k] += from16(x_ref[s, k * SLOTS : (k + 1) * SLOTS, :]) * scale[:, s : s + 1]
    for k in range(3):
        grad_ref[:, k * 128 : (k + 1) * 128] = total[k]
    loss_ref[0, 0] = jnp.sum(decode_loss(tail[:, 1, :]))


def finish(at, x):
    return pl.pallas_call(
        finish_kernel,
        out_shape=(
            jax.ShapeDtypeStruct((SLOTS, LOCAL), F32),
            jax.ShapeDtypeStruct((1, 1), F32),
        ),
        in_specs=[SMEM, VMEM],
        out_specs=(VMEM, SMEM),
        scratch_shapes=[pltpu.VMEM((128, 128), F32)],
        compiler_params=PARAMS,
    )(at, x)


HEAD_BLOCK = 256
HEAD_STEPS = HALF // HEAD_BLOCK


def head_kernel(c_ref, table_ref, sums_ref, o_ref):
    both = dot(table_ref[0], sums_ref[...], ((0,), (0,)))
    both = both[:, 0:LOCAL] + both[:, LOCAL:]
    for j in range(LOCAL // 128):
        o_ref[pl.ds(j, HEAD_BLOCK, stride=LOCAL // 128), :] = both[:, j * 128 : (j + 1) * 128]


def head_gradient(c, table, sums):
    def place(i, c):
        side = lax.rem(c[0] + i // HEAD_STEPS, 2)
        return (side * HEAD_STEPS + i % HEAD_STEPS, 0)

    return pl.pallas_call(
        head_kernel,
        grid_spec=pltpu.PrefetchScalarGridSpec(
            num_scalar_prefetch=1,
            grid=(2 * HEAD_STEPS,),
            in_specs=[
                pl.BlockSpec(
                    (1, ROWS, HEAD_BLOCK), lambda i, c: (i // HEAD_STEPS, 0, i % HEAD_STEPS)
                ),
                pl.BlockSpec((ROWS, 2 * LOCAL), lambda i, c: (0, 0)),
            ],
            out_specs=pl.BlockSpec((HEAD_BLOCK * LOCAL // 128, 128), place),
        ),
        out_shape=jax.ShapeDtypeStruct((D * LOCAL // 128, 128), F32),
        compiler_params=PARAMS,
        cost_estimate=pl.CostEstimate(
            flops=4 * ROWS * D * LOCAL, bytes_accessed=12 * 1024 * 1024, transcendentals=0
        ),
    )(c, table, sums)


PAIR = [(i, i ^ 1) for i in range(SHARDS)]


def along_x(k):
    return [(i, (i + 2 * k) % SHARDS) for i in range(SHARDS)]


RIGHT, LEFT = along_x(1), along_x(-1)


def along_z(k):
    return [(i, (i // Y + k) % Z * Y + i % Y) for i in range(TRAINERS)]


def along_y(k):
    return [(i, i // Y * Y + (i + k) % Y) for i in range(TRAINERS)]


def on_device(hidden_table, head_weight, targets, counts, dest, token):
    me = lax.axis_index("vocab")
    trainer = lax.axis_index("trainer")
    c = lax.rem(me, 2)
    x = me // 2
    y = lax.rem(trainer, Y)
    c1 = c.reshape(1).astype(jnp.int32)
    at_cx = jnp.stack([c, x]).astype(jnp.int32)
    at_cy = jnp.stack([c, y]).astype(jnp.int32)
    z1 = (trainer // Y).reshape(1).astype(jnp.int32)
    weight = head_weight[:, 0, :]

    half = lax.dynamic_slice(hidden_table, (0, c * HALF), (SLOTS, HALF))
    near = [half] + [lax.ppermute(half, "trainer", along_z(k)) for k in (1, 2, -2, -1)]
    near[3:3] = [
        lax.ppermute(near[2], "trainer", along_z(1)),
        lax.ppermute(near[2], "trainer", along_z(2)),
        lax.ppermute(near[3], "trainer", along_z(-1)),
    ]

    gid = dest * SLOTS + token
    index = jnp.arange(ROWS, dtype=jnp.int32)
    live = (index % SLOTS < jnp.repeat(counts, SLOTS)).astype(F32).reshape(1, ROWS)
    gid = gid.astype(F32).reshape(1, ROWS)

    z1, gid, live = lax.optimization_barrier((z1, gid, live))
    plane = in_order(z1, near)
    low0, high0 = plane[: Z // 2], plane[Z // 2 :]
    low1 = lax.ppermute(low0, "trainer", along_y(1))
    high3 = lax.ppermute(high0, "trainer", along_y(-1))
    high1 = lax.ppermute(high0, "trainer", along_y(1))
    low3 = lax.ppermute(low0, "trainer", along_y(-1))
    low2 = lax.ppermute(low1, "trainer", along_y(1))
    high2 = lax.ppermute(high3, "trainer", along_y(-1))
    middle = jnp.concatenate([low1, high3, high1, low3])
    at_cx, targets, _ = lax.optimization_barrier((at_cx, targets, middle))
    split = split_targets(targets[:, 0, :])
    w_own, w_give = turn_weights(at_cx, weight.reshape(4, 2, LOCAL, LOCAL))
    low2, split, w_own, w_give = lax.optimization_barrier((low2, split, w_own, w_give))
    pieces = [plane, middle, jnp.concatenate([low2, high2])]
    pieces += [lax.ppermute(p, "vocab", PAIR) for p in pieces]
    split, _ = lax.optimization_barrier((split, (pieces[2], pieces[3], pieces[4])))
    probs = lax.all_to_all(split, "trainer", split_axis=0, concat_axis=0, tiled=True)

    table, logits, stats, top = logits_and_stats(at_cy, pieces, weight)
    stats = merge_stats([stats, lax.ppermute(stats, "vocab", PAIR)])
    stats = [stats] + [lax.ppermute(stats, "vocab", along_x(k)) for k in (1, 2, 3)]
    stats = merge_stats(stats, TRAINERS)
    w_give, _ = lax.optimization_barrier((w_give, stats))
    w_other = lax.ppermute(w_give, "vocab", PAIR)
    stats, probs = lax.optimization_barrier((stats, probs.reshape(ROWS, LOCAL)))
    stats = lax.all_to_all(stats, "trainer", split_axis=0, concat_axis=0, tiled=True)

    e, mass, cross = select_rows(top, logits, probs, gid, live)
    high, sums, loss = gradients(stats, top, mass, cross, e, probs, gid, live)

    more = lax.ppermute(loss, "vocab", PAIR)
    far = lax.ppermute(high, "vocab", PAIR)
    l2, h2, loss = far_terms(loss, more, high, far, w_own, w_other)
    low_r = lax.ppermute(l2, "vocab", RIGHT)
    high_l = lax.ppermute(h2, "vocab", LEFT)
    l1, h1, l3, h3, t0 = near_terms(loss, high, far, w_own, w_other)
    high_r = lax.ppermute(h1, "vocab", RIGHT)
    low_l = lax.ppermute(l3, "vocab", LEFT)
    low_r = lax.ppermute(relay(l1, low_r), "vocab", RIGHT)
    high_l = lax.ppermute(relay(h3, high_l), "vocab", LEFT)
    head = head_gradient(c1, table, sums)
    packed = pack(loss, t0, low_r, low_l, high_r, high_l)
    packed = lax.all_to_all(packed, "trainer", split_axis=0, concat_axis=0, tiled=True)
    table_grad, loss = finish(lax.rem(trainer, 4).reshape(1).astype(jnp.int32), packed)
    mean_loss = loss[0, 0] / jnp.sum(counts).astype(F32)
    return head.reshape(D, 1, LOCAL), table_grad, mean_loss


def solution(mesh):
    return jax.shard_map(
        on_device,
        mesh=mesh,
        in_specs=(
            P("trainer", None),
            P(None, "vocab", "trainer"),
            P("trainer", "vocab", None),
            P(),
            P(),
            P(),
        ),
        out_specs=(P(None, "vocab", "trainer"), P("trainer", "vocab"), P()),
        check_vma=False,
    )
```

```python
import functools
import math

import jax
import jax.numpy as jnp
from jax import lax
from jax.experimental import pallas as pl
from jax.experimental.pallas import tpu as pltpu
from jax.sharding import PartitionSpec as P

D = 3072
VOCAB = 98304
ROWS = 1024
TRAINERS = 32
SLOTS = 32
SHARDS = 8
LOCAL = VOCAB // (TRAINERS * SHARDS)
HALF = D // 2
BLOCK = 256
BF16 = jnp.bfloat16
F32 = jnp.float32
PARAMS = pltpu.CompilerParams(vmem_limit_bytes=24 * 1024 * 1024)
FULL = pltpu.CompilerParams(vmem_limit_bytes=60 * 1024 * 1024)
VMEM = pl.BlockSpec(memory_space=pltpu.VMEM)
SMEM = pl.BlockSpec(memory_space=pltpu.SMEM)
ANY = pl.BlockSpec(memory_space=pl.ANY)


def dot(a, b, dims=((1,), (0,))):
    return lax.dot_general(a, b, (dims, ((), ())), preferred_element_type=F32)


def split_kernel(x_ref, o_ref):
    for j in range(TRAINERS):
        o_ref[j] = x_ref[:, j * LOCAL : (j + 1) * LOCAL]


def split_targets(x):
    return pl.pallas_call(
        split_kernel,
        out_shape=jax.ShapeDtypeStruct((TRAINERS, SLOTS, LOCAL), BF16),
        in_specs=[VMEM],
        out_specs=VMEM,
        compiler_params=FULL,
    )(x)


Z = 8
Y = 4


PLACES = (((0, 0), (0, 4)), ((1, 0), (1, 8)), ((2, 0), (2, 4)), ((1, 12), (1, 4)))


def order_kernel(z_ref, *refs):
    for k, piece in enumerate(refs[:Z]):
        refs[Z][lax.rem(z_ref[0] + Z - k, Z)] = piece[...]


def in_order(z, pieces):
    return pl.pallas_call(
        order_kernel,
        out_shape=jax.ShapeDtypeStruct((Z, SLOTS, HALF), BF16),
        in_specs=[SMEM] + [VMEM] * Z,
        out_specs=VMEM,
        compiler_params=PARAMS,
    )(z, *pieces)


def logit_kernel(at_ref, *refs):
    pieces, refs = refs[:6], refs[6:]
    far_ref, table_ref, logits_ref, lse_ref, top_ref, *refs = refs
    tabs, w_ref, logit_buf, in_sems, out_sems = refs
    c, y = at_ref[0], at_ref[1]
    copies = [[], []]
    for side in range(2):
        rows = pl.ds(pl.multiple_of((c + side) % 2 * HALF, HALF), HALF)
        copies[side].append(
            pltpu.make_async_copy(far_ref.at[rows], w_ref.at[side], in_sems.at[16 + side])
        )
        for dy in range(Y):
            y_at = lax.rem(y + Y - dy, Y)
            for high in range(2):
                which, first = PLACES[dy][high]
                piece = pieces[side * 3 + which].at[pl.ds(first, Z // 2)]
                place = tabs.at[side, pl.ds(high * (Z // 2), Z // 2), y_at]
                sem = in_sems.at[side * 8 + dy * 2 + high]
                copies[side].append(pltpu.make_async_copy(piece, place, sem))
        for copy in copies[side]:
            copy.start()
    block = 2 * BLOCK
    step = block // (Y * SLOTS)

    def part(side, i):
        rows = tabs[side, pl.ds(i * step, step)].reshape(block, HALF)
        return dot(rows, w_ref[side])

    def store(i):
        rows = pl.ds(i * block, block)
        return pltpu.make_async_copy(logit_buf.at[rows], logits_ref.at[rows], out_sems.at[2 + i])

    stores = []
    for side in range(2):
        for copy in copies[side]:
            copy.wait()
        stores.append(
            pltpu.make_async_copy(tabs.at[side], table_ref.at[side], out_sems.at[side])
        )
        stores[-1].start()
        for i in range(ROWS // block):
            rows = pl.ds(i * block, block)
            if side == 0:
                logit_buf[rows, :] = part(side, i)
                continue
            logits = logit_buf[rows, :] + part(side, i)
            logit_buf[rows, :] = logits
            store(i).start()
            top = jnp.max(logits, axis=1, keepdims=True)
            lse = top + jnp.log(jnp.sum(jnp.exp(logits - top), axis=1, keepdims=True))
            for value, out in ((lse, lse_ref), (top, top_ref)):
                flat = jnp.broadcast_to(value, (block, 128)).T
                for j in range(block // 128):
                    row = flat[0:1, j * 128 : (j + 1) * 128]
                    out[pl.ds(i * (block // 128) + j, 1), :] = row

    for copy in stores + [store(i) for i in range(ROWS // block)]:
        copy.wait()


def logits_and_stats(at, pieces, weight):
    table, logits, lse, top = pl.pallas_call(
        logit_kernel,
        out_shape=(
            jax.ShapeDtypeStruct((2, Z, Y, SLOTS, HALF), BF16),
            jax.ShapeDtypeStruct((ROWS, LOCAL), F32),
            jax.ShapeDtypeStruct((8, 128), F32),
            jax.ShapeDtypeStruct((8, 128), F32),
        ),
        in_specs=[SMEM] + [ANY] * 7,
        out_specs=(ANY, ANY, VMEM, VMEM),
        scratch_shapes=[
            pltpu.VMEM((2, Z, Y, SLOTS, HALF), BF16),
            pltpu.VMEM((2, HALF, LOCAL), BF16),
            pltpu.VMEM((ROWS, LOCAL), F32),
            pltpu.SemaphoreType.DMA((18,)),
            pltpu.SemaphoreType.DMA((6,)),
        ],
        compiler_params=FULL,
    )(at, *pieces, weight)
    return table.reshape(2, ROWS, HALF), logits, lse, top


def merge(x):
    top = jnp.max(x, axis=0)
    return top + jnp.log(jnp.sum(jnp.exp(x - top[None]), axis=0))


def merge_kernel(copies, *refs):
    lse = merge(jnp.stack([ref[...] for ref in refs[:-1]]))
    if copies == 1:
        refs[-1][...] = lse
    for k in range(copies if copies > 1 else 0):
        refs[-1][k] = lse


def merge_stats(parts, copies=1):
    shape = (8, 128) if copies == 1 else (copies, 8, 128)
    return pl.pallas_call(
        functools.partial(merge_kernel, copies),
        out_shape=jax.ShapeDtypeStruct(shape, F32),
        in_specs=[VMEM] * len(parts),
        out_specs=VMEM,
        compiler_params=PARAMS if copies == 1 else FULL,
    )(*parts)


def column(row):
    return jnp.broadcast_to(row, (128, row.shape[1])).T


def select_kernel(
    top_ref, far_ref, targets_ref, gid_ref, live_ref, e_ref, mass_ref, cross_ref, *scratch
):
    logits_ref, p_ref, top_col, parts_ref, out_ref, sems = scratch
    fetch = pltpu.make_async_copy(far_ref, logits_ref, sems.at[0])
    fetch.start()
    fetch_targets = pltpu.make_async_copy(targets_ref, p_ref, sems.at[1])
    fetch_targets.start()
    for j in range(8):
        top_col[pl.ds(j * 128, 128), :] = column(top_ref[j : j + 1, :])
    fetch.wait()

    @pl.loop(0, ROWS // 128)
    def _(i):
        rows = pl.ds(pl.multiple_of(i * 128, 128), 128)
        for j in range(LOCAL // 128):
            p = jnp.exp(logits_ref[rows, pl.ds(j * 128, 128)] - top_col[rows, :])
            first = p.astype(BF16)
            p = p - first.astype(F32)
            second = p.astype(BF16)
            third = (p - second.astype(F32)).astype(BF16)
            parts_ref[rows, pl.ds(j * 128, 128)] = first
            parts_ref[rows, pl.ds(LOCAL + j * 128, 128)] = second
            parts_ref[rows, pl.ds(2 * LOCAL + j * 128, 128)] = third

    def store(i):
        rows = pl.ds(pl.multiple_of(i * BLOCK, BLOCK), BLOCK)
        return pltpu.make_async_copy(out_ref.at[rows], e_ref.at[rows], sems.at[2 + i])

    @pl.loop(0, ROWS // BLOCK)
    def _(i):
        rows = pl.ds(pl.multiple_of(i * BLOCK, BLOCK), BLOCK)
        gid = column(gid_ref[:, rows])
        lane = lax.broadcasted_iota(jnp.int32, (BLOCK, 128), 1).astype(F32)
        hot = jnp.concatenate(
            [
                jnp.where(gid == lane + float(128 * k), 1.0, 0.0).astype(BF16)
                for k in range(ROWS // 128)
            ],
            axis=1,
        )
        sel = dot(hot, parts_ref[...])
        out_ref[rows, :] = sel[:, 0:LOCAL] + sel[:, LOCAL : 2 * LOCAL] + sel[:, 2 * LOCAL :]
        store(i).start()

    fetch_targets.wait()

    def total(i, cross):
        rows = pl.ds(pl.multiple_of(i * BLOCK, BLOCK), BLOCK)
        row = lax.broadcasted_iota(jnp.int32, (BLOCK, ROWS), 0) + i * BLOCK
        hot = jnp.where(gid_ref[...] == row.astype(F32), live_ref[...], 0.0).astype(BF16)
        sums = dot(hot, p_ref[...])
        mass = jnp.broadcast_to(jnp.sum(sums, axis=1, keepdims=True), (BLOCK, 128)).T[0:1]
        for j in range(BLOCK // 128):
            mass_ref[pl.ds(i * (BLOCK // 128) + j, 1), :] = mass[:, j * 128 : (j + 1) * 128]
        return cross + jnp.sum(sums * logits_ref[rows, :])

    cross_ref[0, 0] = lax.fori_loop(0, ROWS // BLOCK, total, jnp.float32(0))
    for i in range(ROWS // BLOCK):
        store(i).wait()


def select_rows(top, logits, probs, gid, live):
    return pl.pallas_call(
        select_kernel,
        out_shape=(
            jax.ShapeDtypeStruct((ROWS, LOCAL), F32),
            jax.ShapeDtypeStruct((8, 128), F32),
            jax.ShapeDtypeStruct((1, 1), F32),
        ),
        in_specs=[VMEM, ANY, ANY, VMEM, VMEM],
        out_specs=(ANY, VMEM, SMEM),
        scratch_shapes=[
            pltpu.VMEM((ROWS, LOCAL), F32),
            pltpu.VMEM((ROWS, LOCAL), BF16),
            pltpu.VMEM((ROWS, 128), F32),
            pltpu.VMEM((ROWS, 3 * LOCAL), BF16),
            pltpu.VMEM((ROWS, LOCAL), F32),
            pltpu.SemaphoreType.DMA((6,)),
        ],
        compiler_params=FULL,
        cost_estimate=pl.CostEstimate(
            flops=4 * 2 * ROWS * ROWS * LOCAL, bytes_accessed=8 * 1024 * 1024, transcendentals=0
        ),
    )(top, logits, probs, gid, live)


def grad_kernel(
    x_ref, top_ref, mass_ref, cross_ref, far_ref, targets_ref, gid_ref, live_ref, *refs
):
    high_ref, both_ref, loss_ref, e_ref, p_ref, g_ref, sums_ref, sems = refs
    fetch = pltpu.make_async_copy(far_ref, e_ref, sems.at[0])
    fetch.start()
    fetch_targets = pltpu.make_async_copy(targets_ref, p_ref, sems.at[1])
    fetch_targets.start()
    lse = merge(x_ref[...])
    loss_ref[0, 0] = jnp.sum(lse * mass_ref[...]) - cross_ref[0, 0]
    share = jnp.exp(top_ref[...] - lse)
    scale = VOCAB / math.sqrt(ROWS)
    fetch.wait()
    fetch_targets.wait()
    lane = lax.broadcasted_iota(jnp.int32, (128, 128), 1).astype(F32)
    for i in range(ROWS // 128):
        rows = pl.ds(i * 128, 128)
        gid = column(gid_ref[:, rows])
        factor = column(live_ref[:, rows]) * scale
        found = jnp.zeros((128, 128), F32)
        for k in range(ROWS // 128):
            found += jnp.where(gid == lane + float(128 * k), share[k : k + 1], 0.0)
        found = jnp.sum(found, axis=1, keepdims=True)
        for j in range(LOCAL // 128):
            cols = pl.ds(j * 128, 128)
            diff = e_ref[rows, cols] * found - p_ref[rows, cols].astype(F32)
            g_ref[rows, cols] = (factor * diff).astype(BF16)

    def stores(i):
        rows = pl.ds(pl.multiple_of(i * BLOCK, BLOCK), BLOCK)
        high = sums_ref.at[rows, pl.ds(0, LOCAL)]
        yield pltpu.make_async_copy(high, high_ref.at[rows], sems.at[2 + i])
        yield pltpu.make_async_copy(sums_ref.at[rows], both_ref.at[rows], sems.at[6 + i])

    @pl.loop(0, ROWS // BLOCK)
    def _(i):
        rows = pl.ds(pl.multiple_of(i * BLOCK, BLOCK), BLOCK)
        row = lax.broadcasted_iota(jnp.int32, (BLOCK, ROWS), 0) + i * BLOCK
        hot = jnp.where(gid_ref[...] == row.astype(F32), 1.0, 0.0).astype(BF16)
        sums = dot(hot, g_ref[...])
        high = sums.astype(BF16)
        sums_ref[rows, 0:LOCAL] = high
        sums_ref[rows, LOCAL:] = (sums - high.astype(F32)).astype(BF16)
        for store in stores(i):
            store.start()

    for i in range(ROWS // BLOCK):
        for store in stores(i):
            store.wait()


def gradients(x, top, mass, cross, e, probs, gid, live):
    return pl.pallas_call(
        grad_kernel,
        out_shape=(
            jax.ShapeDtypeStruct((ROWS, LOCAL), BF16),
            jax.ShapeDtypeStruct((ROWS, 2 * LOCAL), BF16),
            jax.ShapeDtypeStruct((1, 1), F32),
        ),
        in_specs=[VMEM, VMEM, VMEM, SMEM, ANY, ANY, VMEM, VMEM],
        out_specs=(ANY, ANY, SMEM),
        scratch_shapes=[
            pltpu.VMEM((ROWS, LOCAL), F32),
            pltpu.VMEM((ROWS, LOCAL), BF16),
            pltpu.VMEM((ROWS, LOCAL), BF16),
            pltpu.VMEM((ROWS, 2 * LOCAL), BF16),
            pltpu.SemaphoreType.DMA((10,)),
        ],
        compiler_params=FULL,
    )(x, top, mass, cross, e, probs, gid, live)


TOP = 32700.0
ROWS2 = ROWS // 2
TAIL = 16
I16 = jnp.int16


def exponent(x):
    return jnp.ceil(jnp.log(jnp.maximum(x, 1e-30) / TOP) * (256.0 / math.log(2.0)))


def power(e):
    return jnp.exp2(e * (1.0 / 256.0))


def to16(x):
    return x.astype(jnp.int32).astype(I16)


def from16(x):
    return x.astype(jnp.int32).astype(F32)


def encode(val):
    e = exponent(jnp.max(jnp.abs(val), axis=1, keepdims=True))
    return to16(jnp.round(val * power(-e))), jnp.broadcast_to(e, (128, 128)).T[0:1]


def wide(row):
    return jnp.concatenate([row] + [jnp.zeros_like(row)] * (LOCAL // 128 - 1), axis=1)


def write_message(out_ref, block_of, loss, tail_ref):
    for j in range(ROWS2 // 128):
        code, e = encode(block_of(j))
        out_ref[pl.ds(j * 128, 128), :] = code
        tail_ref[pl.ds(j, 1), :] = e
    tail = [tail_ref[0 : ROWS2 // 128, :], loss, jnp.zeros((TAIL - ROWS2 // 128 - 1, 128), F32)]
    tail = jnp.concatenate(tail, axis=0)
    zeros = [jnp.zeros_like(tail)] * (LOCAL // 128 - 1)
    out_ref[pl.ds(ROWS2, TAIL), :] = to16(jnp.concatenate([tail] + zeros, axis=1))


def encode_loss(loss):
    e = exponent(jnp.abs(loss))
    whole = loss * power(-e)
    first = jnp.round(whole)
    rest = jnp.round((whole - first) * TOP)
    lane = lax.broadcasted_iota(jnp.int32, (1, 128), 1)
    return jnp.where(lane == 0, e, jnp.where(lane == 1, first, jnp.where(lane == 2, rest, 0.0)))


def decode_loss(code):
    return (code[:, 1:2] + code[:, 2:3] * (1.0 / TOP)) * power(code[:, 0:1])


def read_tail(ref, tail_ref):
    tail_ref[...] = from16(ref[pl.ds(ROWS2, TAIL), 0:128])


def tail_loss(tail_ref):
    return tail_ref[ROWS2 // 128 : ROWS2 // 128 + 1, :]


def read_message(ref, tail_ref, j):
    scale = power(column(tail_ref[pl.ds(j, 1), :]))
    rows = pl.ds(j * 128, 128)
    parts = [from16(ref[rows, k * 128 : (k + 1) * 128]) * scale for k in range(LOCAL // 128)]
    return jnp.concatenate(parts, axis=1)


TAIL_REF = pltpu.VMEM((TAIL, 128), F32)
MESSAGE = jax.ShapeDtypeStruct((ROWS2 + TAIL, LOCAL), I16)


def weight_kernel(at_ref, all_ref, keep_ref, give_ref, block_ref, sems):
    c, x = at_ref[0], at_ref[1]

    def fetch(n):
        source = all_ref.at[lax.rem(x + (2, 1, 3, 0)[n % 4], 4), lax.rem(c + n // 4, 2)]
        return pltpu.make_async_copy(source, block_ref.at[n], sems.at[n])

    for n in range(8):
        fetch(n).start()
    for n in range(8):
        fetch(n).wait()
        out = (keep_ref, give_ref)[n // 4]
        out[:, n % 4 * LOCAL : (n % 4 + 1) * LOCAL] = block_ref[n].T


def turn_weights(at, blocks):
    half = jax.ShapeDtypeStruct((LOCAL, 4 * LOCAL), BF16)
    return pl.pallas_call(
        weight_kernel,
        out_shape=(half, half),
        in_specs=[SMEM, ANY],
        out_specs=(VMEM, VMEM),
        scratch_shapes=[
            pltpu.VMEM((8, LOCAL, LOCAL), BF16),
            pltpu.SemaphoreType.DMA((8,)),
        ],
        compiler_params=FULL,
    )(at, blocks)


def fetch_pair(own_ref, other_ref, w_own, w_other, first, n, g_ref, w_ref, sems):
    cols = pl.ds(first * LOCAL, n * LOCAL)
    copies = [
        pltpu.make_async_copy(ref, g_ref.at[:, pl.ds(k * LOCAL, LOCAL)], sems.at[k])
        for k, ref in enumerate((own_ref, other_ref))
    ] + [
        pltpu.make_async_copy(ref.at[:, cols], w_ref.at[pl.ds(k * LOCAL, LOCAL)], sems.at[2 + k])
        for k, ref in enumerate((w_own, w_other))
    ]
    for copy in copies:
        copy.start()
    return copies


def far_kernel(
    loss_ref, more_ref, own_ref, other_ref, w_own, w_other, low, high, sum_ref, *refs
):
    g_ref, w_ref, val_ref, tail_ref, sems = refs
    copies = fetch_pair(own_ref, other_ref, w_own, w_other, 0, 1, g_ref, w_ref, sems)
    loss = encode_loss(jnp.full((1, 128), loss_ref[0, 0] + more_ref[0, 0], F32))
    sum_ref[...] = loss
    for copy in copies:
        copy.wait()
    for i, out in enumerate((low, high)):
        val_ref[...] = dot(g_ref[pl.ds(i * ROWS2, ROWS2), :], w_ref[...])
        write_message(out, lambda j: val_ref[pl.ds(j * 128, 128), :], loss, tail_ref)


def near_kernel(
    loss_ref, own_ref, other_ref, w_own, w_other, l1, h1, l3, h3, c0, g_ref, w_ref, val_ref, tail_ref, sems
):
    copies = fetch_pair(own_ref, other_ref, w_own, w_other, 1, 3, g_ref, w_ref, sems)
    for copy in copies:
        copy.wait()
    for i in range(2):
        rows = pl.ds(i * ROWS2, ROWS2)
        val_ref[...] = dot(g_ref[rows, :], w_ref[...])
        for k, out in enumerate(((l1, h1)[i], (l3, h3)[i])):
            cols = slice(k * LOCAL, (k + 1) * LOCAL)
            if out.dtype == F32:
                out[...] = val_ref[:, cols]
            else:
                write_message(
                    out, lambda j: val_ref[pl.ds(j * 128, 128), cols], loss_ref[...], tail_ref
                )
        c0[rows, :] = val_ref[:, 2 * LOCAL :]


def pair_scratch(n):
    return [
        pltpu.VMEM((ROWS, 2 * LOCAL), BF16),
        pltpu.VMEM((2 * LOCAL, n * LOCAL), BF16),
        pltpu.VMEM((ROWS2, n * LOCAL), F32),
        TAIL_REF,
        pltpu.SemaphoreType.DMA((4,)),
    ]


def far_terms(loss, more, own, other, w_own, w_other):
    return pl.pallas_call(
        far_kernel,
        out_shape=(MESSAGE, MESSAGE, jax.ShapeDtypeStruct((1, 128), F32)),
        in_specs=[SMEM, SMEM] + [ANY] * 4,
        out_specs=(VMEM,) * 3,
        scratch_shapes=pair_scratch(1),
        compiler_params=PARAMS,
    )(loss, more, own, other, w_own, w_other)


def near_terms(loss, own, other, w_own, w_other):
    part = jax.ShapeDtypeStruct((ROWS2, LOCAL), F32)
    return pl.pallas_call(
        near_kernel,
        out_shape=(part, MESSAGE, MESSAGE, part, jax.ShapeDtypeStruct((ROWS, LOCAL), F32)),
        in_specs=[VMEM] + [ANY] * 4,
        out_specs=(VMEM,) * 5,
        scratch_shapes=pair_scratch(3),
        compiler_params=PARAMS,
    )(loss, own, other, w_own, w_other)


def relay_kernel(own_ref, got_ref, out_ref, got_tail, tail_ref):
    read_tail(got_ref, got_tail)

    def block(j):
        rows = pl.ds(j * 128, 128)
        return own_ref[rows, :] + read_message(got_ref, got_tail, j)

    write_message(out_ref, block, tail_loss(got_tail), tail_ref)


def relay(own, got):
    return pl.pallas_call(
        relay_kernel,
        out_shape=MESSAGE,
        in_specs=[VMEM] * 2,
        out_specs=VMEM,
        scratch_shapes=[TAIL_REF] * 2,
        compiler_params=PARAMS,
    )(own, got)


PACKED = 3 * SLOTS + TAIL


def pack_kernel(loss_ref, own_ref, low_r, low_l, high_r, high_l, o_ref, *tails):
    messages = (low_r, low_l, high_r, high_l)
    for ref, tail_ref in zip(messages, tails):
        read_tail(ref, tail_ref)
    codes = [loss_ref[...]] + [tail_loss(tail_ref) for tail_ref in tails[:3]]
    loss = decode_loss(jnp.concatenate(codes, axis=0))
    loss = (loss[0:1] + loss[1:2]) + (loss[2:3] + loss[3:4])
    loss = encode_loss(jnp.broadcast_to(loss, (1, 128)))
    pad = jnp.zeros((TAIL - 2, 128), F32)
    for i in range(2):
        for j in range(ROWS2 // 128):
            at = i * (ROWS2 // 128) + j
            val = own_ref[pl.ds(at * 128, 128), :]
            got = [read_message(messages[n], tails[n], j) for n in (2 * i, 2 * i + 1)]
            code, e = encode(val + (got[0] + got[1]))
            tail = to16(jnp.concatenate([e, loss, pad], axis=0))
            for n in range(128 // SLOTS):
                for k in range(3):
                    o_ref[at * 4 + n, k * SLOTS : (k + 1) * SLOTS, :] = code[
                        n * SLOTS : (n + 1) * SLOTS, k * 128 : (k + 1) * 128
                    ]
                o_ref[at * 4 + n, 3 * SLOTS :, :] = tail


def pack(loss, own, low_r, low_l, high_r, high_l):
    return pl.pallas_call(
        pack_kernel,
        out_shape=jax.ShapeDtypeStruct((TRAINERS, PACKED, 128), I16),
        in_specs=[VMEM] * 6,
        out_specs=VMEM,
        scratch_shapes=[TAIL_REF] * 4,
        compiler_params=PARAMS,
    )(loss, own, low_r, low_l, high_r, high_l)


def finish_kernel(at_ref, x_ref, grad_ref, loss_ref, e_ref):
    tail = from16(x_ref[:, 3 * SLOTS :, :])
    e = tail[:, 0, :]
    e_ref[...] = jnp.concatenate([e, jnp.zeros((128 - TRAINERS, 128), F32)], axis=0).T
    scale = power(e_ref[pl.ds(pl.multiple_of(at_ref[0] * SLOTS, SLOTS), SLOTS), :])
    total = [jnp.zeros((SLOTS, 128), F32)] * 3
    for s in range(TRAINERS):
        for k in range(3):
            total[k] += from16(x_ref[s, k * SLOTS : (k + 1) * SLOTS, :]) * scale[:, s : s + 1]
    for k in range(3):
        grad_ref[:, k * 128 : (k + 1) * 128] = total[k]
    loss_ref[0, 0] = jnp.sum(decode_loss(tail[:, 1, :]))


def finish(at, x):
    return pl.pallas_call(
        finish_kernel,
        out_shape=(
            jax.ShapeDtypeStruct((SLOTS, LOCAL), F32),
            jax.ShapeDtypeStruct((1, 1), F32),
        ),
        in_specs=[SMEM, VMEM],
        out_specs=(VMEM, SMEM),
        scratch_shapes=[pltpu.VMEM((128, 128), F32)],
        compiler_params=PARAMS,
    )(at, x)


HEAD_BLOCK = 256
HEAD_STEPS = HALF // HEAD_BLOCK


def head_kernel(c_ref, table_ref, sums_ref, o_ref):
    both = dot(table_ref[0], sums_ref[...], ((0,), (0,)))
    both = both[:, 0:LOCAL] + both[:, LOCAL:]
    for j in range(LOCAL // 128):
        o_ref[pl.ds(j, HEAD_BLOCK, stride=LOCAL // 128), :] = both[:, j * 128 : (j + 1) * 128]


def head_gradient(c, table, sums):
    def place(i, c):
        side = lax.rem(c[0] + i // HEAD_STEPS, 2)
        return (side * HEAD_STEPS + i % HEAD_STEPS, 0)

    return pl.pallas_call(
        head_kernel,
        grid_spec=pltpu.PrefetchScalarGridSpec(
            num_scalar_prefetch=1,
            grid=(2 * HEAD_STEPS,),
            in_specs=[
                pl.BlockSpec(
                    (1, ROWS, HEAD_BLOCK), lambda i, c: (i // HEAD_STEPS, 0, i % HEAD_STEPS)
                ),
                pl.BlockSpec((ROWS, 2 * LOCAL), lambda i, c: (0, 0)),
            ],
            out_specs=pl.BlockSpec((HEAD_BLOCK * LOCAL // 128, 128), place),
        ),
        out_shape=jax.ShapeDtypeStruct((D * LOCAL // 128, 128), F32),
        compiler_params=PARAMS,
        cost_estimate=pl.CostEstimate(
            flops=4 * ROWS * D * LOCAL, bytes_accessed=12 * 1024 * 1024, transcendentals=0
        ),
    )(c, table, sums)


PAIR = [(i, i ^ 1) for i in range(SHARDS)]


def along_x(k):
    return [(i, (i + 2 * k) % SHARDS) for i in range(SHARDS)]


RIGHT, LEFT = along_x(1), along_x(-1)


def along_z(k):
    return [(i, (i // Y + k) % Z * Y + i % Y) for i in range(TRAINERS)]


def along_y(k):
    return [(i, i // Y * Y + (i + k) % Y) for i in range(TRAINERS)]


def on_device(hidden_table, head_weight, targets, counts, dest, token):
    me = lax.axis_index("vocab")
    trainer = lax.axis_index("trainer")
    c = lax.rem(me, 2)
    x = me // 2
    y = lax.rem(trainer, Y)
    c1 = c.reshape(1).astype(jnp.int32)
    at_cx = jnp.stack([c, x]).astype(jnp.int32)
    at_cy = jnp.stack([c, y]).astype(jnp.int32)
    z1 = (trainer // Y).reshape(1).astype(jnp.int32)
    weight = head_weight[:, 0, :]

    half = lax.dynamic_slice(hidden_table, (0, c * HALF), (SLOTS, HALF))
    near = [half] + [lax.ppermute(half, "trainer", along_z(k)) for k in (1, 2, -2, -1)]
    near[3:3] = [
        lax.ppermute(near[2], "trainer", along_z(1)),
        lax.ppermute(near[2], "trainer", along_z(2)),
        lax.ppermute(near[3], "trainer", along_z(-1)),
    ]

    gid = dest * SLOTS + token
    index = jnp.arange(ROWS, dtype=jnp.int32)
    live = (index % SLOTS < jnp.repeat(counts, SLOTS)).astype(F32).reshape(1, ROWS)
    gid = gid.astype(F32).reshape(1, ROWS)

    z1, gid, live = lax.optimization_barrier((z1, gid, live))
    plane = in_order(z1, near)
    low0, high0 = plane[: Z // 2], plane[Z // 2 :]
    low1 = lax.ppermute(low0, "trainer", along_y(1))
    high3 = lax.ppermute(high0, "trainer", along_y(-1))
    high1 = lax.ppermute(high0, "trainer", along_y(1))
    low3 = lax.ppermute(low0, "trainer", along_y(-1))
    low2 = lax.ppermute(low1, "trainer", along_y(1))
    high2 = lax.ppermute(high3, "trainer", along_y(-1))
    middle = jnp.concatenate([low1, high3, high1, low3])
    at_cx, targets, _ = lax.optimization_barrier((at_cx, targets, middle))
    split = split_targets(targets[:, 0, :])
    w_own, w_give = turn_weights(at_cx, weight.reshape(4, 2, LOCAL, LOCAL))
    low2, split, w_own, w_give = lax.optimization_barrier((low2, split, w_own, w_give))
    pieces = [plane, middle, jnp.concatenate([low2, high2])]
    pieces += [lax.ppermute(p, "vocab", PAIR) for p in pieces]
    split, _ = lax.optimization_barrier((split, (w_give, low2, high2, pieces[3])))
    probs = lax.all_to_all(split, "trainer", split_axis=0, concat_axis=0, tiled=True)

    table, logits, stats, top = logits_and_stats(at_cy, pieces, weight)
    stats = merge_stats([stats, lax.ppermute(stats, "vocab", PAIR)])
    stats = [stats] + [lax.ppermute(stats, "vocab", along_x(k)) for k in (1, 2, 3)]
    stats = merge_stats(stats, TRAINERS)
    w_give, _ = lax.optimization_barrier((w_give, stats))
    w_other = lax.ppermute(w_give, "vocab", PAIR)
    stats, probs = lax.optimization_barrier((stats, probs.reshape(ROWS, LOCAL)))
    stats = lax.all_to_all(stats, "trainer", split_axis=0, concat_axis=0, tiled=True)

    e, mass, cross = select_rows(top, logits, probs, gid, live)
    high, sums, loss = gradients(stats, top, mass, cross, e, probs, gid, live)

    more = lax.ppermute(loss, "vocab", PAIR)
    far = lax.ppermute(high, "vocab", PAIR)
    l2, h2, loss = far_terms(loss, more, high, far, w_own, w_other)
    low_r = lax.ppermute(l2, "vocab", RIGHT)
    high_l = lax.ppermute(h2, "vocab", LEFT)
    l1, h1, l3, h3, t0 = near_terms(loss, high, far, w_own, w_other)
    high_r = lax.ppermute(h1, "vocab", RIGHT)
    low_l = lax.ppermute(l3, "vocab", LEFT)
    low_r = lax.ppermute(relay(l1, low_r), "vocab", RIGHT)
    high_l = lax.ppermute(relay(h3, high_l), "vocab", LEFT)
    head = head_gradient(c1, table, sums)
    packed = pack(loss, t0, low_r, low_l, high_r, high_l)
    packed = lax.all_to_all(packed, "trainer", split_axis=0, concat_axis=0, tiled=True)
    table_grad, loss = finish(lax.rem(trainer, 4).reshape(1).astype(jnp.int32), packed)
    mean_loss = loss[0, 0] / jnp.sum(counts).astype(F32)
    return head.reshape(D, 1, LOCAL), table_grad, mean_loss


def solution(mesh):
    return jax.shard_map(
        on_device,
        mesh=mesh,
        in_specs=(
            P("trainer", None),
            P(None, "vocab", "trainer"),
            P("trainer", "vocab", None),
            P(),
            P(),
            P(),
        ),
        out_specs=(P(None, "vocab", "trainer"), P("trainer", "vocab"), P()),
        check_vma=False,
    )
```

```python
import functools
import math

import jax
import jax.numpy as jnp
from jax import lax
from jax.experimental import pallas as pl
from jax.experimental.pallas import tpu as pltpu
from jax.sharding import PartitionSpec as P

D = 3072
VOCAB = 98304
ROWS = 1024
TRAINERS = 32
SLOTS = 32
SHARDS = 8
LOCAL = VOCAB // (TRAINERS * SHARDS)
HALF = D // 2
BLOCK = 256
BF16 = jnp.bfloat16
F32 = jnp.float32
PARAMS = pltpu.CompilerParams(vmem_limit_bytes=24 * 1024 * 1024)
FULL = pltpu.CompilerParams(vmem_limit_bytes=60 * 1024 * 1024)
VMEM = pl.BlockSpec(memory_space=pltpu.VMEM)
SMEM = pl.BlockSpec(memory_space=pltpu.SMEM)
ANY = pl.BlockSpec(memory_space=pl.ANY)


def dot(a, b, dims=((1,), (0,))):
    return lax.dot_general(a, b, (dims, ((), ())), preferred_element_type=F32)


def split_kernel(x_ref, o_ref):
    for j in range(TRAINERS):
        o_ref[j] = x_ref[:, j * LOCAL : (j + 1) * LOCAL]


def split_targets(x):
    return pl.pallas_call(
        split_kernel,
        out_shape=jax.ShapeDtypeStruct((TRAINERS, SLOTS, LOCAL), BF16),
        in_specs=[VMEM],
        out_specs=VMEM,
        compiler_params=FULL,
    )(x)


Z = 8
Y = 4


PLACES = (((0, 0), (0, 4)), ((1, 0), (1, 8)), ((2, 0), (2, 4)), ((1, 12), (1, 4)))


def order_kernel(z_ref, *refs):
    for k, piece in enumerate(refs[:Z]):
        refs[Z][lax.rem(z_ref[0] + Z - k, Z)] = piece[...]


def in_order(z, pieces):
    return pl.pallas_call(
        order_kernel,
        out_shape=jax.ShapeDtypeStruct((Z, SLOTS, HALF), BF16),
        in_specs=[SMEM] + [VMEM] * Z,
        out_specs=VMEM,
        compiler_params=PARAMS,
    )(z, *pieces)


def logit_kernel(at_ref, *refs):
    pieces, refs = refs[:6], refs[6:]
    far_ref, table_ref, logits_ref, lse_ref, top_ref, *refs = refs
    tabs, w_ref, logit_buf, in_sems, out_sems = refs
    c, y = at_ref[0], at_ref[1]
    copies = [[], []]
    for side in range(2):
        rows = pl.ds(pl.multiple_of((c + side) % 2 * HALF, HALF), HALF)
        copies[side].append(
            pltpu.make_async_copy(far_ref.at[rows], w_ref.at[side], in_sems.at[16 + side])
        )
        for dy in range(Y):
            y_at = lax.rem(y + Y - dy, Y)
            for high in range(2):
                which, first = PLACES[dy][high]
                piece = pieces[side * 3 + which].at[pl.ds(first, Z // 2)]
                place = tabs.at[side, pl.ds(high * (Z // 2), Z // 2), y_at]
                sem = in_sems.at[side * 8 + dy * 2 + high]
                copies[side].append(pltpu.make_async_copy(piece, place, sem))
        for copy in copies[side]:
            copy.start()
    block = 2 * BLOCK
    step = block // (Y * SLOTS)

    def part(side, i):
        rows = tabs[side, pl.ds(i * step, step)].reshape(block, HALF)
        return dot(rows, w_ref[side])

    def store(i):
        rows = pl.ds(i * block, block)
        return pltpu.make_async_copy(logit_buf.at[rows], logits_ref.at[rows], out_sems.at[2 + i])

    stores = []
    for side in range(2):
        for copy in copies[side]:
            copy.wait()
        stores.append(
            pltpu.make_async_copy(tabs.at[side], table_ref.at[side], out_sems.at[side])
        )
        stores[-1].start()
        for i in range(ROWS // block):
            rows = pl.ds(i * block, block)
            if side == 0:
                logit_buf[rows, :] = part(side, i)
                continue
            logits = logit_buf[rows, :] + part(side, i)
            logit_buf[rows, :] = logits
            store(i).start()
            top = jnp.max(logits, axis=1, keepdims=True)
            lse = top + jnp.log(jnp.sum(jnp.exp(logits - top), axis=1, keepdims=True))
            for value, out in ((lse, lse_ref), (top, top_ref)):
                flat = jnp.broadcast_to(value, (block, 128)).T
                for j in range(block // 128):
                    row = flat[0:1, j * 128 : (j + 1) * 128]
                    out[pl.ds(i * (block // 128) + j, 1), :] = row

    for copy in stores + [store(i) for i in range(ROWS // block)]:
        copy.wait()


def logits_and_stats(at, pieces, weight):
    table, logits, lse, top = pl.pallas_call(
        logit_kernel,
        out_shape=(
            jax.ShapeDtypeStruct((2, Z, Y, SLOTS, HALF), BF16),
            jax.ShapeDtypeStruct((ROWS, LOCAL), F32),
            jax.ShapeDtypeStruct((8, 128), F32),
            jax.ShapeDtypeStruct((8, 128), F32),
        ),
        in_specs=[SMEM] + [ANY] * 7,
        out_specs=(ANY, ANY, VMEM, VMEM),
        scratch_shapes=[
            pltpu.VMEM((2, Z, Y, SLOTS, HALF), BF16),
            pltpu.VMEM((2, HALF, LOCAL), BF16),
            pltpu.VMEM((ROWS, LOCAL), F32),
            pltpu.SemaphoreType.DMA((18,)),
            pltpu.SemaphoreType.DMA((6,)),
        ],
        compiler_params=FULL,
    )(at, *pieces, weight)
    return table.reshape(2, ROWS, HALF), logits, lse, top


def merge(x):
    top = jnp.max(x, axis=0)
    return top + jnp.log(jnp.sum(jnp.exp(x - top[None]), axis=0))


def merge_kernel(copies, *refs):
    lse = merge(jnp.stack([ref[...] for ref in refs[:-1]]))
    if copies == 1:
        refs[-1][...] = lse
    for k in range(copies if copies > 1 else 0):
        refs[-1][k] = lse


def merge_stats(parts, copies=1):
    shape = (8, 128) if copies == 1 else (copies, 8, 128)
    return pl.pallas_call(
        functools.partial(merge_kernel, copies),
        out_shape=jax.ShapeDtypeStruct(shape, F32),
        in_specs=[VMEM] * len(parts),
        out_specs=VMEM,
        compiler_params=PARAMS if copies == 1 else FULL,
    )(*parts)


def column(row):
    return jnp.broadcast_to(row, (128, row.shape[1])).T


def select_kernel(
    top_ref, far_ref, targets_ref, gid_ref, live_ref, e_ref, mass_ref, cross_ref, *scratch
):
    logits_ref, p_ref, top_col, parts_ref, out_ref, sems = scratch
    fetch = pltpu.make_async_copy(far_ref, logits_ref, sems.at[0])
    fetch.start()
    fetch_targets = pltpu.make_async_copy(targets_ref, p_ref, sems.at[1])
    fetch_targets.start()
    for j in range(8):
        top_col[pl.ds(j * 128, 128), :] = column(top_ref[j : j + 1, :])
    fetch.wait()

    @pl.loop(0, ROWS // 128)
    def _(i):
        rows = pl.ds(pl.multiple_of(i * 128, 128), 128)
        for j in range(LOCAL // 128):
            p = jnp.exp(logits_ref[rows, pl.ds(j * 128, 128)] - top_col[rows, :])
            first = p.astype(BF16)
            p = p - first.astype(F32)
            second = p.astype(BF16)
            third = (p - second.astype(F32)).astype(BF16)
            parts_ref[rows, pl.ds(j * 128, 128)] = first
            parts_ref[rows, pl.ds(LOCAL + j * 128, 128)] = second
            parts_ref[rows, pl.ds(2 * LOCAL + j * 128, 128)] = third

    def store(i):
        rows = pl.ds(pl.multiple_of(i * BLOCK, BLOCK), BLOCK)
        return pltpu.make_async_copy(out_ref.at[rows], e_ref.at[rows], sems.at[2 + i])

    @pl.loop(0, ROWS // BLOCK)
    def _(i):
        rows = pl.ds(pl.multiple_of(i * BLOCK, BLOCK), BLOCK)
        gid = column(gid_ref[:, rows])
        lane = lax.broadcasted_iota(jnp.int32, (BLOCK, 128), 1).astype(F32)
        hot = jnp.concatenate(
            [
                jnp.where(gid == lane + float(128 * k), 1.0, 0.0).astype(BF16)
                for k in range(ROWS // 128)
            ],
            axis=1,
        )
        sel = dot(hot, parts_ref[...])
        out_ref[rows, :] = sel[:, 0:LOCAL] + sel[:, LOCAL : 2 * LOCAL] + sel[:, 2 * LOCAL :]
        store(i).start()

    fetch_targets.wait()

    def total(i, cross):
        rows = pl.ds(pl.multiple_of(i * BLOCK, BLOCK), BLOCK)
        row = lax.broadcasted_iota(jnp.int32, (BLOCK, ROWS), 0) + i * BLOCK
        hot = jnp.where(gid_ref[...] == row.astype(F32), live_ref[...], 0.0).astype(BF16)
        sums = dot(hot, p_ref[...])
        mass = jnp.broadcast_to(jnp.sum(sums, axis=1, keepdims=True), (BLOCK, 128)).T[0:1]
        for j in range(BLOCK // 128):
            mass_ref[pl.ds(i * (BLOCK // 128) + j, 1), :] = mass[:, j * 128 : (j + 1) * 128]
        return cross + jnp.sum(sums * logits_ref[rows, :])

    cross_ref[0, 0] = lax.fori_loop(0, ROWS // BLOCK, total, jnp.float32(0))
    for i in range(ROWS // BLOCK):
        store(i).wait()


def select_rows(top, logits, probs, gid, live):
    return pl.pallas_call(
        select_kernel,
        out_shape=(
            jax.ShapeDtypeStruct((ROWS, LOCAL), F32),
            jax.ShapeDtypeStruct((8, 128), F32),
            jax.ShapeDtypeStruct((1, 1), F32),
        ),
        in_specs=[VMEM, ANY, ANY, VMEM, VMEM],
        out_specs=(ANY, VMEM, SMEM),
        scratch_shapes=[
            pltpu.VMEM((ROWS, LOCAL), F32),
            pltpu.VMEM((ROWS, LOCAL), BF16),
            pltpu.VMEM((ROWS, 128), F32),
            pltpu.VMEM((ROWS, 3 * LOCAL), BF16),
            pltpu.VMEM((ROWS, LOCAL), F32),
            pltpu.SemaphoreType.DMA((6,)),
        ],
        compiler_params=FULL,
        cost_estimate=pl.CostEstimate(
            flops=4 * 2 * ROWS * ROWS * LOCAL, bytes_accessed=8 * 1024 * 1024, transcendentals=0
        ),
    )(top, logits, probs, gid, live)


def grad_kernel(
    x_ref, top_ref, mass_ref, cross_ref, far_ref, targets_ref, gid_ref, live_ref, *refs
):
    high_ref, both_ref, loss_ref, e_ref, p_ref, g_ref, sums_ref, sems = refs
    fetch = pltpu.make_async_copy(far_ref, e_ref, sems.at[0])
    fetch.start()
    fetch_targets = pltpu.make_async_copy(targets_ref, p_ref, sems.at[1])
    fetch_targets.start()
    lse = merge(x_ref[...])
    loss_ref[0, 0] = jnp.sum(lse * mass_ref[...]) - cross_ref[0, 0]
    share = jnp.exp(top_ref[...] - lse)
    scale = VOCAB / math.sqrt(ROWS)
    fetch.wait()
    fetch_targets.wait()
    lane = lax.broadcasted_iota(jnp.int32, (128, 128), 1).astype(F32)
    for i in range(ROWS // 128):
        rows = pl.ds(i * 128, 128)
        gid = column(gid_ref[:, rows])
        factor = column(live_ref[:, rows]) * scale
        found = jnp.zeros((128, 128), F32)
        for k in range(ROWS // 128):
            found += jnp.where(gid == lane + float(128 * k), share[k : k + 1], 0.0)
        found = jnp.sum(found, axis=1, keepdims=True)
        for j in range(LOCAL // 128):
            cols = pl.ds(j * 128, 128)
            diff = e_ref[rows, cols] * found - p_ref[rows, cols].astype(F32)
            g_ref[rows, cols] = (factor * diff).astype(BF16)

    def stores(i):
        rows = pl.ds(pl.multiple_of(i * BLOCK, BLOCK), BLOCK)
        high = sums_ref.at[rows, pl.ds(0, LOCAL)]
        yield pltpu.make_async_copy(high, high_ref.at[rows], sems.at[2 + i])
        yield pltpu.make_async_copy(sums_ref.at[rows], both_ref.at[rows], sems.at[6 + i])

    @pl.loop(0, ROWS // BLOCK)
    def _(i):
        rows = pl.ds(pl.multiple_of(i * BLOCK, BLOCK), BLOCK)
        row = lax.broadcasted_iota(jnp.int32, (BLOCK, ROWS), 0) + i * BLOCK
        hot = jnp.where(gid_ref[...] == row.astype(F32), 1.0, 0.0).astype(BF16)
        sums = dot(hot, g_ref[...])
        high = sums.astype(BF16)
        sums_ref[rows, 0:LOCAL] = high
        sums_ref[rows, LOCAL:] = (sums - high.astype(F32)).astype(BF16)
        for store in stores(i):
            store.start()

    for i in range(ROWS // BLOCK):
        for store in stores(i):
            store.wait()


def gradients(x, top, mass, cross, e, probs, gid, live):
    return pl.pallas_call(
        grad_kernel,
        out_shape=(
            jax.ShapeDtypeStruct((ROWS, LOCAL), BF16),
            jax.ShapeDtypeStruct((ROWS, 2 * LOCAL), BF16),
            jax.ShapeDtypeStruct((1, 1), F32),
        ),
        in_specs=[VMEM, VMEM, VMEM, SMEM, ANY, ANY, VMEM, VMEM],
        out_specs=(ANY, ANY, SMEM),
        scratch_shapes=[
            pltpu.VMEM((ROWS, LOCAL), F32),
            pltpu.VMEM((ROWS, LOCAL), BF16),
            pltpu.VMEM((ROWS, LOCAL), BF16),
            pltpu.VMEM((ROWS, 2 * LOCAL), BF16),
            pltpu.SemaphoreType.DMA((10,)),
        ],
        compiler_params=FULL,
    )(x, top, mass, cross, e, probs, gid, live)


TOP = 32700.0
ROWS2 = ROWS // 2
TAIL = 16
I16 = jnp.int16


def exponent(x):
    return jnp.ceil(jnp.log(jnp.maximum(x, 1e-30) / TOP) * (256.0 / math.log(2.0)))


def power(e):
    return jnp.exp2(e * (1.0 / 256.0))


def to16(x):
    return x.astype(jnp.int32).astype(I16)


def from16(x):
    return x.astype(jnp.int32).astype(F32)


def encode(val):
    e = exponent(jnp.max(jnp.abs(val), axis=1, keepdims=True))
    return to16(jnp.round(val * power(-e))), jnp.broadcast_to(e, (128, 128)).T[0:1]


def wide(row):
    return jnp.concatenate([row] + [jnp.zeros_like(row)] * (LOCAL // 128 - 1), axis=1)


def write_message(out_ref, block_of, loss, tail_ref):
    for j in range(ROWS2 // 128):
        code, e = encode(block_of(j))
        out_ref[pl.ds(j * 128, 128), :] = code
        tail_ref[pl.ds(j, 1), :] = e
    tail = [tail_ref[0 : ROWS2 // 128, :], loss, jnp.zeros((TAIL - ROWS2 // 128 - 1, 128), F32)]
    tail = jnp.concatenate(tail, axis=0)
    zeros = [jnp.zeros_like(tail)] * (LOCAL // 128 - 1)
    out_ref[pl.ds(ROWS2, TAIL), :] = to16(jnp.concatenate([tail] + zeros, axis=1))


def encode_loss(loss):
    e = exponent(jnp.abs(loss))
    whole = loss * power(-e)
    first = jnp.round(whole)
    rest = jnp.round((whole - first) * TOP)
    lane = lax.broadcasted_iota(jnp.int32, (1, 128), 1)
    return jnp.where(lane == 0, e, jnp.where(lane == 1, first, jnp.where(lane == 2, rest, 0.0)))


def decode_loss(code):
    return (code[:, 1:2] + code[:, 2:3] * (1.0 / TOP)) * power(code[:, 0:1])


def read_tail(ref, tail_ref):
    tail_ref[...] = from16(ref[pl.ds(ROWS2, TAIL), 0:128])


def tail_loss(tail_ref):
    return tail_ref[ROWS2 // 128 : ROWS2 // 128 + 1, :]


def read_message(ref, tail_ref, j):
    scale = power(column(tail_ref[pl.ds(j, 1), :]))
    rows = pl.ds(j * 128, 128)
    parts = [from16(ref[rows, k * 128 : (k + 1) * 128]) * scale for k in range(LOCAL // 128)]
    return jnp.concatenate(parts, axis=1)


TAIL_REF = pltpu.VMEM((TAIL, 128), F32)
MESSAGE = jax.ShapeDtypeStruct((ROWS2 + TAIL, LOCAL), I16)


def weight_kernel(at_ref, all_ref, keep_ref, give_ref, block_ref, sems):
    c, x = at_ref[0], at_ref[1]

    def fetch(n):
        source = all_ref.at[lax.rem(x + (2, 1, 3, 0)[n % 4], 4), lax.rem(c + n // 4, 2)]
        return pltpu.make_async_copy(source, block_ref.at[n], sems.at[n])

    for n in range(8):
        fetch(n).start()
    for n in range(8):
        fetch(n).wait()
        out = (keep_ref, give_ref)[n // 4]
        out[:, n % 4 * LOCAL : (n % 4 + 1) * LOCAL] = block_ref[n].T


def turn_weights(at, blocks):
    half = jax.ShapeDtypeStruct((LOCAL, 4 * LOCAL), BF16)
    return pl.pallas_call(
        weight_kernel,
        out_shape=(half, half),
        in_specs=[SMEM, ANY],
        out_specs=(VMEM, VMEM),
        scratch_shapes=[
            pltpu.VMEM((8, LOCAL, LOCAL), BF16),
            pltpu.SemaphoreType.DMA((8,)),
        ],
        compiler_params=FULL,
    )(at, blocks)


def fetch_pair(own_ref, other_ref, w_own, w_other, first, n, g_ref, w_ref, sems):
    cols = pl.ds(first * LOCAL, n * LOCAL)
    copies = [
        pltpu.make_async_copy(ref, g_ref.at[:, pl.ds(k * LOCAL, LOCAL)], sems.at[k])
        for k, ref in enumerate((own_ref, other_ref))
    ] + [
        pltpu.make_async_copy(ref.at[:, cols], w_ref.at[pl.ds(k * LOCAL, LOCAL)], sems.at[2 + k])
        for k, ref in enumerate((w_own, w_other))
    ]
    for copy in copies:
        copy.start()
    return copies


def far_kernel(
    loss_ref, more_ref, own_ref, other_ref, w_own, w_other, low, high, sum_ref, *refs
):
    g_ref, w_ref, val_ref, tail_ref, sems = refs
    copies = fetch_pair(own_ref, other_ref, w_own, w_other, 0, 1, g_ref, w_ref, sems)
    loss = encode_loss(jnp.full((1, 128), loss_ref[0, 0] + more_ref[0, 0], F32))
    sum_ref[...] = loss
    for copy in copies:
        copy.wait()
    for i, out in enumerate((low, high)):
        val_ref[...] = dot(g_ref[pl.ds(i * ROWS2, ROWS2), :], w_ref[...])
        write_message(out, lambda j: val_ref[pl.ds(j * 128, 128), :], loss, tail_ref)


def near_kernel(
    loss_ref, own_ref, other_ref, w_own, w_other, l1, h1, l3, h3, c0, g_ref, w_ref, val_ref, tail_ref, sems
):
    copies = fetch_pair(own_ref, other_ref, w_own, w_other, 1, 3, g_ref, w_ref, sems)
    for copy in copies:
        copy.wait()
    for i in range(2):
        rows = pl.ds(i * ROWS2, ROWS2)
        val_ref[...] = dot(g_ref[rows, :], w_ref[...])
        for k, out in enumerate(((l1, h1)[i], (l3, h3)[i])):
            cols = slice(k * LOCAL, (k + 1) * LOCAL)
            if out.dtype == F32:
                out[...] = val_ref[:, cols]
            else:
                write_message(
                    out, lambda j: val_ref[pl.ds(j * 128, 128), cols], loss_ref[...], tail_ref
                )
        c0[rows, :] = val_ref[:, 2 * LOCAL :]


def pair_scratch(n):
    return [
        pltpu.VMEM((ROWS, 2 * LOCAL), BF16),
        pltpu.VMEM((2 * LOCAL, n * LOCAL), BF16),
        pltpu.VMEM((ROWS2, n * LOCAL), F32),
        TAIL_REF,
        pltpu.SemaphoreType.DMA((4,)),
    ]


def far_terms(loss, more, own, other, w_own, w_other):
    return pl.pallas_call(
        far_kernel,
        out_shape=(MESSAGE, MESSAGE, jax.ShapeDtypeStruct((1, 128), F32)),
        in_specs=[SMEM, SMEM] + [ANY] * 4,
        out_specs=(VMEM,) * 3,
        scratch_shapes=pair_scratch(1),
        compiler_params=PARAMS,
    )(loss, more, own, other, w_own, w_other)


def near_terms(loss, own, other, w_own, w_other):
    part = jax.ShapeDtypeStruct((ROWS2, LOCAL), F32)
    return pl.pallas_call(
        near_kernel,
        out_shape=(part, MESSAGE, MESSAGE, part, jax.ShapeDtypeStruct((ROWS, LOCAL), F32)),
        in_specs=[VMEM] + [ANY] * 4,
        out_specs=(VMEM,) * 5,
        scratch_shapes=pair_scratch(3),
        compiler_params=PARAMS,
    )(loss, own, other, w_own, w_other)


def relay_kernel(own_ref, got_ref, out_ref, got_tail, tail_ref):
    read_tail(got_ref, got_tail)

    def block(j):
        rows = pl.ds(j * 128, 128)
        return own_ref[rows, :] + read_message(got_ref, got_tail, j)

    write_message(out_ref, block, tail_loss(got_tail), tail_ref)


def relay(own, got):
    return pl.pallas_call(
        relay_kernel,
        out_shape=MESSAGE,
        in_specs=[VMEM] * 2,
        out_specs=VMEM,
        scratch_shapes=[TAIL_REF] * 2,
        compiler_params=PARAMS,
    )(own, got)


PACKED = 3 * SLOTS + TAIL


def pack_kernel(loss_ref, own_ref, low_r, low_l, high_r, high_l, o_ref, *tails):
    messages = (low_r, low_l, high_r, high_l)
    for ref, tail_ref in zip(messages, tails):
        read_tail(ref, tail_ref)
    codes = [loss_ref[...]] + [tail_loss(tail_ref) for tail_ref in tails[:3]]
    loss = decode_loss(jnp.concatenate(codes, axis=0))
    loss = (loss[0:1] + loss[1:2]) + (loss[2:3] + loss[3:4])
    loss = encode_loss(jnp.broadcast_to(loss, (1, 128)))
    pad = jnp.zeros((TAIL - 2, 128), F32)
    for i in range(2):
        for j in range(ROWS2 // 128):
            at = i * (ROWS2 // 128) + j
            val = own_ref[pl.ds(at * 128, 128), :]
            got = [read_message(messages[n], tails[n], j) for n in (2 * i, 2 * i + 1)]
            code, e = encode(val + (got[0] + got[1]))
            tail = to16(jnp.concatenate([e, loss, pad], axis=0))
            for n in range(128 // SLOTS):
                for k in range(3):
                    o_ref[at * 4 + n, k * SLOTS : (k + 1) * SLOTS, :] = code[
                        n * SLOTS : (n + 1) * SLOTS, k * 128 : (k + 1) * 128
                    ]
                o_ref[at * 4 + n, 3 * SLOTS :, :] = tail


def pack(loss, own, low_r, low_l, high_r, high_l):
    return pl.pallas_call(
        pack_kernel,
        out_shape=jax.ShapeDtypeStruct((TRAINERS, PACKED, 128), I16),
        in_specs=[VMEM] * 6,
        out_specs=VMEM,
        scratch_shapes=[TAIL_REF] * 4,
        compiler_params=PARAMS,
    )(loss, own, low_r, low_l, high_r, high_l)


def finish_kernel(at_ref, x_ref, grad_ref, loss_ref, e_ref):
    tail = from16(x_ref[:, 3 * SLOTS :, :])
    e = tail[:, 0, :]
    e_ref[...] = jnp.concatenate([e, jnp.zeros((128 - TRAINERS, 128), F32)], axis=0).T
    scale = power(e_ref[pl.ds(pl.multiple_of(at_ref[0] * SLOTS, SLOTS), SLOTS), :])
    total = [jnp.zeros((SLOTS, 128), F32)] * 3
    for s in range(TRAINERS):
        for k in range(3):
            total[k] += from16(x_ref[s, k * SLOTS : (k + 1) * SLOTS, :]) * scale[:, s : s + 1]
    for k in range(3):
        grad_ref[:, k * 128 : (k + 1) * 128] = total[k]
    loss_ref[0, 0] = jnp.sum(decode_loss(tail[:, 1, :]))


def finish(at, x):
    return pl.pallas_call(
        finish_kernel,
        out_shape=(
            jax.ShapeDtypeStruct((SLOTS, LOCAL), F32),
            jax.ShapeDtypeStruct((1, 1), F32),
        ),
        in_specs=[SMEM, VMEM],
        out_specs=(VMEM, SMEM),
        scratch_shapes=[pltpu.VMEM((128, 128), F32)],
        compiler_params=PARAMS,
    )(at, x)


HEAD_BLOCK = 256
HEAD_STEPS = HALF // HEAD_BLOCK


def head_kernel(c_ref, table_ref, sums_ref, o_ref):
    both = dot(table_ref[0], sums_ref[...], ((0,), (0,)))
    both = both[:, 0:LOCAL] + both[:, LOCAL:]
    for j in range(LOCAL // 128):
        o_ref[pl.ds(j, HEAD_BLOCK, stride=LOCAL // 128), :] = both[:, j * 128 : (j + 1) * 128]


def head_gradient(c, table, sums):
    def place(i, c):
        side = lax.rem(c[0] + i // HEAD_STEPS, 2)
        return (side * HEAD_STEPS + i % HEAD_STEPS, 0)

    return pl.pallas_call(
        head_kernel,
        grid_spec=pltpu.PrefetchScalarGridSpec(
            num_scalar_prefetch=1,
            grid=(2 * HEAD_STEPS,),
            in_specs=[
                pl.BlockSpec(
                    (1, ROWS, HEAD_BLOCK), lambda i, c: (i // HEAD_STEPS, 0, i % HEAD_STEPS)
                ),
                pl.BlockSpec((ROWS, 2 * LOCAL), lambda i, c: (0, 0)),
            ],
            out_specs=pl.BlockSpec((HEAD_BLOCK * LOCAL // 128, 128), place),
        ),
        out_shape=jax.ShapeDtypeStruct((D * LOCAL // 128, 128), F32),
        compiler_params=PARAMS,
        cost_estimate=pl.CostEstimate(
            flops=4 * ROWS * D * LOCAL, bytes_accessed=12 * 1024 * 1024, transcendentals=0
        ),
    )(c, table, sums)


PAIR = [(i, i ^ 1) for i in range(SHARDS)]


def along_x(k):
    return [(i, (i + 2 * k) % SHARDS) for i in range(SHARDS)]


RIGHT, LEFT = along_x(1), along_x(-1)


def along_z(k):
    return [(i, (i // Y + k) % Z * Y + i % Y) for i in range(TRAINERS)]


def along_y(k):
    return [(i, i // Y * Y + (i + k) % Y) for i in range(TRAINERS)]


def on_device(hidden_table, head_weight, targets, counts, dest, token):
    me = lax.axis_index("vocab")
    trainer = lax.axis_index("trainer")
    c = lax.rem(me, 2)
    x = me // 2
    y = lax.rem(trainer, Y)
    c1 = c.reshape(1).astype(jnp.int32)
    at_cx = jnp.stack([c, x]).astype(jnp.int32)
    at_cy = jnp.stack([c, y]).astype(jnp.int32)
    z1 = (trainer // Y).reshape(1).astype(jnp.int32)
    weight = head_weight[:, 0, :]

    half = lax.dynamic_slice(hidden_table, (0, c * HALF), (SLOTS, HALF))
    near = [half] + [lax.ppermute(half, "trainer", along_z(k)) for k in (1, 2, -2, -1)]
    near[3:3] = [
        lax.ppermute(near[2], "trainer", along_z(1)),
        lax.ppermute(near[2], "trainer", along_z(2)),
        lax.ppermute(near[3], "trainer", along_z(-1)),
    ]

    gid = dest * SLOTS + token
    index = jnp.arange(ROWS, dtype=jnp.int32)
    live = (index % SLOTS < jnp.repeat(counts, SLOTS)).astype(F32).reshape(1, ROWS)
    gid = gid.astype(F32).reshape(1, ROWS)

    z1, gid, live = lax.optimization_barrier((z1, gid, live))
    plane = in_order(z1, near)
    low0, high0 = plane[: Z // 2], plane[Z // 2 :]
    low1 = lax.ppermute(low0, "trainer", along_y(1))
    high3 = lax.ppermute(high0, "trainer", along_y(-1))
    high1 = lax.ppermute(high0, "trainer", along_y(1))
    low3 = lax.ppermute(low0, "trainer", along_y(-1))
    at_cx, _ = lax.optimization_barrier((at_cx, plane))
    w_own, w_give = turn_weights(at_cx, weight.reshape(4, 2, LOCAL, LOCAL))
    low1, high3, w_own, w_give = lax.optimization_barrier((low1, high3, w_own, w_give))
    low2 = lax.ppermute(low1, "trainer", along_y(1))
    high2 = lax.ppermute(high3, "trainer", along_y(-1))
    targets, _ = lax.optimization_barrier((targets, (low1, high3)))
    split = split_targets(targets[:, 0, :])
    high1, split = lax.optimization_barrier((high1, split))
    middle = jnp.concatenate([low1, high3, high1, low3])
    pieces = [plane, middle, jnp.concatenate([low2, high2])]
    pieces += [lax.ppermute(p, "vocab", PAIR) for p in pieces]
    split, _ = lax.optimization_barrier((split, (w_give, low2, high2, pieces[3])))
    probs = lax.all_to_all(split, "trainer", split_axis=0, concat_axis=0, tiled=True)

    table, logits, stats, top = logits_and_stats(at_cy, pieces, weight)
    stats = merge_stats([stats, lax.ppermute(stats, "vocab", PAIR)])
    stats = [stats] + [lax.ppermute(stats, "vocab", along_x(k)) for k in (1, 2, 3)]
    stats = merge_stats(stats, TRAINERS)
    w_give, _ = lax.optimization_barrier((w_give, stats))
    w_other = lax.ppermute(w_give, "vocab", PAIR)
    stats, probs = lax.optimization_barrier((stats, probs.reshape(ROWS, LOCAL)))
    stats = lax.all_to_all(stats, "trainer", split_axis=0, concat_axis=0, tiled=True)

    e, mass, cross = select_rows(top, logits, probs, gid, live)
    high, sums, loss = gradients(stats, top, mass, cross, e, probs, gid, live)

    more = lax.ppermute(loss, "vocab", PAIR)
    far = lax.ppermute(high, "vocab", PAIR)
    l2, h2, loss = far_terms(loss, more, high, far, w_own, w_other)
    low_r = lax.ppermute(l2, "vocab", RIGHT)
    high_l = lax.ppermute(h2, "vocab", LEFT)
    l1, h1, l3, h3, t0 = near_terms(loss, high, far, w_own, w_other)
    high_r = lax.ppermute(h1, "vocab", RIGHT)
    low_l = lax.ppermute(l3, "vocab", LEFT)
    low_r = lax.ppermute(relay(l1, low_r), "vocab", RIGHT)
    high_l = lax.ppermute(relay(h3, high_l), "vocab", LEFT)
    head = head_gradient(c1, table, sums)
    packed = pack(loss, t0, low_r, low_l, high_r, high_l)
    packed = lax.all_to_all(packed, "trainer", split_axis=0, concat_axis=0, tiled=True)
    table_grad, loss = finish(lax.rem(trainer, 4).reshape(1).astype(jnp.int32), packed)
    mean_loss = loss[0, 0] / jnp.sum(counts).astype(F32)
    return head.reshape(D, 1, LOCAL), table_grad, mean_loss


def solution(mesh):
    return jax.shard_map(
        on_device,
        mesh=mesh,
        in_specs=(
            P("trainer", None),
            P(None, "vocab", "trainer"),
            P("trainer", "vocab", None),
            P(),
            P(),
            P(),
        ),
        out_specs=(P(None, "vocab", "trainer"), P("trainer", "vocab"), P()),
        check_vma=False,
    )
```

```python
import functools
import math

import jax
import jax.numpy as jnp
from jax import lax
from jax.experimental import pallas as pl
from jax.experimental.pallas import tpu as pltpu
from jax.sharding import PartitionSpec as P

D = 3072
VOCAB = 98304
ROWS = 1024
TRAINERS = 32
SLOTS = 32
SHARDS = 8
LOCAL = VOCAB // (TRAINERS * SHARDS)
HALF = D // 2
BLOCK = 256
BF16 = jnp.bfloat16
F32 = jnp.float32
PARAMS = pltpu.CompilerParams(vmem_limit_bytes=24 * 1024 * 1024)
FULL = pltpu.CompilerParams(vmem_limit_bytes=60 * 1024 * 1024)
VMEM = pl.BlockSpec(memory_space=pltpu.VMEM)
SMEM = pl.BlockSpec(memory_space=pltpu.SMEM)
ANY = pl.BlockSpec(memory_space=pl.ANY)


def dot(a, b, dims=((1,), (0,))):
    return lax.dot_general(a, b, (dims, ((), ())), preferred_element_type=F32)


def split_kernel(x_ref, o_ref):
    for j in range(TRAINERS):
        o_ref[j] = x_ref[:, j * LOCAL : (j + 1) * LOCAL]


def split_targets(x):
    return pl.pallas_call(
        split_kernel,
        out_shape=jax.ShapeDtypeStruct((TRAINERS, SLOTS, LOCAL), BF16),
        in_specs=[VMEM],
        out_specs=VMEM,
        compiler_params=FULL,
    )(x)


Z = 8
Y = 4


PLACES = (((0, 0), (0, 4)), ((1, 0), (1, 8)), ((2, 0), (2, 4)), ((1, 12), (1, 4)))


def order_kernel(z_ref, *refs):
    for k, piece in enumerate(refs[:Z]):
        refs[Z][lax.rem(z_ref[0] + Z - k, Z)] = piece[...]


def in_order(z, pieces):
    return pl.pallas_call(
        order_kernel,
        out_shape=jax.ShapeDtypeStruct((Z, SLOTS, HALF), BF16),
        in_specs=[SMEM] + [VMEM] * Z,
        out_specs=VMEM,
        compiler_params=PARAMS,
    )(z, *pieces)


def logit_kernel(at_ref, *refs):
    pieces, refs = refs[:6], refs[6:]
    far_ref, table_ref, logits_ref, lse_ref, top_ref, *refs = refs
    tabs, w_ref, logit_buf, in_sems, out_sems = refs
    c, y = at_ref[0], at_ref[1]
    copies = [[], []]
    for side in range(2):
        rows = pl.ds(pl.multiple_of((c + side) % 2 * HALF, HALF), HALF)
        copies[side].append(
            pltpu.make_async_copy(far_ref.at[rows], w_ref.at[side], in_sems.at[16 + side])
        )
        for dy in range(Y):
            y_at = lax.rem(y + Y - dy, Y)
            for high in range(2):
                which, first = PLACES[dy][high]
                piece = pieces[side * 3 + which].at[pl.ds(first, Z // 2)]
                place = tabs.at[side, pl.ds(high * (Z // 2), Z // 2), y_at]
                sem = in_sems.at[side * 8 + dy * 2 + high]
                copies[side].append(pltpu.make_async_copy(piece, place, sem))
        for copy in copies[side]:
            copy.start()
    block = 2 * BLOCK
    step = block // (Y * SLOTS)

    def part(side, i):
        rows = tabs[side, pl.ds(i * step, step)].reshape(block, HALF)
        return dot(rows, w_ref[side])

    def store(i):
        rows = pl.ds(i * block, block)
        return pltpu.make_async_copy(logit_buf.at[rows], logits_ref.at[rows], out_sems.at[2 + i])

    stores = []
    for side in range(2):
        for copy in copies[side]:
            copy.wait()
        stores.append(
            pltpu.make_async_copy(tabs.at[side], table_ref.at[side], out_sems.at[side])
        )
        stores[-1].start()
        for i in range(ROWS // block):
            rows = pl.ds(i * block, block)
            if side == 0:
                logit_buf[rows, :] = part(side, i)
                continue
            logits = logit_buf[rows, :] + part(side, i)
            logit_buf[rows, :] = logits
            store(i).start()
            top = jnp.max(logits, axis=1, keepdims=True)
            lse = top + jnp.log(jnp.sum(jnp.exp(logits - top), axis=1, keepdims=True))
            for value, out in ((lse, lse_ref), (top, top_ref)):
                flat = jnp.broadcast_to(value, (block, 128)).T
                for j in range(block // 128):
                    row = flat[0:1, j * 128 : (j + 1) * 128]
                    out[pl.ds(i * (block // 128) + j, 1), :] = row

    for copy in stores + [store(i) for i in range(ROWS // block)]:
        copy.wait()


def logits_and_stats(at, pieces, weight):
    table, logits, lse, top = pl.pallas_call(
        logit_kernel,
        out_shape=(
            jax.ShapeDtypeStruct((2, Z, Y, SLOTS, HALF), BF16),
            jax.ShapeDtypeStruct((ROWS, LOCAL), F32),
            jax.ShapeDtypeStruct((8, 128), F32),
            jax.ShapeDtypeStruct((8, 128), F32),
        ),
        in_specs=[SMEM] + [ANY] * 7,
        out_specs=(ANY, ANY, VMEM, VMEM),
        scratch_shapes=[
            pltpu.VMEM((2, Z, Y, SLOTS, HALF), BF16),
            pltpu.VMEM((2, HALF, LOCAL), BF16),
            pltpu.VMEM((ROWS, LOCAL), F32),
            pltpu.SemaphoreType.DMA((18,)),
            pltpu.SemaphoreType.DMA((6,)),
        ],
        compiler_params=FULL,
    )(at, *pieces, weight)
    return table.reshape(2, ROWS, HALF), logits, lse, top


def merge(x):
    top = jnp.max(x, axis=0)
    return top + jnp.log(jnp.sum(jnp.exp(x - top[None]), axis=0))


def merge_kernel(copies, *refs):
    lse = merge(jnp.stack([ref[...] for ref in refs[:-1]]))
    if copies == 1:
        refs[-1][...] = lse
    for k in range(copies if copies > 1 else 0):
        refs[-1][k] = lse


def merge_stats(parts, copies=1):
    shape = (8, 128) if copies == 1 else (copies, 8, 128)
    return pl.pallas_call(
        functools.partial(merge_kernel, copies),
        out_shape=jax.ShapeDtypeStruct(shape, F32),
        in_specs=[VMEM] * len(parts),
        out_specs=VMEM,
        compiler_params=PARAMS if copies == 1 else FULL,
    )(*parts)


def column(row):
    return jnp.broadcast_to(row, (128, row.shape[1])).T


def select_kernel(
    top_ref, far_ref, targets_ref, gid_ref, live_ref, e_ref, mass_ref, cross_ref, *scratch
):
    logits_ref, p_ref, top_col, parts_ref, out_ref, sems = scratch
    fetch = pltpu.make_async_copy(far_ref, logits_ref, sems.at[0])
    fetch.start()
    fetch_targets = pltpu.make_async_copy(targets_ref, p_ref, sems.at[1])
    fetch_targets.start()
    for j in range(8):
        top_col[pl.ds(j * 128, 128), :] = column(top_ref[j : j + 1, :])
    fetch.wait()

    @pl.loop(0, ROWS // 128)
    def _(i):
        rows = pl.ds(pl.multiple_of(i * 128, 128), 128)
        for j in range(LOCAL // 128):
            p = jnp.exp(logits_ref[rows, pl.ds(j * 128, 128)] - top_col[rows, :])
            first = p.astype(BF16)
            p = p - first.astype(F32)
            second = p.astype(BF16)
            third = (p - second.astype(F32)).astype(BF16)
            parts_ref[rows, pl.ds(j * 128, 128)] = first
            parts_ref[rows, pl.ds(LOCAL + j * 128, 128)] = second
            parts_ref[rows, pl.ds(2 * LOCAL + j * 128, 128)] = third

    def store(i):
        rows = pl.ds(pl.multiple_of(i * BLOCK, BLOCK), BLOCK)
        return pltpu.make_async_copy(out_ref.at[rows], e_ref.at[rows], sems.at[2 + i])

    @pl.loop(0, ROWS // BLOCK)
    def _(i):
        rows = pl.ds(pl.multiple_of(i * BLOCK, BLOCK), BLOCK)
        gid = column(gid_ref[:, rows])
        lane = lax.broadcasted_iota(jnp.int32, (BLOCK, 128), 1).astype(F32)
        hot = jnp.concatenate(
            [
                jnp.where(gid == lane + float(128 * k), 1.0, 0.0).astype(BF16)
                for k in range(ROWS // 128)
            ],
            axis=1,
        )
        sel = dot(hot, parts_ref[...])
        out_ref[rows, :] = sel[:, 0:LOCAL] + sel[:, LOCAL : 2 * LOCAL] + sel[:, 2 * LOCAL :]
        store(i).start()

    fetch_targets.wait()

    def total(i, cross):
        rows = pl.ds(pl.multiple_of(i * BLOCK, BLOCK), BLOCK)
        row = lax.broadcasted_iota(jnp.int32, (BLOCK, ROWS), 0) + i * BLOCK
        hot = jnp.where(gid_ref[...] == row.astype(F32), live_ref[...], 0.0).astype(BF16)
        sums = dot(hot, p_ref[...])
        mass = jnp.broadcast_to(jnp.sum(sums, axis=1, keepdims=True), (BLOCK, 128)).T[0:1]
        for j in range(BLOCK // 128):
            mass_ref[pl.ds(i * (BLOCK // 128) + j, 1), :] = mass[:, j * 128 : (j + 1) * 128]
        return cross + jnp.sum(sums * logits_ref[rows, :])

    cross_ref[0, 0] = lax.fori_loop(0, ROWS // BLOCK, total, jnp.float32(0))
    for i in range(ROWS // BLOCK):
        store(i).wait()


def select_rows(top, logits, probs, gid, live):
    return pl.pallas_call(
        select_kernel,
        out_shape=(
            jax.ShapeDtypeStruct((ROWS, LOCAL), F32),
            jax.ShapeDtypeStruct((8, 128), F32),
            jax.ShapeDtypeStruct((1, 1), F32),
        ),
        in_specs=[VMEM, ANY, ANY, VMEM, VMEM],
        out_specs=(ANY, VMEM, SMEM),
        scratch_shapes=[
            pltpu.VMEM((ROWS, LOCAL), F32),
            pltpu.VMEM((ROWS, LOCAL), BF16),
            pltpu.VMEM((ROWS, 128), F32),
            pltpu.VMEM((ROWS, 3 * LOCAL), BF16),
            pltpu.VMEM((ROWS, LOCAL), F32),
            pltpu.SemaphoreType.DMA((6,)),
        ],
        compiler_params=FULL,
        cost_estimate=pl.CostEstimate(
            flops=4 * 2 * ROWS * ROWS * LOCAL, bytes_accessed=8 * 1024 * 1024, transcendentals=0
        ),
    )(top, logits, probs, gid, live)


def grad_kernel(
    x_ref, top_ref, mass_ref, cross_ref, far_ref, targets_ref, gid_ref, live_ref, *refs
):
    high_ref, both_ref, loss_ref, e_ref, p_ref, g_ref, sums_ref, sems = refs
    fetch = pltpu.make_async_copy(far_ref, e_ref, sems.at[0])
    fetch.start()
    fetch_targets = pltpu.make_async_copy(targets_ref, p_ref, sems.at[1])
    fetch_targets.start()
    lse = merge(x_ref[...])
    loss_ref[0, 0] = jnp.sum(lse * mass_ref[...]) - cross_ref[0, 0]
    share = jnp.exp(top_ref[...] - lse)
    scale = VOCAB / math.sqrt(ROWS)
    fetch.wait()
    fetch_targets.wait()
    lane = lax.broadcasted_iota(jnp.int32, (128, 128), 1).astype(F32)
    for i in range(ROWS // 128):
        rows = pl.ds(i * 128, 128)
        gid = column(gid_ref[:, rows])
        factor = column(live_ref[:, rows]) * scale
        found = jnp.zeros((128, 128), F32)
        for k in range(ROWS // 128):
            found += jnp.where(gid == lane + float(128 * k), share[k : k + 1], 0.0)
        found = jnp.sum(found, axis=1, keepdims=True)
        for j in range(LOCAL // 128):
            cols = pl.ds(j * 128, 128)
            diff = e_ref[rows, cols] * found - p_ref[rows, cols].astype(F32)
            g_ref[rows, cols] = (factor * diff).astype(BF16)

    def stores(i):
        rows = pl.ds(pl.multiple_of(i * BLOCK, BLOCK), BLOCK)
        high = sums_ref.at[rows, pl.ds(0, LOCAL)]
        yield pltpu.make_async_copy(high, high_ref.at[rows], sems.at[2 + i])
        yield pltpu.make_async_copy(sums_ref.at[rows], both_ref.at[rows], sems.at[6 + i])

    @pl.loop(0, ROWS // BLOCK)
    def _(i):
        rows = pl.ds(pl.multiple_of(i * BLOCK, BLOCK), BLOCK)
        row = lax.broadcasted_iota(jnp.int32, (BLOCK, ROWS), 0) + i * BLOCK
        hot = jnp.where(gid_ref[...] == row.astype(F32), 1.0, 0.0).astype(BF16)
        sums = dot(hot, g_ref[...])
        high = sums.astype(BF16)
        sums_ref[rows, 0:LOCAL] = high
        sums_ref[rows, LOCAL:] = (sums - high.astype(F32)).astype(BF16)
        for store in stores(i):
            store.start()

    for i in range(ROWS // BLOCK):
        for store in stores(i):
            store.wait()


def gradients(x, top, mass, cross, e, probs, gid, live):
    return pl.pallas_call(
        grad_kernel,
        out_shape=(
            jax.ShapeDtypeStruct((ROWS, LOCAL), BF16),
            jax.ShapeDtypeStruct((ROWS, 2 * LOCAL), BF16),
            jax.ShapeDtypeStruct((1, 1), F32),
        ),
        in_specs=[VMEM, VMEM, VMEM, SMEM, ANY, ANY, VMEM, VMEM],
        out_specs=(ANY, ANY, SMEM),
        scratch_shapes=[
            pltpu.VMEM((ROWS, LOCAL), F32),
            pltpu.VMEM((ROWS, LOCAL), BF16),
            pltpu.VMEM((ROWS, LOCAL), BF16),
            pltpu.VMEM((ROWS, 2 * LOCAL), BF16),
            pltpu.SemaphoreType.DMA((10,)),
        ],
        compiler_params=FULL,
    )(x, top, mass, cross, e, probs, gid, live)


TOP = 32700.0
ROWS2 = ROWS // 2
TAIL = 16
I16 = jnp.int16


def exponent(x):
    return jnp.ceil(jnp.log(jnp.maximum(x, 1e-30) / TOP) * (256.0 / math.log(2.0)))


def power(e):
    return jnp.exp2(e * (1.0 / 256.0))


def to16(x):
    return x.astype(jnp.int32).astype(I16)


def from16(x):
    return x.astype(jnp.int32).astype(F32)


def encode(val):
    e = exponent(jnp.max(jnp.abs(val), axis=1, keepdims=True))
    return to16(jnp.round(val * power(-e))), jnp.broadcast_to(e, (128, 128)).T[0:1]


def wide(row):
    return jnp.concatenate([row] + [jnp.zeros_like(row)] * (LOCAL // 128 - 1), axis=1)


def write_message(out_ref, block_of, loss, tail_ref):
    for j in range(ROWS2 // 128):
        code, e = encode(block_of(j))
        out_ref[pl.ds(j * 128, 128), :] = code
        tail_ref[pl.ds(j, 1), :] = e
    tail = [tail_ref[0 : ROWS2 // 128, :], loss, jnp.zeros((TAIL - ROWS2 // 128 - 1, 128), F32)]
    tail = jnp.concatenate(tail, axis=0)
    zeros = [jnp.zeros_like(tail)] * (LOCAL // 128 - 1)
    out_ref[pl.ds(ROWS2, TAIL), :] = to16(jnp.concatenate([tail] + zeros, axis=1))


def encode_loss(loss):
    e = exponent(jnp.abs(loss))
    whole = loss * power(-e)
    first = jnp.round(whole)
    rest = jnp.round((whole - first) * TOP)
    lane = lax.broadcasted_iota(jnp.int32, (1, 128), 1)
    return jnp.where(lane == 0, e, jnp.where(lane == 1, first, jnp.where(lane == 2, rest, 0.0)))


def decode_loss(code):
    return (code[:, 1:2] + code[:, 2:3] * (1.0 / TOP)) * power(code[:, 0:1])


def read_tail(ref, tail_ref):
    tail_ref[...] = from16(ref[pl.ds(ROWS2, TAIL), 0:128])


def tail_loss(tail_ref):
    return tail_ref[ROWS2 // 128 : ROWS2 // 128 + 1, :]


def read_message(ref, tail_ref, j):
    scale = power(column(tail_ref[pl.ds(j, 1), :]))
    rows = pl.ds(j * 128, 128)
    parts = [from16(ref[rows, k * 128 : (k + 1) * 128]) * scale for k in range(LOCAL // 128)]
    return jnp.concatenate(parts, axis=1)


TAIL_REF = pltpu.VMEM((TAIL, 128), F32)
MESSAGE = jax.ShapeDtypeStruct((ROWS2 + TAIL, LOCAL), I16)


def weight_kernel(at_ref, all_ref, keep_ref, give_ref, block_ref, sems):
    c, x = at_ref[0], at_ref[1]

    def fetch(n):
        source = all_ref.at[lax.rem(x + (2, 1, 3, 0)[n % 4], 4), lax.rem(c + n // 4, 2)]
        return pltpu.make_async_copy(source, block_ref.at[n], sems.at[n])

    for n in range(8):
        fetch(n).start()
    for n in range(8):
        fetch(n).wait()
        out = (keep_ref, give_ref)[n // 4]
        out[:, n % 4 * LOCAL : (n % 4 + 1) * LOCAL] = block_ref[n].T


def turn_weights(at, blocks):
    half = jax.ShapeDtypeStruct((LOCAL, 4 * LOCAL), BF16)
    return pl.pallas_call(
        weight_kernel,
        out_shape=(half, half),
        in_specs=[SMEM, ANY],
        out_specs=(VMEM, VMEM),
        scratch_shapes=[
            pltpu.VMEM((8, LOCAL, LOCAL), BF16),
            pltpu.SemaphoreType.DMA((8,)),
        ],
        compiler_params=FULL,
    )(at, blocks)


def fetch_pair(own_ref, other_ref, w_own, w_other, first, n, g_ref, w_ref, sems):
    cols = pl.ds(first * LOCAL, n * LOCAL)
    copies = [
        pltpu.make_async_copy(ref, g_ref.at[:, pl.ds(k * LOCAL, LOCAL)], sems.at[k])
        for k, ref in enumerate((own_ref, other_ref))
    ] + [
        pltpu.make_async_copy(ref.at[:, cols], w_ref.at[pl.ds(k * LOCAL, LOCAL)], sems.at[2 + k])
        for k, ref in enumerate((w_own, w_other))
    ]
    for copy in copies:
        copy.start()
    return copies


def far_kernel(
    loss_ref, more_ref, own_ref, other_ref, w_own, w_other, low, high, sum_ref, *refs
):
    g_ref, w_ref, val_ref, tail_ref, sems = refs
    copies = fetch_pair(own_ref, other_ref, w_own, w_other, 0, 1, g_ref, w_ref, sems)
    loss = encode_loss(jnp.full((1, 128), loss_ref[0, 0] + more_ref[0, 0], F32))
    sum_ref[...] = loss
    for copy in copies:
        copy.wait()
    for i, out in enumerate((low, high)):
        val_ref[...] = dot(g_ref[pl.ds(i * ROWS2, ROWS2), :], w_ref[...])
        write_message(out, lambda j: val_ref[pl.ds(j * 128, 128), :], loss, tail_ref)


def near_kernel(
    loss_ref, own_ref, other_ref, w_own, w_other, l1, h1, l3, h3, c0, g_ref, w_ref, val_ref, tail_ref, sems
):
    copies = fetch_pair(own_ref, other_ref, w_own, w_other, 1, 3, g_ref, w_ref, sems)
    for copy in copies:
        copy.wait()
    for i in range(2):
        rows = pl.ds(i * ROWS2, ROWS2)
        val_ref[...] = dot(g_ref[rows, :], w_ref[...])
        for k, out in enumerate(((l1, h1)[i], (l3, h3)[i])):
            cols = slice(k * LOCAL, (k + 1) * LOCAL)
            if out.dtype == F32:
                out[...] = val_ref[:, cols]
            else:
                write_message(
                    out, lambda j: val_ref[pl.ds(j * 128, 128), cols], loss_ref[...], tail_ref
                )
        c0[rows, :] = val_ref[:, 2 * LOCAL :]


def pair_scratch(n):
    return [
        pltpu.VMEM((ROWS, 2 * LOCAL), BF16),
        pltpu.VMEM((2 * LOCAL, n * LOCAL), BF16),
        pltpu.VMEM((ROWS2, n * LOCAL), F32),
        TAIL_REF,
        pltpu.SemaphoreType.DMA((4,)),
    ]


def far_terms(loss, more, own, other, w_own, w_other):
    return pl.pallas_call(
        far_kernel,
        out_shape=(MESSAGE, MESSAGE, jax.ShapeDtypeStruct((1, 128), F32)),
        in_specs=[SMEM, SMEM] + [ANY] * 4,
        out_specs=(VMEM,) * 3,
        scratch_shapes=pair_scratch(1),
        compiler_params=PARAMS,
    )(loss, more, own, other, w_own, w_other)


def near_terms(loss, own, other, w_own, w_other):
    part = jax.ShapeDtypeStruct((ROWS2, LOCAL), F32)
    return pl.pallas_call(
        near_kernel,
        out_shape=(part, MESSAGE, MESSAGE, part, jax.ShapeDtypeStruct((ROWS, LOCAL), F32)),
        in_specs=[VMEM] + [ANY] * 4,
        out_specs=(VMEM,) * 5,
        scratch_shapes=pair_scratch(3),
        compiler_params=PARAMS,
    )(loss, own, other, w_own, w_other)


def relay_kernel(own_ref, got_ref, out_ref, got_tail, tail_ref):
    read_tail(got_ref, got_tail)

    def block(j):
        rows = pl.ds(j * 128, 128)
        return own_ref[rows, :] + read_message(got_ref, got_tail, j)

    write_message(out_ref, block, tail_loss(got_tail), tail_ref)


def relay(own, got):
    return pl.pallas_call(
        relay_kernel,
        out_shape=MESSAGE,
        in_specs=[VMEM] * 2,
        out_specs=VMEM,
        scratch_shapes=[TAIL_REF] * 2,
        compiler_params=PARAMS,
    )(own, got)


PACKED = 3 * SLOTS + TAIL


def collect_kernel(own_ref, low_l, high_r, o_ref, *tails):
    for i, (ref, tail_ref) in enumerate(zip((low_l, high_r), tails)):
        read_tail(ref, tail_ref)
        for j in range(ROWS2 // 128):
            rows = pl.ds(i * ROWS2 + j * 128, 128)
            o_ref[rows, :] = own_ref[rows, :] + read_message(ref, tail_ref, j)


def collect(own, low_l, high_r):
    return pl.pallas_call(
        collect_kernel,
        out_shape=jax.ShapeDtypeStruct((ROWS, LOCAL), F32),
        in_specs=[VMEM] * 3,
        out_specs=VMEM,
        scratch_shapes=[TAIL_REF] * 2,
        compiler_params=PARAMS,
    )(own, low_l, high_r)


def pack_kernel(loss_ref, own_ref, low_r, low_l, high_r, high_l, o_ref, *tails):
    for ref, tail_ref in zip((low_r, low_l, high_r, high_l), tails):
        read_tail(ref, tail_ref)
    codes = [loss_ref[...]] + [tail_loss(tail_ref) for tail_ref in tails[:3]]
    loss = decode_loss(jnp.concatenate(codes, axis=0))
    loss = (loss[0:1] + loss[1:2]) + (loss[2:3] + loss[3:4])
    loss = encode_loss(jnp.broadcast_to(loss, (1, 128)))
    pad = jnp.zeros((TAIL - 2, 128), F32)
    for i in range(2):
        for j in range(ROWS2 // 128):
            at = i * (ROWS2 // 128) + j
            val = own_ref[pl.ds(at * 128, 128), :]
            code, e = encode(val + read_message((low_r, high_l)[i], tails[3 * i], j))
            tail = to16(jnp.concatenate([e, loss, pad], axis=0))
            for n in range(128 // SLOTS):
                for k in range(3):
                    o_ref[at * 4 + n, k * SLOTS : (k + 1) * SLOTS, :] = code[
                        n * SLOTS : (n + 1) * SLOTS, k * 128 : (k + 1) * 128
                    ]
                o_ref[at * 4 + n, 3 * SLOTS :, :] = tail


def pack(loss, own, low_r, low_l, high_r, high_l):
    return pl.pallas_call(
        pack_kernel,
        out_shape=jax.ShapeDtypeStruct((TRAINERS, PACKED, 128), I16),
        in_specs=[VMEM] * 6,
        out_specs=VMEM,
        scratch_shapes=[TAIL_REF] * 4,
        compiler_params=PARAMS,
    )(loss, own, low_r, low_l, high_r, high_l)


def finish_kernel(at_ref, x_ref, grad_ref, loss_ref, e_ref):
    tail = from16(x_ref[:, 3 * SLOTS :, :])
    e = tail[:, 0, :]
    e_ref[...] = jnp.concatenate([e, jnp.zeros((128 - TRAINERS, 128), F32)], axis=0).T
    scale = power(e_ref[pl.ds(pl.multiple_of(at_ref[0] * SLOTS, SLOTS), SLOTS), :])
    total = [jnp.zeros((SLOTS, 128), F32)] * 3
    for s in range(TRAINERS):
        for k in range(3):
            total[k] += from16(x_ref[s, k * SLOTS : (k + 1) * SLOTS, :]) * scale[:, s : s + 1]
    for k in range(3):
        grad_ref[:, k * 128 : (k + 1) * 128] = total[k]
    loss_ref[0, 0] = jnp.sum(decode_loss(tail[:, 1, :]))


def finish(at, x):
    return pl.pallas_call(
        finish_kernel,
        out_shape=(
            jax.ShapeDtypeStruct((SLOTS, LOCAL), F32),
            jax.ShapeDtypeStruct((1, 1), F32),
        ),
        in_specs=[SMEM, VMEM],
        out_specs=(VMEM, SMEM),
        scratch_shapes=[pltpu.VMEM((128, 128), F32)],
        compiler_params=PARAMS,
    )(at, x)


HEAD_BLOCK = 256
HEAD_STEPS = HALF // HEAD_BLOCK


def head_kernel(c_ref, table_ref, sums_ref, o_ref):
    both = dot(table_ref[0], sums_ref[...], ((0,), (0,)))
    both = both[:, 0:LOCAL] + both[:, LOCAL:]
    for j in range(LOCAL // 128):
        o_ref[pl.ds(j, HEAD_BLOCK, stride=LOCAL // 128), :] = both[:, j * 128 : (j + 1) * 128]


def head_gradient(c, table, sums):
    def place(i, c):
        side = lax.rem(c[0] + i // HEAD_STEPS, 2)
        return (side * HEAD_STEPS + i % HEAD_STEPS, 0)

    return pl.pallas_call(
        head_kernel,
        grid_spec=pltpu.PrefetchScalarGridSpec(
            num_scalar_prefetch=1,
            grid=(2 * HEAD_STEPS,),
            in_specs=[
                pl.BlockSpec(
                    (1, ROWS, HEAD_BLOCK), lambda i, c: (i // HEAD_STEPS, 0, i % HEAD_STEPS)
                ),
                pl.BlockSpec((ROWS, 2 * LOCAL), lambda i, c: (0, 0)),
            ],
            out_specs=pl.BlockSpec((HEAD_BLOCK * LOCAL // 128, 128), place),
        ),
        out_shape=jax.ShapeDtypeStruct((D * LOCAL // 128, 128), F32),
        compiler_params=PARAMS,
        cost_estimate=pl.CostEstimate(
            flops=4 * ROWS * D * LOCAL, bytes_accessed=12 * 1024 * 1024, transcendentals=0
        ),
    )(c, table, sums)


PAIR = [(i, i ^ 1) for i in range(SHARDS)]


def along_x(k):
    return [(i, (i + 2 * k) % SHARDS) for i in range(SHARDS)]


RIGHT, LEFT = along_x(1), along_x(-1)


def along_z(k):
    return [(i, (i // Y + k) % Z * Y + i % Y) for i in range(TRAINERS)]


def along_y(k):
    return [(i, i // Y * Y + (i + k) % Y) for i in range(TRAINERS)]


def on_device(hidden_table, head_weight, targets, counts, dest, token):
    me = lax.axis_index("vocab")
    trainer = lax.axis_index("trainer")
    c = lax.rem(me, 2)
    x = me // 2
    y = lax.rem(trainer, Y)
    c1 = c.reshape(1).astype(jnp.int32)
    at_cx = jnp.stack([c, x]).astype(jnp.int32)
    at_cy = jnp.stack([c, y]).astype(jnp.int32)
    z1 = (trainer // Y).reshape(1).astype(jnp.int32)
    weight = head_weight[:, 0, :]

    half = lax.dynamic_slice(hidden_table, (0, c * HALF), (SLOTS, HALF))
    near = [half] + [lax.ppermute(half, "trainer", along_z(k)) for k in (1, 2, -2, -1)]
    near[3:3] = [
        lax.ppermute(near[2], "trainer", along_z(1)),
        lax.ppermute(near[2], "trainer", along_z(2)),
        lax.ppermute(near[3], "trainer", along_z(-1)),
    ]

    gid = dest * SLOTS + token
    index = jnp.arange(ROWS, dtype=jnp.int32)
    live = (index % SLOTS < jnp.repeat(counts, SLOTS)).astype(F32).reshape(1, ROWS)
    gid = gid.astype(F32).reshape(1, ROWS)

    z1, gid, live = lax.optimization_barrier((z1, gid, live))
    plane = in_order(z1, near)
    low0, high0 = plane[: Z // 2], plane[Z // 2 :]
    low1 = lax.ppermute(low0, "trainer", along_y(1))
    high3 = lax.ppermute(high0, "trainer", along_y(-1))
    high1 = lax.ppermute(high0, "trainer", along_y(1))
    low3 = lax.ppermute(low0, "trainer", along_y(-1))
    at_cx, _ = lax.optimization_barrier((at_cx, plane))
    w_own, w_give = turn_weights(at_cx, weight.reshape(4, 2, LOCAL, LOCAL))
    low1, high3, w_own, w_give = lax.optimization_barrier((low1, high3, w_own, w_give))
    low2 = lax.ppermute(low1, "trainer", along_y(1))
    high2 = lax.ppermute(high3, "trainer", along_y(-1))
    targets, _ = lax.optimization_barrier((targets, (low1, high3)))
    split = split_targets(targets[:, 0, :])
    high1, split = lax.optimization_barrier((high1, split))
    middle = jnp.concatenate([low1, high3, high1, low3])
    pieces = [plane, middle, jnp.concatenate([low2, high2])]
    pieces += [lax.ppermute(p, "vocab", PAIR) for p in pieces]
    split, _ = lax.optimization_barrier((split, (w_give, low2, high2, pieces[3])))
    probs = lax.all_to_all(split, "trainer", split_axis=0, concat_axis=0, tiled=True)

    table, logits, stats, top = logits_and_stats(at_cy, pieces, weight)
    stats = merge_stats([stats, lax.ppermute(stats, "vocab", PAIR)])
    stats = [stats] + [lax.ppermute(stats, "vocab", along_x(k)) for k in (1, 2, 3)]
    stats = merge_stats(stats, TRAINERS)
    w_give, _ = lax.optimization_barrier((w_give, stats))
    w_other = lax.ppermute(w_give, "vocab", PAIR)
    stats, probs = lax.optimization_barrier((stats, probs.reshape(ROWS, LOCAL)))
    stats = lax.all_to_all(stats, "trainer", split_axis=0, concat_axis=0, tiled=True)

    e, mass, cross = select_rows(top, logits, probs, gid, live)
    high, sums, loss = gradients(stats, top, mass, cross, e, probs, gid, live)

    more = lax.ppermute(loss, "vocab", PAIR)
    far = lax.ppermute(high, "vocab", PAIR)
    l2, h2, loss = far_terms(loss, more, high, far, w_own, w_other)
    low_r = lax.ppermute(l2, "vocab", RIGHT)
    high_l = lax.ppermute(h2, "vocab", LEFT)
    l1, h1, l3, h3, t0 = near_terms(loss, high, far, w_own, w_other)
    high_r = lax.ppermute(h1, "vocab", RIGHT)
    low_l = lax.ppermute(l3, "vocab", LEFT)
    low_r = lax.ppermute(relay(l1, low_r), "vocab", RIGHT)
    high_l = lax.ppermute(relay(h3, high_l), "vocab", LEFT)
    head = head_gradient(c1, table, sums)
    packed = pack(loss, collect(t0, low_l, high_r), low_r, low_l, high_r, high_l)
    packed = lax.all_to_all(packed, "trainer", split_axis=0, concat_axis=0, tiled=True)
    table_grad, loss = finish(lax.rem(trainer, 4).reshape(1).astype(jnp.int32), packed)
    mean_loss = loss[0, 0] / jnp.sum(counts).astype(F32)
    return head.reshape(D, 1, LOCAL), table_grad, mean_loss


def solution(mesh):
    return jax.shard_map(
        on_device,
        mesh=mesh,
        in_specs=(
            P("trainer", None),
            P(None, "vocab", "trainer"),
            P("trainer", "vocab", None),
            P(),
            P(),
            P(),
        ),
        out_specs=(P(None, "vocab", "trainer"), P("trainer", "vocab"), P()),
        check_vma=False,
    )
```
